32 devices in a mesh: stream: 2 (over x), dp: 16 (over z, y, core).
Axes of the slice: x: 2, y: 2, z: 4, core: 2. Of those that a mesh axis runs over, the one named last changes fastest.
Arguments:
- text_in: bfloat16 [32768, 768], P(('stream', 'dp')), may hold values from -6 to 6
- image_in: bfloat16 [9216, 1024], P(('stream', 'dp')), may hold values from -6 to 6
- lengths: int32 [256], P(('stream', 'dp')), may hold values from 16 to 128, as said below
- t_proj: bfloat16 [768, 8448], P(('stream', 'dp')), may hold values from -0.21875 to 0.21875
- t_out: bfloat16 [4864, 768], P(('stream', 'dp'))
- t_bias_wide: bfloat16 [5120], P(('stream', 'dp')), may hold values from -3 to 3
- t_bias: bfloat16 [8, 768], P(None, ('stream', 'dp')), may hold values from -3 to 3
- t_gain: bfloat16 [3, 768], P(None, ('stream', 'dp')), may hold values from 0.25 to 1.75
- i_proj: bfloat16 [1024, 7168], P(('stream', 'dp')), may hold values from -0.1875 to 0.1875
- i_out: bfloat16 [3072, 1024], P(('stream', 'dp'))
- i_bias_wide: bfloat16 [3072], P(('stream', 'dp')), may hold values from -3 to 3
- i_bias: bfloat16 [8, 1024], P(None, ('stream', 'dp')), may hold values from -3 to 3
- i_gain: bfloat16 [3, 1024], P(None, ('stream', 'dp')), may hold values from 0.25 to 1.75
- text_cot: bfloat16 [32768, 768], P(('stream', 'dp')), may hold values from -6 to 6
- image_cot: bfloat16 [9216, 1024], P(('stream', 'dp')), may hold values from -6 to 6
Outputs:
- text_out: float32 [32768, 768], P(('stream', 'dp'))
- image_out: float32 [9216, 1024], P(('stream', 'dp'))
- text_grad: float32 [32768, 768], P(('stream', 'dp'))
- image_grad: float32 [9216, 1024], P(('stream', 'dp'))
- t_proj_grad: float32 [768, 8448], P(('stream', 'dp'))
- t_out_grad: float32 [4864, 768], P(('stream', 'dp'))
- t_bias_wide_grad: float32 [5120], P(('stream', 'dp'))
- t_bias_grad: float32 [8, 768], P(None, ('stream', 'dp'))
- t_gain_grad: float32 [3, 768], P(None, ('stream', 'dp'))
- i_proj_grad: float32 [1024, 7168], P(('stream', 'dp'))
- i_out_grad: float32 [3072, 1024], P(('stream', 'dp'))
- i_bias_wide_grad: float32 [3072], P(('stream', 'dp'))
- i_bias_grad: float32 [8, 1024], P(None, ('stream', 'dp'))
- i_gain_grad: float32 [3, 1024], P(None, ('stream', 'dp'))
The draws below stay inside these ranges and needn't reach their ends.
Inputs may be any that keep to these rules, and one draw needn't show every extreme that they name: `lengths`: some caption has 128 tokens and some has 16.
All inputs are finite; a program needn't handle non-finite values.
Results may differ from the reference program's by a relative error of at most 0.019.
Values may be sent and summed in bfloat16 or wider, within the bound.
No kernel may reach another device: no remote copies, remote signals or barrier semaphores. Data moves between devices by JAX's collectives and lax.ppermute only.
A program may use at most 320 MiB of HBM per device.

```python
import math
import jax
import jax.numpy as jnp
from jax import lax

D_T = 768
D_I = 1024
CO_W = 1024
FF_T = 3072
FF_I = 1024
HEADS_T = 12
HEADS_I = 8
CO_HEADS = 8
CAP = 128
REGIONS = 36
PAIRS = 256
TEXT_TOK = 32768
IMAGE_TOK = 9216


def scaled_rows(key, first_rows, second_rows, third_rows, columns, boosted):
    total_rows = first_rows + second_rows + third_rows
    normal_draw = jnp.clip(jax.random.normal(key, (total_rows, columns), jnp.float32), -6.0, 6.0)
    row_index = lax.broadcasted_iota(jnp.int32, (total_rows, columns), 0)
    factor = jnp.where(row_index < first_rows, boosted * first_rows ** (-0.5), jnp.where(row_index < first_rows + second_rows, boosted * second_rows ** (-0.5), third_rows ** (-0.5)))
    return (normal_draw * factor).astype(jnp.bfloat16)


def draw_t_out(key, part):
    key = jax.random.fold_in(key, 11)
    return scaled_rows(key, CO_W, D_T, FF_T, D_T, 3.0)


def draw_i_out(key, part):
    key = jax.random.fold_in(key, 12)
    return scaled_rows(key, CO_W, D_I, FF_I, D_I, 3.0)


def draw_lengths(key, part):
    key = jax.random.fold_in(key, 13)
    first_key, second_key = jax.random.split(key)
    lengths_drawn = jax.random.randint(first_key, (PAIRS,), CAP // 8, CAP + 1)
    shuffled = jax.random.permutation(second_key, PAIRS)
    return lengths_drawn.at[shuffled[0]].set(CAP).at[shuffled[1]].set(CAP // 8)


def with_spikes(entries, rng, source, target, shards_of, factor):
    def block_of(dim):
        return (jnp.arange(entries.shape[dim]) // (entries.shape[dim] // shards_of)).reshape((-1,) + (1,) * (entries.ndim - 1 - dim))

    one_side = jax.random.permutation(rng, shards_of)[block_of(target)]
    other_side = (block_of(target) + shards_of // 2) % shards_of
    return jnp.where((block_of(source) == one_side) | (block_of(source) == other_side), factor * entries, entries)


def level_of(rng, extent, cuts, smallest, high):
    def one(axis_at, shards_of):
        heights = jax.random.uniform(jax.random.fold_in(jax.random.fold_in(rng, 6), axis_at), (shards_of,), jnp.float32, smallest / len(cuts), high / len(cuts))
        return jnp.repeat(jnp.exp(heights), extent[axis_at] // shards_of).reshape((-1,) + (1,) * (len(extent) - axis_at - 1))

    factor_of = one(*cuts[0])
    for cut in cuts[1:]:
        factor_of = factor_of * one(*cut)
    return factor_of


def noise(own_key, shape, scale, limit, cuts=(), held_as=jnp.bfloat16):
    factor_of = level_of(own_key, shape, cuts, -0.22, 0.18) if cuts else 1.0
    drawn = jax.random.normal(own_key, shape, jnp.float32) * scale * factor_of
    return jnp.minimum(jnp.maximum(drawn, -limit), limit).astype(held_as)


def noise_with(key, extent, scale, reach, cuts, heavy, dtype=jnp.bfloat16):
    drawn = scale * jax.random.normal(key, extent, jnp.float32)
    if cuts:
        drawn = drawn * level_of(key, extent, cuts, -0.22, 0.18)
    return jnp.clip(with_spikes(drawn, jax.random.fold_in(key, 3), *heavy), -reach, reach).astype(dtype)


def setup_inputs(seed: int = 0) -> dict:
    seeds = jax.random.split(jax.random.key(seed), 16)
    text_in = noise_with(seeds[0], (TEXT_TOK, D_T), 1.0, 6.0, ((0, 32),), (0, 1, 32, 2.75))
    image_in = noise_with(seeds[1], (IMAGE_TOK, D_I), 1.0, 6.0, ((0, 32),), (0, 1, 32, 2.75))
    lengths = draw_lengths(jax.random.fold_in(seeds[15], 71), 0)
    t_proj = noise(seeds[3], (D_T, 3 * CO_W + 3 * D_T + FF_T), D_T ** -0.5, 0.21875, ((0, 32),))
    t_out = draw_t_out(jax.random.fold_in(seeds[15], 71), 0)
    t_bias_wide = noise(seeds[5], (2 * CO_W + FF_T,), 0.5, 3.0, ((0, 32),))
    t_bias = noise(seeds[6], (8, D_T), 0.5, 3.0, ((1, 32),))
    t_gain = jnp.clip(1.0 + 0.15 * jax.random.normal(seeds[7], (3, D_T), jnp.float32), 0.25, 1.75).astype(jnp.bfloat16)
    i_proj = noise(seeds[8], (D_I, 3 * CO_W + 3 * D_I + FF_I), D_I ** -0.5, 0.1875, ((0, 32),))
    i_out = draw_i_out(jax.random.fold_in(seeds[15], 71), 0)
    i_bias_wide = noise(seeds[10], (2 * CO_W + FF_I,), 0.5, 3.0, ((0, 32),))
    i_bias = noise(seeds[11], (8, D_I), 0.5, 3.0, ((1, 32),))
    i_gain = jnp.clip(1.0 + 0.15 * jax.random.normal(seeds[12], (3, D_I), jnp.float32), 0.25, 1.75).astype(jnp.bfloat16)
    text_cot = noise(seeds[13], (TEXT_TOK, D_T), 1.0, 6.0, ((0, 32),))
    image_cot = noise(seeds[14], (IMAGE_TOK, D_I), 1.0, 6.0, ((0, 32),))
    return dict(text_in=text_in, image_in=image_in, lengths=lengths, t_proj=t_proj, t_out=t_out, t_bias_wide=t_bias_wide, t_bias=t_bias, t_gain=t_gain, i_proj=i_proj, i_out=i_out, i_bias_wide=i_bias_wide, i_bias=i_bias, i_gain=i_gain, text_cot=text_cot, image_cot=image_cot)


@jax.custom_vjp
def low(v):
    return lax.optimization_barrier(v.astype(jnp.bfloat16)).astype(jnp.float32)

@jax.custom_vjp
def low_back(v):
    return v

def low_keep(v):
    return (low(v), None)

def low_pass(kept, grad):
    return (grad,)

def back_keep(v):
    return (v, None)

def back_low(kept, grad):
    return (low(grad),)
low.defvjp(low_keep, low_pass)
low_back.defvjp(back_keep, back_low)
highest = lax.Precision.HIGHEST
epsilon = 1e-05
negative = -1e+30

def matmul(left_side, right_side):
    return jnp.dot(left_side, right_side, precision=highest, preferred_element_type=jnp.float32)

def project(inputs, weight, bias_row):
    return low_back(low(matmul(inputs, weight) + bias_row))

def layer_norm(pre_norm, gain_row, beta_row):
    average = lax.optimization_barrier(jnp.mean(pre_norm, -1, keepdims=True))
    centered = pre_norm - average
    spread = lax.optimization_barrier(jnp.mean(centered * centered, -1, keepdims=True))
    return centered * lax.rsqrt(spread + epsilon) * gain_row + beta_row

def attend(queries, key_rows, values, mask_add, head_count):
    groups = mask_add.shape[0]
    query_heads = queries.reshape(groups, -1, head_count, queries.shape[1] // head_count)
    key_heads = key_rows.reshape(groups, -1, head_count, key_rows.shape[1] // head_count)
    value_heads = values.reshape(groups, -1, head_count, values.shape[1] // head_count)
    factor = query_heads.shape[-1] ** (-0.5)
    scores = low_back(jnp.einsum('gqhd,gkhd->ghqk', query_heads, key_heads, precision=highest)) * factor + mask_add[:, None, None, :]
    weights = jax.nn.softmax(scores, axis=-1)
    context = jnp.einsum('ghqk,gkhd->gqhd', low(weights), value_heads, precision=highest)
    return low_back(low(context.reshape(queries.shape[0], -1)))

def stream_layer(context, residual, proj_weight, out_weight, wide_bias, bias_rows, gain_rows, mask_add, head_count):
    features = residual.shape[1]
    first_norm = layer_norm(residual + low_back(matmul(context, out_weight[:CO_W])) + bias_rows[0], gain_rows[0], bias_rows[1])
    triple_bias = jnp.concatenate([bias_rows[2], jnp.zeros((features,), jnp.float32), bias_rows[3]])
    triple = project(low(first_norm), proj_weight[:, 3 * CO_W:3 * CO_W + 3 * features], triple_bias)
    attended = attend(triple[:, :features], triple[:, features:2 * features], triple[:, 2 * features:], mask_add, head_count)
    second_norm = layer_norm(first_norm + low_back(matmul(attended, out_weight[CO_W:CO_W + features])) + bias_rows[4], gain_rows[1], bias_rows[5])
    hidden = low_back(matmul(low(second_norm), proj_weight[:, 3 * CO_W + 3 * features:])) + wide_bias[2 * CO_W:]
    active = jax.nn.gelu(hidden, approximate=False)
    return layer_norm(second_norm + low_back(matmul(low(active), out_weight[CO_W + features:])) + bias_rows[6], gain_rows[2], bias_rows[7])

def co_inputs(inputs, proj_weight, wide_bias):
    queries = project(inputs, proj_weight[:, :CO_W], wide_bias[:CO_W])
    pair_bias = jnp.concatenate([jnp.zeros((CO_W,), jnp.float32), wide_bias[CO_W:2 * CO_W]])
    pair_kv = project(inputs, proj_weight[:, CO_W:3 * CO_W], pair_bias)
    return (queries, pair_kv)

def whole_block(params, text_rows, image_rows, text_mask, image_mask):
    text_query, text_kv = co_inputs(text_rows, params[0], params[2])
    image_query, image_kv = co_inputs(image_rows, params[5], params[7])
    text_context = attend(text_query, image_kv[:, :CO_W], image_kv[:, CO_W:], image_mask, CO_HEADS)
    image_context = attend(image_query, text_kv[:, :CO_W], text_kv[:, CO_W:], text_mask, CO_HEADS)
    text_final = stream_layer(text_context, text_rows, params[0], params[1], params[2], params[3], params[4], text_mask, HEADS_T)
    image_final = stream_layer(image_context, image_rows, params[5], params[6], params[7], params[8], params[9], image_mask, HEADS_I)
    return (text_final, image_final)

def reference(text_in, image_in, lengths, t_proj, t_out, t_bias_wide, t_bias, t_gain, i_proj, i_out, i_bias_wide, i_bias, i_gain, text_cot, image_cot):
    half_way = PAIRS // 2
    params = tuple((argument.astype(jnp.float32) for argument in (t_proj, t_out, t_bias_wide, t_bias, t_gain, i_proj, i_out, i_bias_wide, i_bias, i_gain)))
    present = lax.broadcasted_iota(jnp.int32, (PAIRS, CAP), 1) < lengths[:, None]
    text_mask = jnp.where(present, 0.0, negative).astype(jnp.float32)
    image_mask = jnp.zeros((PAIRS, REGIONS), jnp.float32)
    per_group = math.gcd(PAIRS, 32)
    group_count = PAIRS // per_group
    text_rows = text_in.astype(jnp.float32).reshape(PAIRS, CAP, D_T)
    image_rows = jnp.roll(image_in.astype(jnp.float32).reshape(PAIRS, REGIONS, D_I), half_way, 0)

    def run_groups(weights_all, text_all, image_all):

        def one_group(members):
            text_part, image_part, text_part_mask, image_part_mask = members
            finals = whole_block(weights_all, text_part.reshape(-1, D_T), image_part.reshape(-1, D_I), text_part_mask, image_part_mask)
            return (finals[0].reshape(per_group, CAP, D_T), finals[1].reshape(per_group, REGIONS, D_I))
        results = lax.map(jax.checkpoint(one_group), (text_all.reshape(group_count, per_group, CAP, D_T), image_all.reshape(group_count, per_group, REGIONS, D_I), text_mask.reshape(group_count, per_group, CAP), image_mask.reshape(group_count, per_group, REGIONS)))
        return (results[0].reshape(PAIRS, CAP, D_T), results[1].reshape(PAIRS, REGIONS, D_I))
    (text_final, image_final), pullback = jax.vjp(run_groups, params, text_rows, image_rows)
    text_upstream = text_cot.astype(jnp.float32).reshape(PAIRS, CAP, D_T)
    image_upstream = jnp.roll(image_cot.astype(jnp.float32).reshape(PAIRS, REGIONS, D_I), half_way, 0)
    gradients = pullback((text_upstream, image_upstream))
    param_grads = gradients[0]
    return (text_final.reshape(TEXT_TOK, D_T), jnp.roll(image_final, half_way, 0).reshape(IMAGE_TOK, D_I), gradients[1].reshape(TEXT_TOK, D_T), jnp.roll(gradients[2], half_way, 0).reshape(IMAGE_TOK, D_I), param_grads[0], param_grads[1], param_grads[2], param_grads[3], param_grads[4], param_grads[5], param_grads[6], param_grads[7], param_grads[8], param_grads[9])
```

```python
import functools

import jax
import jax.numpy as jnp
from jax import lax
from jax.experimental import pallas as pl
from jax.experimental.pallas import tpu as pltpu
from jax.sharding import PartitionSpec as P

CO_W = 1024
HEADS_T = 12
HEADS_I = 8
CO_HEADS = 8
CAP = 128
REGIONS = 36
SLOTS = 48

epsilon = 1e-05
negative = -1e30
BF = jnp.bfloat16
F32 = jnp.float32
VMEM_LIMIT = 60 * 1024 * 1024
HALF_ROOT = 0.7071067811865476
INV_ROOT = 0.3989422804014327
ANY = pl.BlockSpec(memory_space=pl.ANY)
SMEM = pl.BlockSpec(memory_space=pltpu.SMEM)


def dot_nn(a, b):
    return lax.dot_general(a, b, (((1,), (0,)), ((), ())), preferred_element_type=F32)


def dot_nt(a, b):
    return lax.dot_general(a, b, (((1,), (1,)), ((), ())), preferred_element_type=F32)


def dot_tn(a, b):
    return lax.dot_general(a, b, (((0,), (0,)), ((), ())), preferred_element_type=F32)


def params():
    return pltpu.CompilerParams(vmem_limit_bytes=VMEM_LIMIT)


def dp_parts():
    total = lax.axis_size("dp")
    index = lax.axis_index("dp")
    return total // 4, index // 4, (index // 2) % 2, index % 2


def over_core(block):
    total = lax.axis_size("dp")
    return lax.ppermute(block, "dp", [(d, d ^ 1) for d in range(total)])


def over_y(block):
    total = lax.axis_size("dp")
    return lax.ppermute(block, "dp", [(d, d ^ 2) for d in range(total)])


def over_x(block):
    total = lax.axis_size("stream")
    return lax.ppermute(block, "stream", [(d, d ^ 1) for d in range(total)])


def over_z(block, shift):
    total = lax.axis_size("dp")
    return lax.ppermute(block, "dp", [(d, (d + 4 * shift) % total) for d in range(total)])


def pick(buffer, position, axis):
    return lax.dynamic_index_in_dim(buffer, position, axis, keepdims=False)


def place_kernel(table_ref, *refs):
    pieces, out_ref = refs[:-1], refs[-1]
    step = pl.program_id(0)
    for number, piece in enumerate(pieces):

        @pl.when(step == number)
        def _(piece=piece):
            out_ref[...] = piece[...]


def place(shape, block_in, grid, steps, block_out, spot, pieces, table):
    def read(number):
        def index(i, j, table_ref):
            return steps(jnp.where(i == number, j, jnp.where(i < number, 0, grid - 1)))

        return pl.BlockSpec(block_in, index)

    return pl.pallas_call(
        place_kernel,
        grid_spec=pltpu.PrefetchScalarGridSpec(
            num_scalar_prefetch=1,
            grid=(len(pieces), grid),
            in_specs=[read(number) for number in range(len(pieces))],
            out_specs=pl.BlockSpec(
                block_out, lambda i, j, table_ref: spot(table_ref[2 * i], table_ref[2 * i + 1], j)
            ),
        ),
        out_shape=jax.ShapeDtypeStruct(shape, pieces[0].dtype),
        compiler_params=params(),
    )(table, *pieces)


def table_of(pairs):
    return jnp.stack([jnp.asarray(v, jnp.int32) for pair in pairs for v in pair])


def gather_rows(own, y_first):
    nz, z, y, c = dp_parts()
    x = lax.axis_index("stream")
    rows, cols = own.shape
    column = place(
        (nz, rows, cols),
        (rows, cols),
        1,
        lambda j: (0, 0),
        (None, rows, cols),
        lambda p, q, j: (p, 0, 0),
        [own] + [over_z(own, shift) for shift in range(1, nz)],
        table_of([((z - shift) % nz, 0) for shift in range(nz)]),
    )

    def pair(first, second):
        return place(
            (nz, 2, rows, cols),
            (nz, rows, cols),
            1,
            lambda j: (0, 0, 0),
            (nz, None, rows, cols),
            lambda p, q, j: (0, p, 0, 0),
            [first, second],
            table_of([(y, 0), (1 - y, 0)]),
        )

    plane = pair(column, over_y(column))
    if y_first:
        far = over_x(plane)
    else:
        over = over_x(column)
        far = pair(over, over_y(over))
    full = place(
        (2, nz, 2, 2, rows, cols),
        (None, 2, rows, cols),
        nz,
        lambda j: (j, 0, 0, 0),
        (None, None, 2, None, rows, cols),
        lambda p, q, j: (p, j, 0, q, 0, 0),
        [plane, far, over_core(plane), over_core(far)],
        table_of([(x, c), (1 - x, c), (x, 1 - c), (1 - x, 1 - c)]),
    )
    return full.reshape(-1, cols)


def add_low(kept, came):
    return (kept.astype(F32) + came.astype(F32)).astype(BF)


def scatter_rows(grad, y_first):
    nz, z, y, c = dp_parts()
    x = lax.axis_index("stream")
    cols = grad.shape[1]
    part = grad.reshape(2, nz, 2, 2, -1, cols)
    part = add_low(pick(part, c, 3), over_core(pick(part, 1 - c, 3)))
    if y_first:
        part = add_low(pick(part, y, 2), over_y(pick(part, 1 - y, 2)))
        part = add_low(pick(part, x, 0), over_x(pick(part, 1 - x, 0)))
    else:
        part = add_low(pick(part, x, 0), over_x(pick(part, 1 - x, 0)))
        part = add_low(pick(part, y, 1), over_y(pick(part, 1 - y, 1)))
    total = pick(part, z, 0).astype(F32)
    for shift in range(1, nz):
        total = total + over_z(pick(part, (z + shift) % nz, 0), shift).astype(F32)
    return total


def softmax_rows(scores):
    high = jnp.max(scores, -1, keepdims=True)
    exponent = jnp.exp(scores - high)
    return exponent * (1.0 / jnp.sum(exponent, -1, keepdims=True))


def norm_rows(pre_norm):
    centered = pre_norm - jnp.mean(pre_norm, -1, keepdims=True)
    inverse = lax.rsqrt(jnp.mean(centered * centered, -1, keepdims=True) + epsilon)
    return centered * inverse, inverse


def norm_back_rows(upstream, gain, normed, inverse):
    scaled = upstream * gain
    return inverse * (
        scaled
        - jnp.mean(scaled, -1, keepdims=True)
        - normed * jnp.mean(scaled * normed, -1, keepdims=True)
    )


def col_sum(block):
    return jnp.sum(block, 0, keepdims=True)


def key_mask(shape, count):
    return jnp.where(lax.broadcasted_iota(jnp.int32, shape, 1) < count, 0.0, negative)


def attend_all(units, factor):
    scores = [dot_nt(q, k) * factor + mask for q, k, _, mask in units]
    probs = [softmax_rows(score).astype(BF) for score in scores]
    return [dot_nn(prob, unit[2]) for prob, unit in zip(probs, units)]


def attend_back_all(units, upstreams, factor):
    scores = [dot_nt(q, k) * factor + mask for q, k, _, mask in units]
    raised = [dot_nt(up, unit[2]) for up, unit in zip(upstreams, units)]
    probs = [softmax_rows(score) for score in scores]
    values_grad = [dot_tn(prob.astype(BF), up) for prob, up in zip(probs, upstreams)]
    rounded = [
        (prob * (grad - jnp.sum(prob * grad, -1, keepdims=True)) * factor).astype(BF)
        for prob, grad in zip(probs, raised)
    ]
    queries_grad = [dot_nn(low, unit[1]) for low, unit in zip(rounded, units)]
    keys_grad = [dot_tn(low, unit[0]) for low, unit in zip(rounded, units)]
    return list(zip(queries_grad, keys_grad, values_grad))


def co_forward_kernel(len_ref, text_ref, image_ref, text_out, image_out):
    step = pl.program_id(0)
    factor = (CO_W // CO_HEADS) ** -0.5
    region_mask = key_mask((1, SLOTS), REGIONS)
    text_mask = key_mask((1, CAP), len_ref[step])
    units, places = [], []
    for head in range(CO_HEADS):
        at = [slice(part * CO_W + head * 128, part * CO_W + head * 128 + 128) for part in range(3)]
        tq, tk, tv = [text_ref[:, where] for where in at]
        iq, ik, iv = [image_ref[:, where] for where in at]
        units += [(tq, ik, iv, region_mask), (iq, tk, tv, text_mask)]
        places += [(text_out, at[0]), (image_out, at[0])]
    for (out_ref, where), context in zip(places, attend_all(units, factor)):
        out_ref[:, where] = context.astype(BF)


def co_forward(lengths, text_co, image_co):
    pairs = lengths.shape[0]
    return pl.pallas_call(
        co_forward_kernel,
        grid=(pairs,),
        in_specs=[
            SMEM,
            pl.BlockSpec((CAP, 3 * CO_W), lambda i: (i, 0)),
            pl.BlockSpec((SLOTS, 3 * CO_W), lambda i: (i, 0)),
        ],
        out_specs=[
            pl.BlockSpec((CAP, CO_W), lambda i: (i, 0)),
            pl.BlockSpec((SLOTS, CO_W), lambda i: (i, 0)),
        ],
        out_shape=[
            jax.ShapeDtypeStruct((pairs * CAP, CO_W), BF),
            jax.ShapeDtypeStruct((pairs * SLOTS, CO_W), BF),
        ],
        compiler_params=params(),
    )(lengths, text_co, image_co)


def co_backward_kernel(
    len_ref, text_ref, image_ref, text_up, image_up, text_out, image_out, text_sum, image_sum
):
    step = pl.program_id(0)
    factor = (CO_W // CO_HEADS) ** -0.5
    region_mask = key_mask((1, SLOTS), REGIONS)
    text_mask = key_mask((1, CAP), len_ref[step])

    @pl.when(step == 0)
    def _():
        text_sum[...] = jnp.zeros_like(text_sum)
        image_sum[...] = jnp.zeros_like(image_sum)

    def store(out_ref, sum_ref, where, grad):
        low = grad.astype(BF)
        out_ref[:, where] = low
        sum_ref[:, where] += col_sum(low.astype(F32))

    units, ups, places = [], [], []
    for head in range(CO_HEADS):
        at = [slice(part * CO_W + head * 128, part * CO_W + head * 128 + 128) for part in range(3)]
        tq, tk, tv = [text_ref[:, where] for where in at]
        iq, ik, iv = [image_ref[:, where] for where in at]
        units += [(tq, ik, iv, region_mask), (iq, tk, tv, text_mask)]
        ups += [text_up[:, at[0]], image_up[:, at[0]]]
        places.append(at)
    grads = attend_back_all(units, ups, factor)
    for head, at in enumerate(places):
        dtq, dik, div = grads[2 * head]
        diq, dtk, dtv = grads[2 * head + 1]
        for where, grad in zip(at, (dtq, dtk, dtv)):
            store(text_out, text_sum, where, grad)
        for where, grad in zip(at, (diq, dik, div)):
            store(image_out, image_sum, where, grad)


def co_backward(lengths, text_co, image_co, text_up, image_up):
    pairs = lengths.shape[0]
    wide = 3 * CO_W
    return pl.pallas_call(
        co_backward_kernel,
        grid=(pairs,),
        in_specs=[
            SMEM,
            pl.BlockSpec((CAP, wide), lambda i: (i, 0)),
            pl.BlockSpec((SLOTS, wide), lambda i: (i, 0)),
            pl.BlockSpec((CAP, CO_W), lambda i: (i, 0)),
            pl.BlockSpec((SLOTS, CO_W), lambda i: (i, 0)),
        ],
        out_specs=[
            pl.BlockSpec((CAP, wide), lambda i: (i, 0)),
            pl.BlockSpec((SLOTS, wide), lambda i: (i, 0)),
            pl.BlockSpec((1, wide), lambda i: (0, 0)),
            pl.BlockSpec((1, wide), lambda i: (0, 0)),
        ],
        out_shape=[
            jax.ShapeDtypeStruct((pairs * CAP, wide), BF),
            jax.ShapeDtypeStruct((pairs * SLOTS, wide), BF),
            jax.ShapeDtypeStruct((1, wide), F32),
            jax.ShapeDtypeStruct((1, wide), F32),
        ],
        compiler_params=params(),
    )(lengths, text_co, image_co, text_up, image_up)


def fetch(step, copies):
    @pl.when(step == 0)
    def _():
        for copy in copies:
            copy.start()
        for copy in copies:
            copy.wait()


def text_units(len_ref, step, pair_count):
    for pair in range(pair_count):
        mask = key_mask((1, CAP), len_ref[step * pair_count + pair])
        for block in range(HEADS_T // 2):
            yield slice(pair * CAP, pair * CAP + CAP), block * 128, mask


def image_mask():
    shape = (2 * SLOTS, 2 * SLOTS)
    row = lax.broadcasted_iota(jnp.int32, shape, 0)
    col = lax.broadcasted_iota(jnp.int32, shape, 1)
    same = (row >= SLOTS) == (col >= SLOTS)
    local = jnp.where(col >= SLOTS, col - SLOTS, col)
    return jnp.where(same & (local < REGIONS), 0.0, negative)


def image_units(rows):
    mask = image_mask()
    return [
        (slice(start, start + 2 * SLOTS), head * 128, mask)
        for start in range(0, rows, 2 * SLOTS)
        for head in range(HEADS_I)
    ]


def halves(block):
    low = lax.broadcasted_iota(jnp.int32, block.shape, 1) < 64
    zero = jnp.zeros_like(block)
    return jnp.concatenate([jnp.where(low, block, zero), jnp.where(low, zero, block)], 0)


def unhalve(stacked):
    rows = stacked.shape[0] // 2
    low = lax.broadcasted_iota(jnp.int32, (rows, stacked.shape[1]), 1) < 64
    return jnp.where(low, stacked[:rows], stacked[rows:])


def attn_forward_kernel(
    is_text,
    down_at,
    len_ref,
    context_ref,
    input_ref,
    proj_ref,
    out_w_ref,
    bias_ref,
    gain_ref,
    zhat1_ref,
    inv1_ref,
    low1_ref,
    triple_ref,
    attended_ref,
    zhat2_ref,
    inv2_ref,
    wco,
    wqkv,
    wo,
    sems,
):
    step = pl.program_id(0)
    width = input_ref.shape[1]
    rows = input_ref.shape[0]
    fetch(
        step,
        [
            pltpu.make_async_copy(out_w_ref.at[pl.ds(0, CO_W)], wco, sems.at[0]),
            pltpu.make_async_copy(proj_ref.at[:, pl.ds(0, 3 * width)], wqkv, sems.at[1]),
            pltpu.make_async_copy(out_w_ref.at[pl.ds(CO_W, width)], wo, sems.at[2]),
        ],
    )
    normed, inverse = norm_rows(
        input_ref[...].astype(F32) + dot_nn(context_ref[...], wco[...]) + bias_ref[0:1]
    )
    zhat1_ref[...] = normed
    inv1_ref[...] = inverse
    first = normed * gain_ref[0:1] + bias_ref[1:2]
    first_low = first.astype(BF)
    low1_ref[...] = first_low
    for part in range(3):
        at = slice(part * width, part * width + width)
        piece = dot_nn(first_low, wqkv[:, at])
        if part == 0:
            piece = piece + bias_ref[2:3]
        if part == 2:
            piece = piece + bias_ref[3:4]
        triple_ref[:, at] = piece.astype(BF)

    def lanes(part, lane):
        return slice(part * width + lane, part * width + lane + 128)

    if is_text:
        places = list(text_units(len_ref, step, rows // CAP))
        factor = (width // HEADS_T) ** -0.5
    else:
        places = image_units(rows)
        factor = (width // HEADS_I) ** -0.5
    units = []
    for where, lane, mask in places:
        q, k, v = [triple_ref[where, lanes(part, lane)] for part in range(3)]
        units.append((halves(q) if is_text else q, k, v, mask))
    for (where, lane, _), context in zip(places, attend_all(units, factor)):
        context = unhalve(context) if is_text else context
        attended_ref[where, lane : lane + 128] = context.astype(BF)
    normed, inverse = norm_rows(first + dot_nn(attended_ref[...], wo[...]) + bias_ref[4:5])
    zhat2_ref[...] = normed
    inv2_ref[...] = inverse


def row_spec(rows, cols):
    return pl.BlockSpec((rows, cols), lambda i: (i, 0))


def whole_spec(rows, cols):
    return pl.BlockSpec((rows, cols), lambda i: (0, 0))


def attn_forward(is_text, block, lengths, context, inputs, proj, out_w, bias, gain):
    rows, width = inputs.shape
    shape = jax.ShapeDtypeStruct
    return pl.pallas_call(
        functools.partial(attn_forward_kernel, is_text, CO_W + width),
        grid=(rows // block,),
        in_specs=[
            SMEM,
            row_spec(block, CO_W),
            row_spec(block, width),
            ANY,
            ANY,
            whole_spec(8, width),
            whole_spec(3, width),
        ],
        out_specs=[
            row_spec(block, width),
            row_spec(block, 1),
            row_spec(block, width),
            row_spec(block, 3 * width),
            row_spec(block, width),
            row_spec(block, width),
            row_spec(block, 1),
        ],
        out_shape=[
            shape((rows, width), F32),
            shape((rows, 1), F32),
            shape((rows, width), BF),
            shape((rows, 3 * width), BF),
            shape((rows, width), BF),
            shape((rows, width), F32),
            shape((rows, 1), F32),
        ],
        scratch_shapes=[
            pltpu.VMEM((CO_W, width), BF),
            pltpu.VMEM((width, 3 * width), BF),
            pltpu.VMEM((width, width), BF),
            pltpu.SemaphoreType.DMA((3,)),
        ],
        compiler_params=params(),
    )(lengths, context, inputs, proj, out_w, bias, gain)


def ffn_kernel(
    chunk,
    zhat2_ref,
    inv2_ref,
    cot_ref,
    proj_ref,
    out_w_ref,
    up_bias_ref,
    bias_ref,
    gain_ref,
    final_ref,
    low2_ref,
    active_ref,
    third_low_ref,
    hidden_low_ref,
    second_grad_ref,
    sums_ref,
    up_sum_ref,
    wup,
    wdown,
    slope,
    sems,
):
    step = pl.program_id(0)
    width = zhat2_ref.shape[1]
    hidden = wup.shape[1]
    fetch(
        step,
        [
            pltpu.make_async_copy(proj_ref.at[:, pl.ds(3 * width, hidden)], wup, sems.at[0]),
            pltpu.make_async_copy(out_w_ref.at[pl.ds(CO_W + width, hidden)], wdown, sems.at[1]),
        ],
    )

    @pl.when(step == 0)
    def _():
        sums_ref[...] = jnp.zeros_like(sums_ref)
        up_sum_ref[...] = jnp.zeros_like(up_sum_ref)

    second = zhat2_ref[...] * gain_ref[1:2] + bias_ref[5:6]
    second_low = second.astype(BF)
    low2_ref[...] = second_low
    total = second + bias_ref[6:7]
    for start in range(0, hidden, chunk):
        at = slice(start, start + chunk)
        u = dot_nn(second_low, wup[:, at]) + up_bias_ref[:, at]
        phi = 0.5 + 0.5 * lax.erf(u * HALF_ROOT)
        active = (u * phi).astype(BF)
        active_ref[:, at] = active
        slope[:, at] = phi + (u * INV_ROOT) * jnp.exp(-0.5 * u * u)
        total = total + dot_nn(active, wdown[at])
    normed, inverse = norm_rows(total)
    final_ref[...] = normed * gain_ref[2:3] + bias_ref[7:8]
    upstream = cot_ref[...].astype(F32)
    third = norm_back_rows(upstream, gain_ref[2:3], normed, inverse)
    third_low = third.astype(BF)
    third_low_ref[...] = third_low
    sums_ref[0:1] += col_sum(upstream * normed)
    sums_ref[1:2] += col_sum(upstream)
    sums_ref[2:3] += col_sum(third)
    back = third
    for start in range(0, hidden, chunk):
        at = slice(start, start + chunk)
        grad = dot_nt(third_low, wdown[at]) * slope[:, at]
        up_sum_ref[:, at] += col_sum(grad)
        grad_low = grad.astype(BF)
        hidden_low_ref[:, at] = grad_low
        back = back + dot_nt(grad_low, wup[:, at])
    zhat2 = zhat2_ref[...]
    second_grad = norm_back_rows(back, gain_ref[1:2], zhat2, inv2_ref[...])
    second_grad_ref[...] = second_grad
    sums_ref[3:4] += col_sum(back * zhat2)
    sums_ref[4:5] += col_sum(back)
    sums_ref[5:6] += col_sum(second_grad)


def ffn(block, chunk, hidden, zhat2, inv2, cot, proj, out_w, up_bias, bias, gain):
    rows, width = zhat2.shape
    shape = jax.ShapeDtypeStruct
    return pl.pallas_call(
        functools.partial(ffn_kernel, chunk),
        grid=(rows // block,),
        in_specs=[
            row_spec(block, width),
            row_spec(block, 1),
            row_spec(block, width),
            ANY,
            ANY,
            whole_spec(1, hidden),
            whole_spec(8, width),
            whole_spec(3, width),
        ],
        out_specs=[
            row_spec(block, width),
            row_spec(block, width),
            row_spec(block, hidden),
            row_spec(block, width),
            row_spec(block, hidden),
            row_spec(block, width),
            whole_spec(8, width),
            whole_spec(1, hidden),
        ],
        out_shape=[
            shape((rows, width), F32),
            shape((rows, width), BF),
            shape((rows, hidden), BF),
            shape((rows, width), BF),
            shape((rows, hidden), BF),
            shape((rows, width), F32),
            shape((8, width), F32),
            shape((1, hidden), F32),
        ],
        scratch_shapes=[
            pltpu.VMEM((width, hidden), BF),
            pltpu.VMEM((hidden, width), BF),
            pltpu.VMEM((block, hidden), F32),
            pltpu.SemaphoreType.DMA((2,)),
        ],
        compiler_params=params(),
    )(zhat2, inv2, cot, proj, out_w, up_bias, bias, gain)


def attn_backward_kernel(
    is_text,
    len_ref,
    second_grad_ref,
    triple_ref,
    zhat1_ref,
    inv1_ref,
    proj_ref,
    out_w_ref,
    gain_ref,
    second_low_ref,
    triple_low_ref,
    first_grad_ref,
    first_low_ref,
    context_low_ref,
    sums_ref,
    wco,
    wqkv,
    wo,
    upstream,
    sems,
):
    step = pl.program_id(0)
    rows, width = second_grad_ref.shape
    fetch(
        step,
        [
            pltpu.make_async_copy(out_w_ref.at[pl.ds(0, CO_W)], wco, sems.at[0]),
            pltpu.make_async_copy(proj_ref.at[:, pl.ds(0, 3 * width)], wqkv, sems.at[1]),
            pltpu.make_async_copy(out_w_ref.at[pl.ds(CO_W, width)], wo, sems.at[2]),
        ],
    )

    @pl.when(step == 0)
    def _():
        sums_ref[...] = jnp.zeros_like(sums_ref)

    second_low = second_grad_ref[...].astype(BF)
    second_low_ref[...] = second_low
    upstream[...] = dot_nt(second_low, wo[...]).astype(BF)

    def lanes(part, lane):
        return slice(part * width + lane, part * width + lane + 128)

    if is_text:
        places = list(text_units(len_ref, step, rows // CAP))
        factor = (width // HEADS_T) ** -0.5
    else:
        places = image_units(rows)
        factor = (width // HEADS_I) ** -0.5
    units, ups = [], []
    for where, lane, mask in places:
        q, k, v = [triple_ref[where, lanes(part, lane)] for part in range(3)]
        up = upstream[where, lane : lane + 128]
        units.append((halves(q) if is_text else q, k, v, mask))
        ups.append(halves(up) if is_text else up)
    for (where, lane, _), grads in zip(places, attend_back_all(units, ups, factor)):
        dq, dk, dv = grads
        for part, grad in enumerate((unhalve(dq) if is_text else dq, dk, dv)):
            triple_low_ref[where, lanes(part, lane)] = grad.astype(BF)
    back = second_grad_ref[...]
    for part in range(3):
        at = slice(part * width, part * width + width)
        piece = triple_low_ref[:, at]
        back = back + dot_nt(piece, wqkv[:, at])
        if part != 1:
            row = 3 + part // 2
            sums_ref[row : row + 1] += col_sum(piece.astype(F32))
    zhat1 = zhat1_ref[...]
    first_grad = norm_back_rows(back, gain_ref[0:1], zhat1, inv1_ref[...])
    first_grad_ref[...] = first_grad
    sums_ref[0:1] += col_sum(back * zhat1)
    sums_ref[1:2] += col_sum(back)
    sums_ref[2:3] += col_sum(first_grad)
    first_low = first_grad.astype(BF)
    first_low_ref[...] = first_low
    context_low_ref[...] = dot_nt(first_low, wco[...]).astype(BF)


def attn_backward(is_text, block, lengths, second_grad, triple, zhat1, inv1, proj, out_w, gain):
    rows, width = zhat1.shape
    shape = jax.ShapeDtypeStruct
    return pl.pallas_call(
        functools.partial(attn_backward_kernel, is_text),
        grid=(rows // block,),
        in_specs=[
            SMEM,
            row_spec(block, width),
            row_spec(block, 3 * width),
            row_spec(block, width),
            row_spec(block, 1),
            ANY,
            ANY,
            whole_spec(3, width),
        ],
        out_specs=[
            row_spec(block, width),
            row_spec(block, 3 * width),
            row_spec(block, width),
            row_spec(block, width),
            row_spec(block, CO_W),
            whole_spec(8, width),
        ],
        out_shape=[
            shape((rows, width), BF),
            shape((rows, 3 * width), BF),
            shape((rows, width), F32),
            shape((rows, width), BF),
            shape((rows, CO_W), BF),
            shape((8, width), F32),
        ],
        scratch_shapes=[
            pltpu.VMEM((CO_W, width), BF),
            pltpu.VMEM((width, 3 * width), BF),
            pltpu.VMEM((width, width), BF),
            pltpu.VMEM((block, width), BF),
            pltpu.SemaphoreType.DMA((3,)),
        ],
        compiler_params=params(),
    )(lengths, second_grad, triple, zhat1, inv1, proj, out_w, gain)


def weight_grad(inputs, upstream):
    return dot_tn(inputs, upstream).astype(BF)


def co_project(inputs, weight, wide):
    bias = jnp.concatenate([wide[:CO_W], jnp.zeros((CO_W,), F32), wide[CO_W : 2 * CO_W]])
    return (dot_nn(inputs, weight[:, : 3 * CO_W]) + bias).astype(BF)


def pad_pairs(block):
    wide = block.reshape(-1, REGIONS, block.shape[1])
    return jnp.pad(wide, ((0, 0), (0, SLOTS - REGIONS), (0, 0))).reshape(-1, block.shape[1])


def unpad_pairs(block):
    return block.reshape(-1, SLOTS, block.shape[1])[:, :REGIONS].reshape(-1, block.shape[1])


def shards(
    text_in,
    image_in,
    lengths,
    t_proj,
    t_out,
    t_bias_wide,
    t_bias,
    t_gain,
    i_proj,
    i_out,
    i_bias_wide,
    i_bias,
    i_gain,
    text_cot,
    image_cot,
):
    small = (t_bias_wide, t_bias, t_gain, i_bias_wide, i_bias, i_gain)
    flat = jnp.concatenate([piece.reshape(-1) for piece in small])
    t_rows = t_proj.shape[0]
    extra = -(-flat.shape[0] // (t_rows * 128)) * 128
    riders = jnp.pad(flat, (0, extra * t_rows - flat.shape[0])).reshape(t_rows, extra)
    near_image = over_x(image_in)
    near_cot = over_x(image_cot)

    t_co = gather_rows(jnp.concatenate([t_proj[:, : 3 * CO_W], riders], 1), True)
    i_co = gather_rows(i_proj[:, : 3 * CO_W], False)
    t_outw = gather_rows(t_out, True)
    i_outw = gather_rows(i_out, False)
    i_rest = gather_rows(i_proj[:, 3 * CO_W :], True)
    t_rest = gather_rows(t_proj[:, 3 * CO_W :], False)

    shard_count = t_co.shape[0] // t_rows
    table = t_co[:, 3 * CO_W :].reshape(shard_count, -1)[:, : flat.shape[0]].astype(F32)
    taken = []
    offset = 0
    for piece in small:
        block = table[:, offset : offset + piece.size].reshape((shard_count,) + piece.shape)
        offset += piece.size
        if piece.ndim == 1:
            taken.append(block.reshape(1, -1))
        else:
            taken.append(block.transpose(1, 0, 2).reshape(piece.shape[0], -1))
    t_wide, t_rows8, t_gains, i_wide, i_rows8, i_gains = taken

    image_rows = pad_pairs(near_image)
    image_up = pad_pairs(near_cot)
    text_co = co_project(text_in, t_co, t_wide[0])
    image_co = co_project(image_rows, i_co, i_wide[0])
    text_context, image_context = co_forward(lengths, text_co, image_co)

    image_block = image_rows.shape[0]
    streams = (
        (True, 256, 512, text_context, text_in, text_cot, t_rest, t_outw, t_wide, t_rows8, t_gains),
        (
            False,
            image_block,
            512,
            image_context,
            image_rows,
            image_up,
            i_rest,
            i_outw,
            i_wide,
            i_rows8,
            i_gains,
        ),
    )
    finished = []
    for is_text, block, chunk, context, inputs, cot, rest, outw, wide, rows8, gains in streams:
        width = inputs.shape[1]
        hidden = wide.shape[1] - 2 * CO_W
        zhat1, inv1, low1, triple, attended, zhat2, inv2 = attn_forward(
            is_text, block, lengths, context, inputs, rest, outw, rows8, gains
        )
        final, low2, active, third_low, hidden_low, second_grad, sums2, up_sum = ffn(
            block, chunk, hidden, zhat2, inv2, cot, rest, outw, wide[:, 2 * CO_W :], rows8, gains
        )
        up_grad = weight_grad(low2, hidden_low)
        down_grad = weight_grad(active, third_low)
        second_low, triple_low, first_grad, first_low, context_low, sums1 = attn_backward(
            is_text, block, lengths, second_grad, triple, zhat1, inv1, rest, outw, gains
        )
        triple_grad = weight_grad(low1, triple_low)
        out_grad = jnp.concatenate(
            [weight_grad(context, first_low), weight_grad(attended, second_low), down_grad], 0
        )
        finished.append(
            (final, first_grad, context_low, up_grad, triple_grad, out_grad, sums1, sums2, up_sum)
        )
    (
        (t_final, t_first, t_ctx, t_up, t_qkv, t_outg, t_sums1, t_sums2, t_upsum),
        (i_final, i_first, i_ctx, i_up, i_qkv, i_outg, i_sums1, i_sums2, i_upsum),
    ) = finished

    image_final = over_x(unpad_pairs(i_final).astype(BF)).astype(F32)

    t_co_grad, i_co_grad, t_co_sum, i_co_sum = co_backward(
        lengths, text_co, image_co, t_ctx, i_ctx
    )
    text_grad = t_first + dot_nt(t_co_grad, t_co[:, : 3 * CO_W])
    image_grad = i_first + dot_nt(i_co_grad, i_co)
    image_grad = over_x(unpad_pairs(image_grad).astype(BF)).astype(F32)

    def small_grads(sums1, sums2, up_sum, co_sum):
        wide = jnp.concatenate([co_sum[0, :CO_W], co_sum[0, 2 * CO_W :], up_sum[0]])
        rows8 = jnp.stack(
            [sums1[2], sums1[1], sums1[3], sums1[4], sums2[5], sums2[4], sums2[2], sums2[1]]
        )
        return wide, rows8, jnp.stack([sums1[0], sums2[3], sums2[0]])

    pieces = small_grads(t_sums1, t_sums2, t_upsum, t_co_sum) + small_grads(
        i_sums1, i_sums2, i_upsum, i_co_sum
    )
    packed = []
    for piece in pieces:
        if piece.ndim == 1:
            packed.append(piece.reshape(shard_count, -1))
        else:
            packed.append(
                piece.reshape(piece.shape[0], shard_count, -1)
                .transpose(1, 0, 2)
                .reshape(shard_count, -1)
            )
    packed = jnp.concatenate(packed, 1)
    count = packed.shape[1]
    packed = jnp.pad(packed, ((0, 0), (0, extra * t_rows - count))).reshape(-1, extra).astype(BF)

    t_up = scatter_rows(t_up, True)
    i_up = scatter_rows(i_up, False)
    t_qkv = scatter_rows(t_qkv, False)
    i_qkv = scatter_rows(i_qkv, True)
    t_outg = scatter_rows(t_outg, True)
    i_outg = scatter_rows(i_outg, False)
    i_cog = scatter_rows(weight_grad(image_rows, i_co_grad), True)
    t_cog = scatter_rows(
        jnp.concatenate([weight_grad(text_in, t_co_grad), packed], 1), False
    )

    mine = t_cog[:, 3 * CO_W :].reshape(-1)
    outs = []
    offset = 0
    for piece in small:
        outs.append(mine[offset : offset + piece.size].reshape(piece.shape))
        offset += piece.size
    t_wide_g, t_rows_g, t_gain_g, i_wide_g, i_rows_g, i_gain_g = outs
    return (
        t_final,
        image_final,
        text_grad,
        image_grad,
        jnp.concatenate([t_cog[:, : 3 * CO_W], t_qkv, t_up], 1),
        t_outg,
        t_wide_g,
        t_rows_g,
        t_gain_g,
        jnp.concatenate([i_cog, i_qkv, i_up], 1),
        i_outg,
        i_wide_g,
        i_rows_g,
        i_gain_g,
    )


def solution(mesh):
    both = ("stream", "dp")
    rows, cols, flat = P(both, None), P(None, both), P(both)
    weights = (rows, rows, flat, cols, cols)
    return jax.shard_map(
        shards,
        mesh=mesh,
        in_specs=(rows, rows, flat) + weights + weights + (rows, rows),
        out_specs=(rows, rows, rows, rows) + weights + weights,
        check_vma=False,
    )
```

```python
import functools

import jax
import jax.numpy as jnp
from jax import lax
from jax.experimental import pallas as pl
from jax.experimental.pallas import tpu as pltpu
from jax.sharding import PartitionSpec as P

CO_W = 1024
HEADS_T = 12
HEADS_I = 8
CO_HEADS = 8
CAP = 128
REGIONS = 36
SLOTS = 48

epsilon = 1e-05
negative = -1e30
BF = jnp.bfloat16
F32 = jnp.float32
VMEM_LIMIT = 60 * 1024 * 1024
HALF_ROOT = 0.7071067811865476
INV_ROOT = 0.3989422804014327
ANY = pl.BlockSpec(memory_space=pl.ANY)
SMEM = pl.BlockSpec(memory_space=pltpu.SMEM)


def dot_nn(a, b):
    return lax.dot_general(a, b, (((1,), (0,)), ((), ())), preferred_element_type=F32)


def dot_nt(a, b):
    return lax.dot_general(a, b, (((1,), (1,)), ((), ())), preferred_element_type=F32)


def dot_tn(a, b):
    return lax.dot_general(a, b, (((0,), (0,)), ((), ())), preferred_element_type=F32)


def params():
    return pltpu.CompilerParams(vmem_limit_bytes=VMEM_LIMIT)


def call(kernel, deps, operands, in_specs, **kwargs):
    count = len(operands)

    def body(*refs):
        kernel(*refs[:count], *refs[count + len(deps) :])

    return pl.pallas_call(
        body,
        in_specs=in_specs + [ANY] * len(deps),
        compiler_params=params(),
        **kwargs,
    )(*operands, *deps)


def cost(gmacs, mbytes):
    return pl.CostEstimate(
        flops=int(2e9 * gmacs), bytes_accessed=int(1e6 * mbytes), transcendentals=0
    )


def dp_parts():
    total = lax.axis_size("dp")
    index = lax.axis_index("dp")
    return total // 4, index // 4, (index // 2) % 2, index % 2


def over_core(block):
    total = lax.axis_size("dp")
    return lax.ppermute(block, "dp", [(d, d ^ 1) for d in range(total)])


def over_y(block):
    total = lax.axis_size("dp")
    return lax.ppermute(block, "dp", [(d, d ^ 2) for d in range(total)])


def over_x(block):
    total = lax.axis_size("stream")
    return lax.ppermute(block, "stream", [(d, d ^ 1) for d in range(total)])


def over_z(block, shift):
    total = lax.axis_size("dp")
    return lax.ppermute(block, "dp", [(d, (d + 4 * shift) % total) for d in range(total)])


def pick(buffer, position, axis):
    return lax.dynamic_index_in_dim(buffer, position, axis, keepdims=False)


def place_kernel(blocks, table_ref, *refs):
    count = (len(refs) - 3) // 2
    pieces, out_ref = refs[:count], refs[count]
    held, in_sems, out_sems = refs[count + 1 : 2 * count + 1], refs[2 * count + 1], refs[2 * count + 2]
    loads, stores = [], []
    for number in range(count * blocks):
        piece, block = number // blocks, number % blocks
        x, y, c = [table_ref[3 * number + i] for i in range(3)]
        loads.append(
            pltpu.make_async_copy(pieces[piece].at[block], held[piece].at[block], in_sems.at[number])
        )
        stores.append(
            pltpu.make_async_copy(
                held[piece].at[block], out_ref.at[x, :, y, c], out_sems.at[number]
            )
        )
    for load in loads:
        load.start()
    for load, store in zip(loads, stores):
        load.wait()
        store.start()
    for store in stores:
        store.wait()


def place(pieces, table, deps):
    blocks, nz, rows, cols = pieces[0].shape
    size = 4 * len(pieces) * pieces[0].size
    return call(
        functools.partial(place_kernel, blocks),
        deps,
        (table, *pieces),
        [SMEM] + [ANY] * len(pieces),
        out_specs=ANY,
        out_shape=jax.ShapeDtypeStruct((2, nz, 2, 2, rows, cols), pieces[0].dtype),
        scratch_shapes=[pltpu.VMEM(piece.shape, piece.dtype) for piece in pieces]
        + [pltpu.SemaphoreType.DMA((len(pieces) * blocks,))] * 2,
        cost_estimate=pl.CostEstimate(flops=0, bytes_accessed=size, transcendentals=0),
    )


def table_of(rows):
    return jnp.stack([jnp.asarray(v, jnp.int32) for row in rows for v in row])


def z_groups():
    total = lax.axis_size("dp")
    return [[first + 4 * k for k in range(total // 4)] for first in range(4)]


def after_kernel(*refs):
    pass


def after(block, *earlier):
    return pl.pallas_call(
        after_kernel,
        in_specs=[ANY] * (1 + len(earlier)),
        out_specs=ANY,
        out_shape=jax.ShapeDtypeStruct(block.shape, block.dtype),
        input_output_aliases={0: 0},
        compiler_params=params(),
        cost_estimate=pl.CostEstimate(flops=0, bytes_accessed=0, transcendentals=0),
    )(block, *earlier)


def column_by_permutes(own):
    nz, z, _, _ = dp_parts()
    came = jnp.stack([own] + [over_z(own, shift) for shift in range(1, nz)])
    turned = jnp.concatenate([came[::-1]] * 2)
    return lax.dynamic_slice_in_dim(turned, nz - 1 - z, nz, 0)


def column_by_gather(own, rows, cols):
    full = lax.all_gather(own, "dp", axis_index_groups=z_groups(), axis=0)
    return full[:, :rows, :cols]


class Gather:
    def __init__(self, column, y_first):
        self.column = column
        self.links = (over_y, over_x) if y_first else (over_x, over_y)
        self.y_first = y_first
        self.over = self.links[0](column)

    def second(self):
        self.pair = jnp.stack([self.column, self.over])
        self.far = self.links[1](self.pair)

    def core(self):
        self.others = [over_core(self.pair), over_core(self.far)]

    def full(self, deps):
        _, _, y, c = dp_parts()
        x = lax.axis_index("stream")
        table = []
        for core in (0, 1):
            for outer in (0, 1):
                for inner in (0, 1):
                    dx, dy = (outer, inner) if self.y_first else (inner, outer)
                    table.append((x ^ dx, y ^ dy, c ^ core))
        whole = place([self.pair, self.far] + self.others, table_of(table), deps)
        return whole.reshape(-1, whole.shape[-1])


def add_low(kept, came):
    return (kept.astype(F32) + came.astype(F32)).astype(BF)


class Scatter:
    def __init__(self, halves, y_first):
        self.send, self.keep = halves
        self.came = over_core(self.send)
        self.axes = ("y", "x") if y_first else ("x", "y")

    def link(self):
        axis, self.axes = self.axes[0], self.axes[1:]
        at = dp_parts()[2] if axis == "y" else lax.axis_index("stream")
        self.send = add_low(pick(self.keep, 1 - at, 0), pick(self.came, 1 - at, 0))
        self.keep = add_low(pick(self.keep, at, 0), pick(self.came, at, 0))
        self.came = over_y(self.send) if axis == "y" else over_x(self.send)

    def column_by_permutes(self):
        nz, z, _, _ = dp_parts()
        self.send = add_low(self.keep, self.came)
        self.sum = pick(self.send, z, 0).astype(F32)
        for shift in range(1, nz):
            came = over_z(pick(self.send, (z + shift) % nz, 0), shift)
            self.sum = self.sum + came.astype(F32)

    def column(self):
        self.send = add_low(self.keep, self.came)
        self.sum = lax.psum_scatter(
            self.send.reshape(-1, self.send.shape[-1]),
            "dp",
            axis_index_groups=z_groups(),
            scatter_dimension=0,
            tiled=True,
        )

    def total(self):
        return self.sum.astype(F32)


def store_halves(y_first, core_ref, send_ref, keep_ref, block, at):
    columns, rows = send_ref.shape[:2]
    nz = columns // 4

    def store(even_ref, odd_ref):
        for number in range(columns):
            x, z, y = number // (2 * nz), number // 2 % nz, number % 2
            spot = (y * 2 + x if y_first else x * 2 + y) * nz + z
            start = 2 * number * rows
            even_ref[spot, :, at] = block[start : start + rows].astype(BF)
            odd_ref[spot, :, at] = block[start + rows : start + 2 * rows].astype(BF)

    @pl.when(core_ref[0] == 0)
    def _():
        store(keep_ref, send_ref)

    @pl.when(core_ref[0] == 1)
    def _():
        store(send_ref, keep_ref)


def cols_grad_kernel(y_first, counts, tile, has_riders, core_ref, *refs):
    segments = len(counts)
    lhs, ups = refs[:segments], refs[segments : 2 * segments]
    riders = refs[2 * segments] if has_riders else None
    send_ref, keep_ref = refs[2 * segments + has_riders : 2 * segments + has_riders + 2]
    turned = refs[2 * segments + has_riders + 2 :]
    step = pl.program_id(0)

    @pl.when(step == 0)
    def _():
        for flat, kept in zip(lhs, turned):
            kept[...] = flat[...].T

    first = 0
    for count, kept, up in zip(counts, turned, ups):

        @pl.when((step >= first) & (step < first + count))
        def _(kept=kept, up=up):
            at = pl.ds(pl.multiple_of(step * tile, 128), tile) if has_riders else slice(None)
            store_halves(y_first, core_ref, send_ref, keep_ref, dot_nn(kept[...], up[...]), at)

        first += count
    if has_riders:

        @pl.when(step == 0)
        def _():
            width = riders.shape[1]
            start = sum(counts) * tile
            store_halves(y_first, core_ref, send_ref, keep_ref, riders[...], slice(start, start + width))


def half_shapes(shards, rows, cols):
    return [jax.ShapeDtypeStruct((shards // 2, rows, cols), BF)] * 2


def cols_grad(shards, y_first, segments, tile, riders=None, deps=()):
    counts = [up.shape[1] // tile for _, up in segments]
    width = segments[0][0].shape[1]
    length = segments[0][0].shape[0]
    rows = width // shards
    total = sum(counts) * tile + (0 if riders is None else riders.shape[1])
    starts = [sum(counts[:i]) for i in range(len(counts))]

    def up_spec(start, count):
        return pl.BlockSpec((length, tile), lambda j: (0, jnp.clip(j - start, 0, count - 1)))

    whole = [pl.BlockSpec(lhs.shape, lambda j: (0, 0)) for lhs, _ in segments]
    tiles = [up_spec(start, count) for start, count in zip(starts, counts)]
    extra = [] if riders is None else [riders]
    core = jnp.reshape(dp_parts()[3], (1,)).astype(jnp.int32)
    if riders is None:
        out = pl.BlockSpec((shards // 2, rows, tile), lambda j: (0, 0, j))
    else:
        out = pl.BlockSpec((shards // 2, rows, total), lambda j: (0, 0, 0))
    halves = call(
        functools.partial(cols_grad_kernel, y_first, counts, tile, len(extra)),
        deps,
        (core,) + tuple(lhs for lhs, _ in segments) + tuple(up for _, up in segments) + tuple(extra),
        [SMEM] + whole + tiles + [pl.BlockSpec(block.shape, lambda j: (0, 0)) for block in extra],
        grid=(sum(counts),),
        out_specs=[out, out],
        out_shape=half_shapes(shards, rows, total),
        scratch_shapes=[pltpu.VMEM((width, length), BF) for _ in segments],
        cost_estimate=cost(1.3e-9 * length * width * total, 20),
    )
    return [half.reshape(2, 2, -1, rows, total) for half in halves]


def rows_grad_kernel(y_first, segments, tile, core_ref, *refs):
    lhs, ups = refs[:segments], refs[segments : 2 * segments]
    send_ref, keep_ref, total = refs[2 * segments : 2 * segments + 3]
    turned = refs[2 * segments + 3 :]

    @pl.when(pl.program_id(0) == 0)
    def _():
        for flat, kept in zip(lhs, turned):
            kept[...] = flat[...].T

    start = 0
    for kept, up in zip(turned, ups):
        for row in range(0, kept.shape[0], 256):
            total[start + row : start + row + 256] = dot_nn(kept[row : row + 256], up[...])
        start += kept.shape[0]
    store_halves(y_first, core_ref, send_ref, keep_ref, total, slice(None))


def rows_grad(shards, y_first, segments, tile, deps=()):
    length = segments[0][0].shape[0]
    height = sum(lhs.shape[1] for lhs, _ in segments)
    width = segments[0][1].shape[1]
    rows = height // shards
    core = jnp.reshape(dp_parts()[3], (1,)).astype(jnp.int32)
    out = pl.BlockSpec((shards // 2, rows, tile), lambda j: (0, 0, j))
    halves = call(
        functools.partial(rows_grad_kernel, y_first, len(segments), tile),
        deps,
        (core,) + tuple(lhs for lhs, _ in segments) + tuple(up for _, up in segments),
        [SMEM]
        + [
            pl.BlockSpec(lhs.shape, lambda j: (0, 0), pipeline_mode=pl.Buffered(1))
            for lhs, _ in segments
        ]
        + [pl.BlockSpec((length, tile), lambda j: (0, j)) for _ in segments],
        grid=(width // tile,),
        out_specs=[out, out],
        out_shape=half_shapes(shards, rows, width),
        scratch_shapes=[pltpu.VMEM((height, tile), F32)]
        + [pltpu.VMEM((lhs.shape[1], length), BF) for lhs, _ in segments],
        cost_estimate=cost(1.3e-9 * length * height * width, 20),
    )
    return [half.reshape(2, 2, -1, rows, width) for half in halves]


def softmax_rows(scores):
    high = jnp.max(scores, -1, keepdims=True)
    exponent = jnp.exp(scores - high)
    return exponent * (1.0 / jnp.sum(exponent, -1, keepdims=True))


def norm_rows(pre_norm):
    centered = pre_norm - jnp.mean(pre_norm, -1, keepdims=True)
    inverse = lax.rsqrt(jnp.mean(centered * centered, -1, keepdims=True) + epsilon)
    return centered * inverse, inverse


def norm_back_rows(upstream, gain, normed, inverse):
    scaled = upstream * gain
    return inverse * (
        scaled
        - jnp.mean(scaled, -1, keepdims=True)
        - normed * jnp.mean(scaled * normed, -1, keepdims=True)
    )


def col_sum(block):
    return jnp.sum(block, 0, keepdims=True)


def key_mask(shape, count):
    return jnp.where(lax.broadcasted_iota(jnp.int32, shape, 1) < count, 0.0, negative)


def attend_all(units, factor):
    scores = [dot_nt(q, k) * factor + mask for q, k, _, mask in units]
    probs = [softmax_rows(score).astype(BF) for score in scores]
    return [dot_nn(prob, unit[2]) for prob, unit in zip(probs, units)]


def attend_back_all(units, upstreams, factor):
    scores = [dot_nt(q, k) * factor + mask for q, k, _, mask in units]
    raised = [dot_nt(up, unit[2]) for up, unit in zip(upstreams, units)]
    probs = [softmax_rows(score) for score in scores]
    values_grad = [dot_tn(prob.astype(BF), up) for prob, up in zip(probs, upstreams)]
    rounded = [
        (prob * (grad - jnp.sum(prob * grad, -1, keepdims=True)) * factor).astype(BF)
        for prob, grad in zip(probs, raised)
    ]
    queries_grad = [dot_nn(low, unit[1]) for low, unit in zip(rounded, units)]
    keys_grad = [dot_tn(low, unit[0]) for low, unit in zip(rounded, units)]
    return list(zip(queries_grad, keys_grad, values_grad))


def co_forward_kernel(len_ref, text_ref, image_ref, text_out, image_out):
    step = pl.program_id(0)
    factor = (CO_W // CO_HEADS) ** -0.5
    region_mask = key_mask((1, SLOTS), REGIONS)
    text_mask = key_mask((1, CAP), len_ref[step])
    units, places = [], []
    for head in range(CO_HEADS):
        at = [slice(part * CO_W + head * 128, part * CO_W + head * 128 + 128) for part in range(3)]
        tq, tk, tv = [text_ref[:, where] for where in at]
        iq, ik, iv = [image_ref[:, where] for where in at]
        units += [(tq, ik, iv, region_mask), (iq, tk, tv, text_mask)]
        places += [(text_out, at[0]), (image_out, at[0])]
    for (out_ref, where), context in zip(places, attend_all(units, factor)):
        out_ref[:, where] = context.astype(BF)


def co_forward(lengths, text_co, image_co, deps):
    pairs = lengths.shape[0]
    return call(
        co_forward_kernel,
        deps,
        (lengths, text_co, image_co,),
        [
            SMEM,
            pl.BlockSpec((CAP, 3 * CO_W), lambda i: (i, 0)),
            pl.BlockSpec((SLOTS, 3 * CO_W), lambda i: (i, 0)),
        ],
        grid=(pairs,),
        out_specs=[
            pl.BlockSpec((CAP, CO_W), lambda i: (i, 0)),
            pl.BlockSpec((SLOTS, CO_W), lambda i: (i, 0)),
        ],
        out_shape=[
            jax.ShapeDtypeStruct((pairs * CAP, CO_W), BF),
            jax.ShapeDtypeStruct((pairs * SLOTS, CO_W), BF),
        ],
        cost_estimate=cost(2 * lengths.shape[0] * 0.4, 8),
    )


def co_backward_kernel(
    len_ref, text_ref, image_ref, text_up, image_up, text_out, image_out, text_sum, image_sum
):
    step = pl.program_id(0)
    factor = (CO_W // CO_HEADS) ** -0.5
    region_mask = key_mask((1, SLOTS), REGIONS)
    text_mask = key_mask((1, CAP), len_ref[step])

    @pl.when(step == 0)
    def _():
        text_sum[...] = jnp.zeros_like(text_sum)
        image_sum[...] = jnp.zeros_like(image_sum)

    def store(out_ref, sum_ref, where, grad):
        low = grad.astype(BF)
        out_ref[:, where] = low
        sum_ref[:, where] += col_sum(low.astype(F32))

    units, ups, places = [], [], []
    for head in range(CO_HEADS):
        at = [slice(part * CO_W + head * 128, part * CO_W + head * 128 + 128) for part in range(3)]
        tq, tk, tv = [text_ref[:, where] for where in at]
        iq, ik, iv = [image_ref[:, where] for where in at]
        units += [(tq, ik, iv, region_mask), (iq, tk, tv, text_mask)]
        ups += [text_up[:, at[0]], image_up[:, at[0]]]
        places.append(at)
    grads = attend_back_all(units, ups, factor)
    for head, at in enumerate(places):
        dtq, dik, div = grads[2 * head]
        diq, dtk, dtv = grads[2 * head + 1]
        for where, grad in zip(at, (dtq, dtk, dtv)):
            store(text_out, text_sum, where, grad)
        for where, grad in zip(at, (diq, dik, div)):
            store(image_out, image_sum, where, grad)


def co_backward(lengths, text_co, image_co, text_up, image_up, deps):
    pairs = lengths.shape[0]
    wide = 3 * CO_W
    return call(
        co_backward_kernel,
        deps,
        (lengths, text_co, image_co, text_up, image_up,),
        [
            SMEM,
            pl.BlockSpec((CAP, wide), lambda i: (i, 0)),
            pl.BlockSpec((SLOTS, wide), lambda i: (i, 0)),
            pl.BlockSpec((CAP, CO_W), lambda i: (i, 0)),
            pl.BlockSpec((SLOTS, CO_W), lambda i: (i, 0)),
        ],
        grid=(pairs,),
        out_specs=[
            pl.BlockSpec((CAP, wide), lambda i: (i, 0)),
            pl.BlockSpec((SLOTS, wide), lambda i: (i, 0)),
            pl.BlockSpec((1, wide), lambda i: (0, 0)),
            pl.BlockSpec((1, wide), lambda i: (0, 0)),
        ],
        out_shape=[
            jax.ShapeDtypeStruct((pairs * CAP, wide), BF),
            jax.ShapeDtypeStruct((pairs * SLOTS, wide), BF),
            jax.ShapeDtypeStruct((1, wide), F32),
            jax.ShapeDtypeStruct((1, wide), F32),
        ],
        cost_estimate=cost(2 * lengths.shape[0] * 0.5, 20),
    )


def fetch(step, copies):
    @pl.when(step == 0)
    def _():
        for copy in copies:
            copy.start()

    def arrived(number):
        @pl.when(step == 0)
        def _():
            copies[number].wait()

    return arrived


def text_units(len_ref, step, pair_count):
    for pair in range(pair_count):
        mask = key_mask((1, CAP), len_ref[step * pair_count + pair])
        for block in range(HEADS_T // 2):
            yield slice(pair * CAP, pair * CAP + CAP), block * 128, mask


def image_mask():
    shape = (2 * SLOTS, 2 * SLOTS)
    row = lax.broadcasted_iota(jnp.int32, shape, 0)
    col = lax.broadcasted_iota(jnp.int32, shape, 1)
    same = (row >= SLOTS) == (col >= SLOTS)
    local = jnp.where(col >= SLOTS, col - SLOTS, col)
    return jnp.where(same & (local < REGIONS), 0.0, negative)


def image_units(rows):
    mask = image_mask()
    return [
        (slice(start, start + 2 * SLOTS), head * 128, mask)
        for start in range(0, rows, 2 * SLOTS)
        for head in range(HEADS_I)
    ]


def halves(block):
    low = lax.broadcasted_iota(jnp.int32, block.shape, 1) < 64
    zero = jnp.zeros_like(block)
    return jnp.concatenate([jnp.where(low, block, zero), jnp.where(low, zero, block)], 0)


def unhalve(stacked):
    rows = stacked.shape[0] // 2
    low = lax.broadcasted_iota(jnp.int32, (rows, stacked.shape[1]), 1) < 64
    return jnp.where(low, stacked[:rows], stacked[rows:])


def attn_forward_kernel(
    is_text,
    down_at,
    len_ref,
    context_ref,
    input_ref,
    proj_ref,
    out_w_ref,
    bias_ref,
    gain_ref,
    zhat1_ref,
    inv1_ref,
    low1_ref,
    triple_ref,
    attended_ref,
    zhat2_ref,
    inv2_ref,
    wco,
    wqkv,
    wo,
    sems,
):
    step = pl.program_id(0)
    width = input_ref.shape[1]
    rows = input_ref.shape[0]
    arrived = fetch(
        step,
        [
            pltpu.make_async_copy(out_w_ref.at[pl.ds(0, CO_W)], wco, sems.at[0]),
            pltpu.make_async_copy(proj_ref.at[:, pl.ds(0, 3 * width)], wqkv, sems.at[1]),
            pltpu.make_async_copy(out_w_ref.at[pl.ds(CO_W, width)], wo, sems.at[2]),
        ],
    )
    arrived(0)
    normed, inverse = norm_rows(
        input_ref[...].astype(F32) + dot_nn(context_ref[...], wco[...]) + bias_ref[0:1]
    )
    zhat1_ref[...] = normed
    inv1_ref[...] = inverse
    first = normed * gain_ref[0:1] + bias_ref[1:2]
    first_low = first.astype(BF)
    low1_ref[...] = first_low
    arrived(1)
    for part in range(3):
        at = slice(part * width, part * width + width)
        piece = dot_nn(first_low, wqkv[:, at])
        if part == 0:
            piece = piece + bias_ref[2:3]
        if part == 2:
            piece = piece + bias_ref[3:4]
        triple_ref[:, at] = piece.astype(BF)

    def lanes(part, lane):
        return slice(part * width + lane, part * width + lane + 128)

    if is_text:
        places = list(text_units(len_ref, step, rows // CAP))
        factor = (width // HEADS_T) ** -0.5
    else:
        places = image_units(rows)
        factor = (width // HEADS_I) ** -0.5
    units = []
    for where, lane, mask in places:
        q, k, v = [triple_ref[where, lanes(part, lane)] for part in range(3)]
        units.append((halves(q) if is_text else q, k, v, mask))
    for (where, lane, _), context in zip(places, attend_all(units, factor)):
        context = unhalve(context) if is_text else context
        attended_ref[where, lane : lane + 128] = context.astype(BF)
    arrived(2)
    normed, inverse = norm_rows(first + dot_nn(attended_ref[...], wo[...]) + bias_ref[4:5])
    zhat2_ref[...] = normed
    inv2_ref[...] = inverse


def row_spec(rows, cols):
    return pl.BlockSpec((rows, cols), lambda i: (i, 0))


def whole_spec(rows, cols):
    return pl.BlockSpec((rows, cols), lambda i: (0, 0))


def attn_forward(is_text, block, lengths, context, inputs, proj, out_w, bias, gain, deps):
    rows, width = inputs.shape
    shape = jax.ShapeDtypeStruct
    return call(
        functools.partial(attn_forward_kernel, is_text, CO_W + width),
        deps,
        (lengths, context, inputs, proj, out_w, bias, gain,),
        [
            SMEM,
            row_spec(block, CO_W),
            row_spec(block, width),
            ANY,
            ANY,
            whole_spec(8, width),
            whole_spec(3, width),
        ],
        grid=(rows // block,),
        out_specs=[
            row_spec(block, width),
            row_spec(block, 1),
            row_spec(block, width),
            row_spec(block, 3 * width),
            row_spec(block, width),
            row_spec(block, width),
            row_spec(block, 1),
        ],
        out_shape=[
            shape((rows, width), F32),
            shape((rows, 1), F32),
            shape((rows, width), BF),
            shape((rows, 3 * width), BF),
            shape((rows, width), BF),
            shape((rows, width), F32),
            shape((rows, 1), F32),
        ],
        scratch_shapes=[
            pltpu.VMEM((CO_W, width), BF),
            pltpu.VMEM((width, 3 * width), BF),
            pltpu.VMEM((width, width), BF),
            pltpu.SemaphoreType.DMA((3,)),
        ],
        cost_estimate=cost(rows * width * width * 1.6e-8, 40),
    )


def ffn_kernel(
    chunk,
    zhat2_ref,
    inv2_ref,
    cot_ref,
    proj_ref,
    out_w_ref,
    up_bias_ref,
    bias_ref,
    gain_ref,
    final_ref,
    low2_ref,
    active_ref,
    third_low_ref,
    hidden_low_ref,
    second_grad_ref,
    sums_ref,
    up_sum_ref,
    wup,
    wdown,
    slope,
    sems,
):
    step = pl.program_id(0)
    width = zhat2_ref.shape[1]
    hidden = wup.shape[1]
    arrived = fetch(
        step,
        [
            pltpu.make_async_copy(proj_ref.at[:, pl.ds(3 * width, hidden)], wup, sems.at[0]),
            pltpu.make_async_copy(out_w_ref.at[pl.ds(CO_W + width, hidden)], wdown, sems.at[1]),
        ],
    )

    @pl.when(step == 0)
    def _():
        sums_ref[...] = jnp.zeros_like(sums_ref)
        up_sum_ref[...] = jnp.zeros_like(up_sum_ref)

    arrived(0)
    arrived(1)
    second = zhat2_ref[...] * gain_ref[1:2] + bias_ref[5:6]
    second_low = second.astype(BF)
    low2_ref[...] = second_low
    total = second + bias_ref[6:7]
    for start in range(0, hidden, chunk):
        at = slice(start, start + chunk)
        u = dot_nn(second_low, wup[:, at]) + up_bias_ref[:, at]
        phi = 0.5 + 0.5 * lax.erf(u * HALF_ROOT)
        active = (u * phi).astype(BF)
        active_ref[:, at] = active
        slope[:, at] = phi + (u * INV_ROOT) * jnp.exp(-0.5 * u * u)
        total = total + dot_nn(active, wdown[at])
    normed, inverse = norm_rows(total)
    final_ref[...] = normed * gain_ref[2:3] + bias_ref[7:8]
    upstream = cot_ref[...].astype(F32)
    third = norm_back_rows(upstream, gain_ref[2:3], normed, inverse)
    third_low = third.astype(BF)
    third_low_ref[...] = third_low
    sums_ref[0:1] += col_sum(upstream * normed)
    sums_ref[1:2] += col_sum(upstream)
    sums_ref[2:3] += col_sum(third)
    back = third
    for start in range(0, hidden, chunk):
        at = slice(start, start + chunk)
        grad = dot_nt(third_low, wdown[at]) * slope[:, at]
        up_sum_ref[:, at] += col_sum(grad)
        grad_low = grad.astype(BF)
        hidden_low_ref[:, at] = grad_low
        back = back + dot_nt(grad_low, wup[:, at])
    zhat2 = zhat2_ref[...]
    second_grad = norm_back_rows(back, gain_ref[1:2], zhat2, inv2_ref[...])
    second_grad_ref[...] = second_grad
    sums_ref[3:4] += col_sum(back * zhat2)
    sums_ref[4:5] += col_sum(back)
    sums_ref[5:6] += col_sum(second_grad)


def ffn(block, chunk, hidden, zhat2, inv2, cot, proj, out_w, up_bias, bias, gain, deps):
    rows, width = zhat2.shape
    shape = jax.ShapeDtypeStruct
    return call(
        functools.partial(ffn_kernel, chunk),
        deps,
        (zhat2, inv2, cot, proj, out_w, up_bias, bias, gain,),
        [
            row_spec(block, width),
            row_spec(block, 1),
            row_spec(block, width),
            ANY,
            ANY,
            whole_spec(1, hidden),
            whole_spec(8, width),
            whole_spec(3, width),
        ],
        grid=(rows // block,),
        out_specs=[
            row_spec(block, width),
            row_spec(block, width),
            row_spec(block, hidden),
            row_spec(block, width),
            row_spec(block, hidden),
            row_spec(block, width),
            whole_spec(8, width),
            whole_spec(1, hidden),
        ],
        out_shape=[
            shape((rows, width), F32),
            shape((rows, width), BF),
            shape((rows, hidden), BF),
            shape((rows, width), BF),
            shape((rows, hidden), BF),
            shape((rows, width), F32),
            shape((8, width), F32),
            shape((1, hidden), F32),
        ],
        scratch_shapes=[
            pltpu.VMEM((width, hidden), BF),
            pltpu.VMEM((hidden, width), BF),
            pltpu.VMEM((block, hidden), F32),
            pltpu.SemaphoreType.DMA((2,)),
        ],
        cost_estimate=cost(rows * width * hidden * 6.5e-9, 40),
    )


def attn_backward_kernel(
    is_text,
    len_ref,
    second_grad_ref,
    triple_ref,
    zhat1_ref,
    inv1_ref,
    proj_ref,
    out_w_ref,
    gain_ref,
    second_low_ref,
    triple_low_ref,
    first_grad_ref,
    first_low_ref,
    context_low_ref,
    sums_ref,
    wco,
    wqkv,
    wo,
    upstream,
    sems,
):
    step = pl.program_id(0)
    rows, width = second_grad_ref.shape
    arrived = fetch(
        step,
        [
            pltpu.make_async_copy(out_w_ref.at[pl.ds(0, CO_W)], wco, sems.at[0]),
            pltpu.make_async_copy(proj_ref.at[:, pl.ds(0, 3 * width)], wqkv, sems.at[1]),
            pltpu.make_async_copy(out_w_ref.at[pl.ds(CO_W, width)], wo, sems.at[2]),
        ],
    )

    @pl.when(step == 0)
    def _():
        sums_ref[...] = jnp.zeros_like(sums_ref)

    second_low = second_grad_ref[...].astype(BF)
    second_low_ref[...] = second_low
    arrived(2)
    upstream[...] = dot_nt(second_low, wo[...]).astype(BF)

    def lanes(part, lane):
        return slice(part * width + lane, part * width + lane + 128)

    if is_text:
        places = list(text_units(len_ref, step, rows // CAP))
        factor = (width // HEADS_T) ** -0.5
    else:
        places = image_units(rows)
        factor = (width // HEADS_I) ** -0.5
    units, ups = [], []
    for where, lane, mask in places:
        q, k, v = [triple_ref[where, lanes(part, lane)] for part in range(3)]
        up = upstream[where, lane : lane + 128]
        units.append((halves(q) if is_text else q, k, v, mask))
        ups.append(halves(up) if is_text else up)
    for (where, lane, _), grads in zip(places, attend_back_all(units, ups, factor)):
        dq, dk, dv = grads
        for part, grad in enumerate((unhalve(dq) if is_text else dq, dk, dv)):
            triple_low_ref[where, lanes(part, lane)] = grad.astype(BF)
    arrived(1)
    back = second_grad_ref[...]
    for part in range(3):
        at = slice(part * width, part * width + width)
        piece = triple_low_ref[:, at]
        back = back + dot_nt(piece, wqkv[:, at])
        if part != 1:
            row = 3 + part // 2
            sums_ref[row : row + 1] += col_sum(piece.astype(F32))
    zhat1 = zhat1_ref[...]
    first_grad = norm_back_rows(back, gain_ref[0:1], zhat1, inv1_ref[...])
    first_grad_ref[...] = first_grad
    sums_ref[0:1] += col_sum(back * zhat1)
    sums_ref[1:2] += col_sum(back)
    sums_ref[2:3] += col_sum(first_grad)
    first_low = first_grad.astype(BF)
    first_low_ref[...] = first_low
    arrived(0)
    context_low_ref[...] = dot_nt(first_low, wco[...]).astype(BF)


def attn_backward(is_text, block, lengths, second_grad, triple, zhat1, inv1, proj, out_w, gain, deps):
    rows, width = zhat1.shape
    shape = jax.ShapeDtypeStruct
    return call(
        functools.partial(attn_backward_kernel, is_text),
        deps,
        (lengths, second_grad, triple, zhat1, inv1, proj, out_w, gain,),
        [
            SMEM,
            row_spec(block, width),
            row_spec(block, 3 * width),
            row_spec(block, width),
            row_spec(block, 1),
            ANY,
            ANY,
            whole_spec(3, width),
        ],
        grid=(rows // block,),
        out_specs=[
            row_spec(block, width),
            row_spec(block, 3 * width),
            row_spec(block, width),
            row_spec(block, width),
            row_spec(block, CO_W),
            whole_spec(8, width),
        ],
        out_shape=[
            shape((rows, width), BF),
            shape((rows, 3 * width), BF),
            shape((rows, width), F32),
            shape((rows, width), BF),
            shape((rows, CO_W), BF),
            shape((8, width), F32),
        ],
        scratch_shapes=[
            pltpu.VMEM((CO_W, width), BF),
            pltpu.VMEM((width, 3 * width), BF),
            pltpu.VMEM((width, width), BF),
            pltpu.VMEM((block, width), BF),
            pltpu.SemaphoreType.DMA((3,)),
        ],
        cost_estimate=cost(rows * width * width * 1.6e-8, 40),
    )


def co_project(inputs, weight, wide):
    bias = jnp.concatenate([wide[:CO_W], jnp.zeros((CO_W,), F32), wide[CO_W : 2 * CO_W]])
    return (dot_nn(inputs, weight[:, : 3 * CO_W]) + bias).astype(BF)


def pad_pairs(block):
    wide = block.reshape(-1, REGIONS, block.shape[1])
    return jnp.pad(wide, ((0, 0), (0, SLOTS - REGIONS), (0, 0))).reshape(-1, block.shape[1])


def unpad_pairs(block):
    return block.reshape(-1, SLOTS, block.shape[1])[:, :REGIONS].reshape(-1, block.shape[1])


def shards(
    text_in,
    image_in,
    lengths,
    t_proj,
    t_out,
    t_bias_wide,
    t_bias,
    t_gain,
    i_proj,
    i_out,
    i_bias_wide,
    i_bias,
    i_gain,
    text_cot,
    image_cot,
):
    small = (t_bias_wide, t_bias, t_gain, i_bias_wide, i_bias, i_gain)
    flat = jnp.concatenate([piece.reshape(-1) for piece in small])
    t_rows = t_proj.shape[0]
    extra = -(-flat.shape[0] // (t_rows * 128)) * 128
    riders = jnp.pad(flat, (0, extra * t_rows - flat.shape[0])).reshape(t_rows, extra)
    near_image = over_x(image_in)
    near_cot = over_x(image_cot)

    def padded(own, rows, cols):
        return jnp.pad(own, ((0, rows - own.shape[0]), (0, cols - own.shape[1])))

    def z_gather(own):
        rows, cols = own.shape
        short = (1 << 20) - 2 * rows * cols * dp_parts()[0]
        if short > 0:
            line = 2 * dp_parts()[0]
            more_rows = -(-short // (line * cols * 8)) * 8
            more_cols = -(-short // (line * rows * 128)) * 128
            if more_rows * cols < more_cols * rows:
                own = padded(own, rows + more_rows, cols)
            else:
                own = padded(own, rows, cols + more_cols)
        return column_by_gather(own, rows, cols)

    t_co_own = jnp.concatenate([t_proj[:, : 3 * CO_W], riders], 1)
    t_co_column = column_by_permutes(t_co_own)
    i_co_column = after(column_by_permutes(i_proj[:, : 3 * CO_W]), near_image, near_cot)
    i_out_column, i_rest_column = z_gather(i_out), z_gather(i_proj[:, 3 * CO_W :])
    t_out_column, t_rest_column = z_gather(t_out), z_gather(t_proj[:, 3 * CO_W :])
    first = [Gather(t_co_column, True), Gather(i_co_column, False)]
    for part in first:
        part.second()
    fars = [part.far for part in first]
    second = [
        Gather(after(i_out_column, *fars), True),
        Gather(after(i_rest_column, *fars), False),
    ]
    for part in first:
        part.core()
    overs = [part.over for part in second]
    t_co, i_co = [part.full(overs) for part in first]
    for part in second:
        part.second()

    shard_count = t_co.shape[0] // t_rows
    table = t_co[:, 3 * CO_W :].reshape(shard_count, -1)[:, : flat.shape[0]].astype(F32)
    taken = []
    offset = 0
    for piece in small:
        block = table[:, offset : offset + piece.size].reshape((shard_count,) + piece.shape)
        offset += piece.size
        if piece.ndim == 1:
            taken.append(block.reshape(1, -1))
        else:
            taken.append(block.transpose(1, 0, 2).reshape(piece.shape[0], -1))
    t_wide, t_rows8, t_gains, i_wide, i_rows8, i_gains = taken

    image_rows = pad_pairs(near_image)
    image_up = pad_pairs(near_cot)
    text_co = co_project(text_in, t_co, t_wide[0])
    image_co = co_project(image_rows, i_co, i_wide[0])
    text_context, image_context = co_forward(
        lengths, text_co, image_co, ()
    )
    fars = [part.far for part in second] + [image_context]
    third = [
        Gather(after(t_out_column, *fars), True),
        Gather(after(t_rest_column, *fars), False),
    ]
    for part in second:
        part.core()
    overs = [part.over for part in third]
    i_outw, i_rest = [part.full(overs) for part in second]
    for part in third:
        part.second()

    image_block = image_rows.shape[0]
    image_hidden = i_wide.shape[1] - 2 * CO_W
    zhat1, inv1, low1, triple, attended, zhat2, inv2 = attn_forward(
        False,
        image_block,
        lengths,
        image_context,
        image_rows,
        i_rest,
        i_outw,
        i_rows8,
        i_gains,
        (),
    )
    i_final, low2, active, third_low, hidden_low, second_grad, i_sums2, i_upsum = ffn(
        image_block,
        512,
        image_hidden,
        zhat2,
        inv2,
        image_up,
        i_rest,
        i_outw,
        i_wide[:, 2 * CO_W :],
        i_rows8,
        i_gains,
        (),
    )
    image_final = over_x(unpad_pairs(i_final).astype(BF))
    second_low, triple_low, i_first, first_low, i_ctx, i_sums1 = attn_backward(
        False, image_block, lengths, second_grad, triple, zhat1, inv1, i_rest, i_outw, i_gains, ()
    )
    i_rest_sum = Scatter(
        cols_grad(shard_count, True, [(low1, triple_low), (low2, hidden_low)], 512), True
    )
    i_out_sum = Scatter(
        rows_grad(
            shard_count, False,
            [(image_context, first_low), (attended, second_low), (active, third_low)],
            256,
        ),
        False,
    )

    for part in third:
        part.core()
    t_outw, t_rest = [part.full([i_first]) for part in third]

    text_block = 256
    text_hidden = t_wide.shape[1] - 2 * CO_W
    zhat1, inv1, low1, triple, attended, zhat2, inv2 = attn_forward(
        True,
        text_block,
        lengths,
        text_context,
        text_in,
        t_rest,
        t_outw,
        t_rows8,
        t_gains,
        [i_rest_sum.keep, i_out_sum.keep, image_final],
    )
    i_rest_sum.link()
    i_out_sum.link()
    t_final, low2, active, third_low, hidden_low, second_grad, t_sums2, t_upsum = ffn(
        text_block,
        512,
        text_hidden,
        zhat2,
        inv2,
        text_cot,
        t_rest,
        t_outw,
        t_wide[:, 2 * CO_W :],
        t_rows8,
        t_gains,
        [i_rest_sum.send, i_out_sum.send],
    )
    i_rest_sum.link()
    i_out_sum.link()
    second_low, triple_low, t_first, first_low, t_ctx, t_sums1 = attn_backward(
        True,
        text_block,
        lengths,
        second_grad,
        triple,
        zhat1,
        inv1,
        t_rest,
        t_outw,
        t_gains,
        [i_rest_sum.send, i_out_sum.send],
    )
    t_rest_sum = Scatter(
        cols_grad(shard_count, False, [(low1, triple_low), (low2, hidden_low)], 768), False
    )
    t_out_sum = Scatter(
        rows_grad(
            shard_count, True,
            [(text_context, first_low), (attended, second_low), (active, third_low)],
            256,
            [t_rest_sum.keep],
        ),
        True,
    )
    i_rest_sum.column()
    i_out_sum.column()

    t_rest_sum.link()
    t_co_grad, i_co_grad, t_co_sum, i_co_sum = co_backward(
        lengths, text_co, image_co, t_ctx, i_ctx, [t_out_sum.keep, i_rest_sum.send, i_out_sum.send, t_rest_sum.send]
    )
    t_out_sum.link()

    def small_grads(sums1, sums2, up_sum, co_sum):
        wide = jnp.concatenate([co_sum[0, :CO_W], co_sum[0, 2 * CO_W :], up_sum[0]])
        rows8 = jnp.stack(
            [sums1[2], sums1[1], sums1[3], sums1[4], sums2[5], sums2[4], sums2[2], sums2[1]]
        )
        return wide, rows8, jnp.stack([sums1[0], sums2[3], sums2[0]])

    pieces = small_grads(t_sums1, t_sums2, t_upsum, t_co_sum) + small_grads(
        i_sums1, i_sums2, i_upsum, i_co_sum
    )
    packed = []
    for piece in pieces:
        if piece.ndim == 1:
            packed.append(piece.reshape(shard_count, -1))
        else:
            packed.append(
                piece.reshape(piece.shape[0], shard_count, -1)
                .transpose(1, 0, 2)
                .reshape(shard_count, -1)
            )
    packed = jnp.concatenate(packed, 1)
    count = packed.shape[1]
    packed = jnp.pad(packed, ((0, 0), (0, extra * t_rows - count))).reshape(-1, extra)

    i_co_sums = Scatter(
        cols_grad(
            shard_count, True,
            [(image_rows, i_co_grad)],
            512,
            deps=[t_rest_sum.send, t_out_sum.send],
        ),
        True,
    )
    t_co_sums = Scatter(
        cols_grad(shard_count, False, [(text_in, t_co_grad)], 768, packed, [i_co_sums.keep]), False
    )
    i_co_sums.link()
    t_co_sums.link()
    image_grad = after(i_first, i_co_sums.send) + dot_nt(i_co_grad, i_co)
    image_grad = over_x(unpad_pairs(image_grad).astype(BF)).astype(F32)
    text_grad = after(t_first, t_co_sums.send) + dot_nt(t_co_grad, t_co[:, : 3 * CO_W])
    t_rest_sum.link()
    t_out_sum.link()
    t_rest_sum.column()
    t_out_sum.column()
    i_co_sums.link()
    t_co_sums.link()
    i_co_sums.column_by_permutes()
    t_co_sums.column_by_permutes()
    image_final = image_final.astype(F32)
    t_cog = t_co_sums.total()

    mine = t_cog[:, 3 * CO_W :].reshape(-1)
    outs = []
    offset = 0
    for piece in small:
        outs.append(mine[offset : offset + piece.size].reshape(piece.shape))
        offset += piece.size
    t_wide_g, t_rows_g, t_gain_g, i_wide_g, i_rows_g, i_gain_g = outs
    return (
        t_final,
        image_final,
        text_grad,
        image_grad,
        jnp.concatenate([t_cog[:, : 3 * CO_W], t_rest_sum.total()], 1),
        t_out_sum.total(),
        t_wide_g,
        t_rows_g,
        t_gain_g,
        jnp.concatenate([i_co_sums.total(), i_rest_sum.total()], 1),
        i_out_sum.total(),
        i_wide_g,
        i_rows_g,
        i_gain_g,
    )


def solution(mesh):
    both = ("stream", "dp")
    rows, cols, flat = P(both, None), P(None, both), P(both)
    weights = (rows, rows, flat, cols, cols)
    return jax.shard_map(
        shards,
        mesh=mesh,
        in_specs=(rows, rows, flat) + weights + weights + (rows, rows),
        out_specs=(rows, rows, rows, rows) + weights + weights,
        check_vma=False,
    )
```

```python
import functools

import jax
import jax.numpy as jnp
from jax import lax
from jax.experimental import pallas as pl
from jax.experimental.pallas import tpu as pltpu
from jax.sharding import PartitionSpec as P

CO_W = 1024
HEADS_T = 12
HEADS_I = 8
CO_HEADS = 8
CAP = 128
REGIONS = 36
SLOTS = 48

epsilon = 1e-05
negative = -1e30
BF = jnp.bfloat16
F32 = jnp.float32
VMEM_LIMIT = 60 * 1024 * 1024
HALF_ROOT = 0.7071067811865476
INV_ROOT = 0.3989422804014327
ANY = pl.BlockSpec(memory_space=pl.ANY)
SMEM = pl.BlockSpec(memory_space=pltpu.SMEM)


def dot_nn(a, b):
    return lax.dot_general(a, b, (((1,), (0,)), ((), ())), preferred_element_type=F32)


def dot_nt(a, b):
    return lax.dot_general(a, b, (((1,), (1,)), ((), ())), preferred_element_type=F32)


def dot_tn(a, b):
    return lax.dot_general(a, b, (((0,), (0,)), ((), ())), preferred_element_type=F32)


def params():
    return pltpu.CompilerParams(vmem_limit_bytes=VMEM_LIMIT)


def call(kernel, deps, operands, in_specs, **kwargs):
    count = len(operands)

    def body(*refs):
        kernel(*refs[:count], *refs[count + len(deps) :])

    return pl.pallas_call(
        body,
        in_specs=in_specs + [ANY] * len(deps),
        compiler_params=params(),
        **kwargs,
    )(*operands, *deps)


def cost(gmacs, mbytes):
    return pl.CostEstimate(
        flops=int(2e9 * gmacs), bytes_accessed=int(1e6 * mbytes), transcendentals=0
    )


def dp_parts():
    total = lax.axis_size("dp")
    index = lax.axis_index("dp")
    return total // 4, index // 4, (index // 2) % 2, index % 2


def over_core(block):
    total = lax.axis_size("dp")
    return lax.ppermute(block, "dp", [(d, d ^ 1) for d in range(total)])


def over_y(block):
    total = lax.axis_size("dp")
    return lax.ppermute(block, "dp", [(d, d ^ 2) for d in range(total)])


def over_x(block):
    total = lax.axis_size("stream")
    return lax.ppermute(block, "stream", [(d, d ^ 1) for d in range(total)])


def over_z(block, shift):
    total = lax.axis_size("dp")
    return lax.ppermute(block, "dp", [(d, (d + 4 * shift) % total) for d in range(total)])


def pick(buffer, position, axis):
    return lax.dynamic_index_in_dim(buffer, position, axis, keepdims=False)


def place_kernel(blocks, table_ref, *refs):
    count = (len(refs) - 3) // 2
    pieces, out_ref = refs[:count], refs[count]
    held, in_sems, out_sems = refs[count + 1 : 2 * count + 1], refs[2 * count + 1], refs[2 * count + 2]
    loads, stores = [], []
    for number in range(count * blocks):
        piece, block = number // blocks, number % blocks
        x, y, c = [table_ref[3 * number + i] for i in range(3)]
        loads.append(
            pltpu.make_async_copy(pieces[piece].at[block], held[piece].at[block], in_sems.at[number])
        )
        stores.append(
            pltpu.make_async_copy(
                held[piece].at[block], out_ref.at[x, :, y, c], out_sems.at[number]
            )
        )
    for load in loads:
        load.start()
    for load, store in zip(loads, stores):
        load.wait()
        store.start()
    for store in stores:
        store.wait()


def place(pieces, table, deps):
    blocks, nz, rows, cols = pieces[0].shape
    size = 4 * len(pieces) * pieces[0].size
    return call(
        functools.partial(place_kernel, blocks),
        deps,
        (table, *pieces),
        [SMEM] + [ANY] * len(pieces),
        out_specs=ANY,
        out_shape=jax.ShapeDtypeStruct((2, nz, 2, 2, rows, cols), pieces[0].dtype),
        scratch_shapes=[pltpu.VMEM(piece.shape, piece.dtype) for piece in pieces]
        + [pltpu.SemaphoreType.DMA((len(pieces) * blocks,))] * 2,
        cost_estimate=pl.CostEstimate(flops=0, bytes_accessed=size, transcendentals=0),
    )


def table_of(rows):
    return jnp.stack([jnp.asarray(v, jnp.int32) for row in rows for v in row])


def z_groups():
    total = lax.axis_size("dp")
    return [[first + 4 * k for k in range(total // 4)] for first in range(4)]


def after_kernel(*refs):
    pass


def after(block, *earlier):
    return pl.pallas_call(
        after_kernel,
        in_specs=[ANY] * (1 + len(earlier)),
        out_specs=ANY,
        out_shape=jax.ShapeDtypeStruct(block.shape, block.dtype),
        input_output_aliases={0: 0},
        compiler_params=params(),
        cost_estimate=pl.CostEstimate(flops=0, bytes_accessed=0, transcendentals=0),
    )(block, *earlier)


def column_by_permutes(own):
    nz, z, _, _ = dp_parts()
    came = jnp.stack([own] + [over_z(own, shift) for shift in range(1, nz)])
    turned = jnp.concatenate([came[::-1]] * 2)
    return lax.dynamic_slice_in_dim(turned, nz - 1 - z, nz, 0)


def column_by_gather(own, rows, cols):
    full = lax.all_gather(own, "dp", axis_index_groups=z_groups(), axis=0)
    return full[:, :rows, :cols]


class Gather:
    def __init__(self, column, y_first):
        self.column = column
        self.links = (over_y, over_x) if y_first else (over_x, over_y)
        self.y_first = y_first
        self.over = self.links[0](column)

    def second(self):
        self.pair = jnp.stack([self.column, self.over])
        self.far = self.links[1](self.pair)

    def core(self):
        self.others = [over_core(self.pair), over_core(self.far)]

    def full(self, deps):
        _, _, y, c = dp_parts()
        x = lax.axis_index("stream")
        table = []
        for core in (0, 1):
            for outer in (0, 1):
                for inner in (0, 1):
                    dx, dy = (outer, inner) if self.y_first else (inner, outer)
                    table.append((x ^ dx, y ^ dy, c ^ core))
        whole = place([self.pair, self.far] + self.others, table_of(table), deps)
        return whole.reshape(-1, whole.shape[-1])


def add_low(kept, came):
    return (kept.astype(F32) + came.astype(F32)).astype(BF)


class Scatter:
    def __init__(self, halves, y_first):
        self.send, self.keep = halves
        self.came = over_core(self.send)
        self.axes = ("y", "x") if y_first else ("x", "y")

    def link(self):
        axis, self.axes = self.axes[0], self.axes[1:]
        at = dp_parts()[2] if axis == "y" else lax.axis_index("stream")
        self.send = add_low(pick(self.keep, 1 - at, 0), pick(self.came, 1 - at, 0))
        self.keep = add_low(pick(self.keep, at, 0), pick(self.came, at, 0))
        self.came = over_y(self.send) if axis == "y" else over_x(self.send)

    def column_by_permutes(self):
        nz, z, _, _ = dp_parts()
        self.send = add_low(self.keep, self.came)
        self.sum = pick(self.send, z, 0).astype(F32)
        for shift in range(1, nz):
            came = over_z(pick(self.send, (z + shift) % nz, 0), shift)
            self.sum = self.sum + came.astype(F32)

    def column(self):
        self.send = add_low(self.keep, self.came)
        self.sum = lax.psum_scatter(
            self.send.reshape(-1, self.send.shape[-1]),
            "dp",
            axis_index_groups=z_groups(),
            scatter_dimension=0,
            tiled=True,
        )

    def total(self):
        return self.sum.astype(F32)


def store_halves(y_first, core_ref, send_ref, keep_ref, block, at):
    columns, rows = send_ref.shape[:2]
    nz = columns // 4

    def store(even_ref, odd_ref):
        for number in range(columns):
            x, z, y = number // (2 * nz), number // 2 % nz, number % 2
            spot = (y * 2 + x if y_first else x * 2 + y) * nz + z
            start = 2 * number * rows
            even_ref[spot, :, at] = block[start : start + rows].astype(BF)
            odd_ref[spot, :, at] = block[start + rows : start + 2 * rows].astype(BF)

    @pl.when(core_ref[0] == 0)
    def _():
        store(keep_ref, send_ref)

    @pl.when(core_ref[0] == 1)
    def _():
        store(send_ref, keep_ref)


def cols_grad_kernel(y_first, counts, tile, has_riders, core_ref, *refs):
    segments = len(counts)
    lhs, ups = refs[:segments], refs[segments : 2 * segments]
    riders = refs[2 * segments] if has_riders else None
    send_ref, keep_ref = refs[2 * segments + has_riders : 2 * segments + has_riders + 2]
    turned = refs[2 * segments + has_riders + 2 :]
    step = pl.program_id(0)

    @pl.when(step == 0)
    def _():
        for flat, kept in zip(lhs, turned):
            kept[...] = flat[...].T

    first = 0
    for count, kept, up in zip(counts, turned, ups):

        @pl.when((step >= first) & (step < first + count))
        def _(kept=kept, up=up):
            at = pl.ds(pl.multiple_of(step * tile, 128), tile) if has_riders else slice(None)
            store_halves(y_first, core_ref, send_ref, keep_ref, dot_nn(kept[...], up[...]), at)

        first += count
    if has_riders:

        @pl.when(step == 0)
        def _():
            width = riders.shape[1]
            start = sum(counts) * tile
            store_halves(y_first, core_ref, send_ref, keep_ref, riders[...], slice(start, start + width))


def half_shapes(shards, rows, cols):
    return [jax.ShapeDtypeStruct((shards // 2, rows, cols), BF)] * 2


def cols_grad(shards, y_first, segments, tile, riders=None, deps=()):
    counts = [up.shape[1] // tile for _, up in segments]
    width = segments[0][0].shape[1]
    length = segments[0][0].shape[0]
    rows = width // shards
    total = sum(counts) * tile + (0 if riders is None else riders.shape[1])
    starts = [sum(counts[:i]) for i in range(len(counts))]

    def up_spec(start, count):
        return pl.BlockSpec((length, tile), lambda j: (0, jnp.clip(j - start, 0, count - 1)))

    whole = [pl.BlockSpec(lhs.shape, lambda j: (0, 0)) for lhs, _ in segments]
    tiles = [up_spec(start, count) for start, count in zip(starts, counts)]
    extra = [] if riders is None else [riders]
    core = jnp.reshape(dp_parts()[3], (1,)).astype(jnp.int32)
    if riders is None:
        out = pl.BlockSpec((shards // 2, rows, tile), lambda j: (0, 0, j))
    else:
        out = pl.BlockSpec((shards // 2, rows, total), lambda j: (0, 0, 0))
    halves = call(
        functools.partial(cols_grad_kernel, y_first, counts, tile, len(extra)),
        deps,
        (core,) + tuple(lhs for lhs, _ in segments) + tuple(up for _, up in segments) + tuple(extra),
        [SMEM] + whole + tiles + [pl.BlockSpec(block.shape, lambda j: (0, 0)) for block in extra],
        grid=(sum(counts),),
        out_specs=[out, out],
        out_shape=half_shapes(shards, rows, total),
        scratch_shapes=[pltpu.VMEM((width, length), BF) for _ in segments],
        cost_estimate=cost(1.3e-9 * length * width * total, 20),
    )
    return [half.reshape(2, 2, -1, rows, total) for half in halves]


def rows_grad_kernel(y_first, segments, tile, core_ref, *refs):
    lhs, ups = refs[:segments], refs[segments : 2 * segments]
    send_ref, keep_ref, total = refs[2 * segments : 2 * segments + 3]
    turned = refs[2 * segments + 3 :]

    @pl.when(pl.program_id(0) == 0)
    def _():
        for flat, kept in zip(lhs, turned):
            kept[...] = flat[...].T

    start = 0
    for kept, up in zip(turned, ups):
        for row in range(0, kept.shape[0], 256):
            total[start + row : start + row + 256] = dot_nn(kept[row : row + 256], up[...])
        start += kept.shape[0]
    store_halves(y_first, core_ref, send_ref, keep_ref, total, slice(None))


def rows_grad(shards, y_first, segments, tile, deps=()):
    length = segments[0][0].shape[0]
    height = sum(lhs.shape[1] for lhs, _ in segments)
    width = segments[0][1].shape[1]
    rows = height // shards
    core = jnp.reshape(dp_parts()[3], (1,)).astype(jnp.int32)
    out = pl.BlockSpec((shards // 2, rows, tile), lambda j: (0, 0, j))
    halves = call(
        functools.partial(rows_grad_kernel, y_first, len(segments), tile),
        deps,
        (core,) + tuple(lhs for lhs, _ in segments) + tuple(up for _, up in segments),
        [SMEM]
        + [
            pl.BlockSpec(lhs.shape, lambda j: (0, 0), pipeline_mode=pl.Buffered(1))
            for lhs, _ in segments
        ]
        + [pl.BlockSpec((length, tile), lambda j: (0, j)) for _ in segments],
        grid=(width // tile,),
        out_specs=[out, out],
        out_shape=half_shapes(shards, rows, width),
        scratch_shapes=[pltpu.VMEM((height, tile), F32)]
        + [pltpu.VMEM((lhs.shape[1], length), BF) for lhs, _ in segments],
        cost_estimate=cost(1.3e-9 * length * height * width, 20),
    )
    return [half.reshape(2, 2, -1, rows, width) for half in halves]


def softmax_rows(scores):
    high = jnp.max(scores, -1, keepdims=True)
    exponent = jnp.exp(scores - high)
    return exponent * (1.0 / jnp.sum(exponent, -1, keepdims=True))


def norm_rows(pre_norm):
    centered = pre_norm - jnp.mean(pre_norm, -1, keepdims=True)
    inverse = lax.rsqrt(jnp.mean(centered * centered, -1, keepdims=True) + epsilon)
    return centered * inverse, inverse


def norm_back_rows(upstream, gain, normed, inverse):
    scaled = upstream * gain
    return inverse * (
        scaled
        - jnp.mean(scaled, -1, keepdims=True)
        - normed * jnp.mean(scaled * normed, -1, keepdims=True)
    )


def col_sum(block):
    return jnp.sum(block, 0, keepdims=True)


def key_mask(shape, count):
    return jnp.where(lax.broadcasted_iota(jnp.int32, shape, 1) < count, 0.0, negative)


def attend_all(units, factor):
    scores = [dot_nt(q, k) * factor + mask for q, k, _, mask in units]
    probs = [softmax_rows(score).astype(BF) for score in scores]
    return [dot_nn(prob, unit[2]) for prob, unit in zip(probs, units)]


def attend_back_all(units, upstreams, factor):
    scores = [dot_nt(q, k) * factor + mask for q, k, _, mask in units]
    raised = [dot_nt(up, unit[2]) for up, unit in zip(upstreams, units)]
    probs = [softmax_rows(score) for score in scores]
    values_grad = [dot_tn(prob.astype(BF), up) for prob, up in zip(probs, upstreams)]
    rounded = [
        (prob * (grad - jnp.sum(prob * grad, -1, keepdims=True)) * factor).astype(BF)
        for prob, grad in zip(probs, raised)
    ]
    queries_grad = [dot_nn(low, unit[1]) for low, unit in zip(rounded, units)]
    keys_grad = [dot_tn(low, unit[0]) for low, unit in zip(rounded, units)]
    return list(zip(queries_grad, keys_grad, values_grad))


def co_forward_kernel(len_ref, text_ref, image_ref, text_out, image_out):
    step = pl.program_id(0)
    factor = (CO_W // CO_HEADS) ** -0.5
    region_mask = key_mask((1, SLOTS), REGIONS)
    text_mask = key_mask((1, CAP), len_ref[step])
    units, places = [], []
    for head in range(CO_HEADS):
        at = [slice(part * CO_W + head * 128, part * CO_W + head * 128 + 128) for part in range(3)]
        tq, tk, tv = [text_ref[:, where] for where in at]
        iq, ik, iv = [image_ref[:, where] for where in at]
        units += [(tq, ik, iv, region_mask), (iq, tk, tv, text_mask)]
        places += [(text_out, at[0]), (image_out, at[0])]
    for (out_ref, where), context in zip(places, attend_all(units, factor)):
        out_ref[:, where] = context.astype(BF)


def co_forward(lengths, text_co, image_co, deps):
    pairs = lengths.shape[0]
    return call(
        co_forward_kernel,
        deps,
        (lengths, text_co, image_co,),
        [
            SMEM,
            pl.BlockSpec((CAP, 3 * CO_W), lambda i: (i, 0)),
            pl.BlockSpec((SLOTS, 3 * CO_W), lambda i: (i, 0)),
        ],
        grid=(pairs,),
        out_specs=[
            pl.BlockSpec((CAP, CO_W), lambda i: (i, 0)),
            pl.BlockSpec((SLOTS, CO_W), lambda i: (i, 0)),
        ],
        out_shape=[
            jax.ShapeDtypeStruct((pairs * CAP, CO_W), BF),
            jax.ShapeDtypeStruct((pairs * SLOTS, CO_W), BF),
        ],
        cost_estimate=cost(2 * lengths.shape[0] * 0.4, 8),
    )


def co_backward_kernel(
    len_ref, text_ref, image_ref, text_up, image_up, text_out, image_out, text_sum, image_sum
):
    step = pl.program_id(0)
    factor = (CO_W // CO_HEADS) ** -0.5
    region_mask = key_mask((1, SLOTS), REGIONS)
    text_mask = key_mask((1, CAP), len_ref[step])

    @pl.when(step == 0)
    def _():
        text_sum[...] = jnp.zeros_like(text_sum)
        image_sum[...] = jnp.zeros_like(image_sum)

    def store(out_ref, sum_ref, where, grad):
        low = grad.astype(BF)
        out_ref[:, where] = low
        sum_ref[:, where] += col_sum(low.astype(F32))

    units, ups, places = [], [], []
    for head in range(CO_HEADS):
        at = [slice(part * CO_W + head * 128, part * CO_W + head * 128 + 128) for part in range(3)]
        tq, tk, tv = [text_ref[:, where] for where in at]
        iq, ik, iv = [image_ref[:, where] for where in at]
        units += [(tq, ik, iv, region_mask), (iq, tk, tv, text_mask)]
        ups += [text_up[:, at[0]], image_up[:, at[0]]]
        places.append(at)
    grads = attend_back_all(units, ups, factor)
    for head, at in enumerate(places):
        dtq, dik, div = grads[2 * head]
        diq, dtk, dtv = grads[2 * head + 1]
        for where, grad in zip(at, (dtq, dtk, dtv)):
            store(text_out, text_sum, where, grad)
        for where, grad in zip(at, (diq, dik, div)):
            store(image_out, image_sum, where, grad)


def co_backward(lengths, text_co, image_co, text_up, image_up, deps):
    pairs = lengths.shape[0]
    wide = 3 * CO_W
    return call(
        co_backward_kernel,
        deps,
        (lengths, text_co, image_co, text_up, image_up,),
        [
            SMEM,
            pl.BlockSpec((CAP, wide), lambda i: (i, 0)),
            pl.BlockSpec((SLOTS, wide), lambda i: (i, 0)),
            pl.BlockSpec((CAP, CO_W), lambda i: (i, 0)),
            pl.BlockSpec((SLOTS, CO_W), lambda i: (i, 0)),
        ],
        grid=(pairs,),
        out_specs=[
            pl.BlockSpec((CAP, wide), lambda i: (i, 0)),
            pl.BlockSpec((SLOTS, wide), lambda i: (i, 0)),
            pl.BlockSpec((1, wide), lambda i: (0, 0)),
            pl.BlockSpec((1, wide), lambda i: (0, 0)),
        ],
        out_shape=[
            jax.ShapeDtypeStruct((pairs * CAP, wide), BF),
            jax.ShapeDtypeStruct((pairs * SLOTS, wide), BF),
            jax.ShapeDtypeStruct((1, wide), F32),
            jax.ShapeDtypeStruct((1, wide), F32),
        ],
        cost_estimate=cost(2 * lengths.shape[0] * 0.5, 20),
    )


def fetch(step, copies):
    @pl.when(step == 0)
    def _():
        for copy in copies:
            copy.start()

    def arrived(number):
        @pl.when(step == 0)
        def _():
            copies[number].wait()

    return arrived


def text_units(len_ref, step, pair_count):
    for pair in range(pair_count):
        mask = key_mask((1, CAP), len_ref[step * pair_count + pair])
        for block in range(HEADS_T // 2):
            yield slice(pair * CAP, pair * CAP + CAP), block * 128, mask


def image_mask():
    shape = (2 * SLOTS, 2 * SLOTS)
    row = lax.broadcasted_iota(jnp.int32, shape, 0)
    col = lax.broadcasted_iota(jnp.int32, shape, 1)
    same = (row >= SLOTS) == (col >= SLOTS)
    local = jnp.where(col >= SLOTS, col - SLOTS, col)
    return jnp.where(same & (local < REGIONS), 0.0, negative)


def image_units(rows):
    mask = image_mask()
    return [
        (slice(start, start + 2 * SLOTS), head * 128, mask)
        for start in range(0, rows, 2 * SLOTS)
        for head in range(HEADS_I)
    ]


def halves(block):
    low = lax.broadcasted_iota(jnp.int32, block.shape, 1) < 64
    zero = jnp.zeros_like(block)
    return jnp.concatenate([jnp.where(low, block, zero), jnp.where(low, zero, block)], 0)


def unhalve(stacked):
    rows = stacked.shape[0] // 2
    low = lax.broadcasted_iota(jnp.int32, (rows, stacked.shape[1]), 1) < 64
    return jnp.where(low, stacked[:rows], stacked[rows:])


def attn_forward_kernel(
    is_text,
    down_at,
    len_ref,
    context_ref,
    input_ref,
    proj_ref,
    out_w_ref,
    bias_ref,
    gain_ref,
    zhat1_ref,
    inv1_ref,
    low1_ref,
    triple_ref,
    attended_ref,
    zhat2_ref,
    inv2_ref,
    wco,
    wqkv,
    wo,
    sems,
):
    step = pl.program_id(0)
    width = input_ref.shape[1]
    rows = input_ref.shape[0]
    arrived = fetch(
        step,
        [
            pltpu.make_async_copy(out_w_ref.at[pl.ds(0, CO_W)], wco, sems.at[0]),
            pltpu.make_async_copy(proj_ref.at[:, pl.ds(0, 3 * width)], wqkv, sems.at[1]),
            pltpu.make_async_copy(out_w_ref.at[pl.ds(CO_W, width)], wo, sems.at[2]),
        ],
    )
    arrived(0)
    normed, inverse = norm_rows(
        input_ref[...].astype(F32) + dot_nn(context_ref[...], wco[...]) + bias_ref[0:1]
    )
    zhat1_ref[...] = normed
    inv1_ref[...] = inverse
    first = normed * gain_ref[0:1] + bias_ref[1:2]
    first_low = first.astype(BF)
    low1_ref[...] = first_low
    arrived(1)
    for part in range(3):
        at = slice(part * width, part * width + width)
        piece = dot_nn(first_low, wqkv[:, at])
        if part == 0:
            piece = piece + bias_ref[2:3]
        if part == 2:
            piece = piece + bias_ref[3:4]
        triple_ref[:, at] = piece.astype(BF)

    def lanes(part, lane):
        return slice(part * width + lane, part * width + lane + 128)

    if is_text:
        places = list(text_units(len_ref, step, rows // CAP))
        factor = (width // HEADS_T) ** -0.5
    else:
        places = image_units(rows)
        factor = (width // HEADS_I) ** -0.5
    units = []
    for where, lane, mask in places:
        q, k, v = [triple_ref[where, lanes(part, lane)] for part in range(3)]
        units.append((halves(q) if is_text else q, k, v, mask))
    for (where, lane, _), context in zip(places, attend_all(units, factor)):
        context = unhalve(context) if is_text else context
        attended_ref[where, lane : lane + 128] = context.astype(BF)
    arrived(2)
    normed, inverse = norm_rows(first + dot_nn(attended_ref[...], wo[...]) + bias_ref[4:5])
    zhat2_ref[...] = normed
    inv2_ref[...] = inverse


def row_spec(rows, cols):
    return pl.BlockSpec((rows, cols), lambda i: (i, 0))


def whole_spec(rows, cols):
    return pl.BlockSpec((rows, cols), lambda i: (0, 0))


def attn_forward(is_text, block, lengths, context, inputs, proj, out_w, bias, gain, deps):
    rows, width = inputs.shape
    shape = jax.ShapeDtypeStruct
    return call(
        functools.partial(attn_forward_kernel, is_text, CO_W + width),
        deps,
        (lengths, context, inputs, proj, out_w, bias, gain,),
        [
            SMEM,
            row_spec(block, CO_W),
            row_spec(block, width),
            ANY,
            ANY,
            whole_spec(8, width),
            whole_spec(3, width),
        ],
        grid=(rows // block,),
        out_specs=[
            row_spec(block, width),
            row_spec(block, 1),
            row_spec(block, width),
            row_spec(block, 3 * width),
            row_spec(block, width),
            row_spec(block, width),
            row_spec(block, 1),
        ],
        out_shape=[
            shape((rows, width), F32),
            shape((rows, 1), F32),
            shape((rows, width), BF),
            shape((rows, 3 * width), BF),
            shape((rows, width), BF),
            shape((rows, width), F32),
            shape((rows, 1), F32),
        ],
        scratch_shapes=[
            pltpu.VMEM((CO_W, width), BF),
            pltpu.VMEM((width, 3 * width), BF),
            pltpu.VMEM((width, width), BF),
            pltpu.SemaphoreType.DMA((3,)),
        ],
        cost_estimate=cost(rows * width * width * 1.6e-8, 40),
    )


def ffn_kernel(
    chunk,
    zhat2_ref,
    inv2_ref,
    cot_ref,
    proj_ref,
    out_w_ref,
    up_bias_ref,
    bias_ref,
    gain_ref,
    final_ref,
    low2_ref,
    active_ref,
    third_low_ref,
    hidden_low_ref,
    second_grad_ref,
    sums_ref,
    up_sum_ref,
    wup,
    wdown,
    slope,
    sems,
):
    step = pl.program_id(0)
    width = zhat2_ref.shape[1]
    hidden = wup.shape[1]
    arrived = fetch(
        step,
        [
            pltpu.make_async_copy(proj_ref.at[:, pl.ds(3 * width, hidden)], wup, sems.at[0]),
            pltpu.make_async_copy(out_w_ref.at[pl.ds(CO_W + width, hidden)], wdown, sems.at[1]),
        ],
    )

    @pl.when(step == 0)
    def _():
        sums_ref[...] = jnp.zeros_like(sums_ref)
        up_sum_ref[...] = jnp.zeros_like(up_sum_ref)

    arrived(0)
    arrived(1)
    second = zhat2_ref[...] * gain_ref[1:2] + bias_ref[5:6]
    second_low = second.astype(BF)
    low2_ref[...] = second_low
    total = second + bias_ref[6:7]
    for start in range(0, hidden, chunk):
        at = slice(start, start + chunk)
        u = dot_nn(second_low, wup[:, at]) + up_bias_ref[:, at]
        phi = 0.5 + 0.5 * lax.erf(u * HALF_ROOT)
        active = (u * phi).astype(BF)
        active_ref[:, at] = active
        slope[:, at] = phi + (u * INV_ROOT) * jnp.exp(-0.5 * u * u)
        total = total + dot_nn(active, wdown[at])
    normed, inverse = norm_rows(total)
    final_ref[...] = normed * gain_ref[2:3] + bias_ref[7:8]
    upstream = cot_ref[...].astype(F32)
    third = norm_back_rows(upstream, gain_ref[2:3], normed, inverse)
    third_low = third.astype(BF)
    third_low_ref[...] = third_low
    sums_ref[0:1] += col_sum(upstream * normed)
    sums_ref[1:2] += col_sum(upstream)
    sums_ref[2:3] += col_sum(third)
    back = third
    for start in range(0, hidden, chunk):
        at = slice(start, start + chunk)
        grad = dot_nt(third_low, wdown[at]) * slope[:, at]
        up_sum_ref[:, at] += col_sum(grad)
        grad_low = grad.astype(BF)
        hidden_low_ref[:, at] = grad_low
        back = back + dot_nt(grad_low, wup[:, at])
    zhat2 = zhat2_ref[...]
    second_grad = norm_back_rows(back, gain_ref[1:2], zhat2, inv2_ref[...])
    second_grad_ref[...] = second_grad
    sums_ref[3:4] += col_sum(back * zhat2)
    sums_ref[4:5] += col_sum(back)
    sums_ref[5:6] += col_sum(second_grad)


def ffn(block, chunk, hidden, zhat2, inv2, cot, proj, out_w, up_bias, bias, gain, deps):
    rows, width = zhat2.shape
    shape = jax.ShapeDtypeStruct
    return call(
        functools.partial(ffn_kernel, chunk),
        deps,
        (zhat2, inv2, cot, proj, out_w, up_bias, bias, gain,),
        [
            row_spec(block, width),
            row_spec(block, 1),
            row_spec(block, width),
            ANY,
            ANY,
            whole_spec(1, hidden),
            whole_spec(8, width),
            whole_spec(3, width),
        ],
        grid=(rows // block,),
        out_specs=[
            row_spec(block, width),
            row_spec(block, width),
            row_spec(block, hidden),
            row_spec(block, width),
            row_spec(block, hidden),
            row_spec(block, width),
            whole_spec(8, width),
            whole_spec(1, hidden),
        ],
        out_shape=[
            shape((rows, width), F32),
            shape((rows, width), BF),
            shape((rows, hidden), BF),
            shape((rows, width), BF),
            shape((rows, hidden), BF),
            shape((rows, width), F32),
            shape((8, width), F32),
            shape((1, hidden), F32),
        ],
        scratch_shapes=[
            pltpu.VMEM((width, hidden), BF),
            pltpu.VMEM((hidden, width), BF),
            pltpu.VMEM((block, hidden), F32),
            pltpu.SemaphoreType.DMA((2,)),
        ],
        cost_estimate=cost(rows * width * hidden * 6.5e-9, 40),
    )


def attn_backward_kernel(
    is_text,
    len_ref,
    second_grad_ref,
    triple_ref,
    zhat1_ref,
    inv1_ref,
    proj_ref,
    out_w_ref,
    gain_ref,
    second_low_ref,
    triple_low_ref,
    first_grad_ref,
    first_low_ref,
    context_low_ref,
    sums_ref,
    wco,
    wqkv,
    wo,
    upstream,
    sems,
):
    step = pl.program_id(0)
    rows, width = second_grad_ref.shape
    arrived = fetch(
        step,
        [
            pltpu.make_async_copy(out_w_ref.at[pl.ds(0, CO_W)], wco, sems.at[0]),
            pltpu.make_async_copy(proj_ref.at[:, pl.ds(0, 3 * width)], wqkv, sems.at[1]),
            pltpu.make_async_copy(out_w_ref.at[pl.ds(CO_W, width)], wo, sems.at[2]),
        ],
    )

    @pl.when(step == 0)
    def _():
        sums_ref[...] = jnp.zeros_like(sums_ref)

    second_low = second_grad_ref[...].astype(BF)
    second_low_ref[...] = second_low
    arrived(2)
    upstream[...] = dot_nt(second_low, wo[...]).astype(BF)

    def lanes(part, lane):
        return slice(part * width + lane, part * width + lane + 128)

    if is_text:
        places = list(text_units(len_ref, step, rows // CAP))
        factor = (width // HEADS_T) ** -0.5
    else:
        places = image_units(rows)
        factor = (width // HEADS_I) ** -0.5
    units, ups = [], []
    for where, lane, mask in places:
        q, k, v = [triple_ref[where, lanes(part, lane)] for part in range(3)]
        up = upstream[where, lane : lane + 128]
        units.append((halves(q) if is_text else q, k, v, mask))
        ups.append(halves(up) if is_text else up)
    for (where, lane, _), grads in zip(places, attend_back_all(units, ups, factor)):
        dq, dk, dv = grads
        for part, grad in enumerate((unhalve(dq) if is_text else dq, dk, dv)):
            triple_low_ref[where, lanes(part, lane)] = grad.astype(BF)
    arrived(1)
    back = second_grad_ref[...]
    for part in range(3):
        at = slice(part * width, part * width + width)
        piece = triple_low_ref[:, at]
        back = back + dot_nt(piece, wqkv[:, at])
        if part != 1:
            row = 3 + part // 2
            sums_ref[row : row + 1] += col_sum(piece.astype(F32))
    zhat1 = zhat1_ref[...]
    first_grad = norm_back_rows(back, gain_ref[0:1], zhat1, inv1_ref[...])
    first_grad_ref[...] = first_grad
    sums_ref[0:1] += col_sum(back * zhat1)
    sums_ref[1:2] += col_sum(back)
    sums_ref[2:3] += col_sum(first_grad)
    first_low = first_grad.astype(BF)
    first_low_ref[...] = first_low
    arrived(0)
    context_low_ref[...] = dot_nt(first_low, wco[...]).astype(BF)


def attn_backward(is_text, block, lengths, second_grad, triple, zhat1, inv1, proj, out_w, gain, deps):
    rows, width = zhat1.shape
    shape = jax.ShapeDtypeStruct
    return call(
        functools.partial(attn_backward_kernel, is_text),
        deps,
        (lengths, second_grad, triple, zhat1, inv1, proj, out_w, gain,),
        [
            SMEM,
            row_spec(block, width),
            row_spec(block, 3 * width),
            row_spec(block, width),
            row_spec(block, 1),
            ANY,
            ANY,
            whole_spec(3, width),
        ],
        grid=(rows // block,),
        out_specs=[
            row_spec(block, width),
            row_spec(block, 3 * width),
            row_spec(block, width),
            row_spec(block, width),
            row_spec(block, CO_W),
            whole_spec(8, width),
        ],
        out_shape=[
            shape((rows, width), BF),
            shape((rows, 3 * width), BF),
            shape((rows, width), F32),
            shape((rows, width), BF),
            shape((rows, CO_W), BF),
            shape((8, width), F32),
        ],
        scratch_shapes=[
            pltpu.VMEM((CO_W, width), BF),
            pltpu.VMEM((width, 3 * width), BF),
            pltpu.VMEM((width, width), BF),
            pltpu.VMEM((block, width), BF),
            pltpu.SemaphoreType.DMA((3,)),
        ],
        cost_estimate=cost(rows * width * width * 1.6e-8, 40),
    )


def co_project(inputs, weight, wide):
    bias = jnp.concatenate([wide[:CO_W], jnp.zeros((CO_W,), F32), wide[CO_W : 2 * CO_W]])
    return (dot_nn(inputs, weight[:, : 3 * CO_W]) + bias).astype(BF)


def pad_pairs(block):
    wide = block.reshape(-1, REGIONS, block.shape[1])
    return jnp.pad(wide, ((0, 0), (0, SLOTS - REGIONS), (0, 0))).reshape(-1, block.shape[1])


def unpad_pairs(block):
    return block.reshape(-1, SLOTS, block.shape[1])[:, :REGIONS].reshape(-1, block.shape[1])


def shards(
    text_in,
    image_in,
    lengths,
    t_proj,
    t_out,
    t_bias_wide,
    t_bias,
    t_gain,
    i_proj,
    i_out,
    i_bias_wide,
    i_bias,
    i_gain,
    text_cot,
    image_cot,
):
    small = (t_bias_wide, t_bias, t_gain, i_bias_wide, i_bias, i_gain)
    flat = jnp.concatenate([piece.reshape(-1) for piece in small])
    t_rows = t_proj.shape[0]
    extra = -(-flat.shape[0] // (t_rows * 128)) * 128
    riders = jnp.pad(flat, (0, extra * t_rows - flat.shape[0])).reshape(t_rows, extra)
    near_image = over_x(image_in)
    near_cot = over_x(image_cot)

    def padded(own, rows, cols):
        return jnp.pad(own, ((0, rows - own.shape[0]), (0, cols - own.shape[1])))

    def z_gather(own):
        rows, cols = own.shape
        short = (1 << 20) - 2 * rows * cols * dp_parts()[0]
        if short > 0:
            line = 2 * dp_parts()[0]
            more_rows = -(-short // (line * cols * 8)) * 8
            more_cols = -(-short // (line * rows * 128)) * 128
            if more_rows * cols < more_cols * rows:
                own = padded(own, rows + more_rows, cols)
            else:
                own = padded(own, rows, cols + more_cols)
        return column_by_gather(own, rows, cols)

    t_co_own = jnp.concatenate([t_proj[:, : 3 * CO_W], riders], 1)
    t_co_column = column_by_permutes(t_co_own)
    i_co_column = after(column_by_permutes(i_proj[:, : 3 * CO_W]), near_image, near_cot)
    i_out_column, i_rest_column = z_gather(i_out), z_gather(i_proj[:, 3 * CO_W :])
    t_out_column, t_rest_column = z_gather(t_out), z_gather(t_proj[:, 3 * CO_W :])
    first = [Gather(t_co_column, True), Gather(i_co_column, False)]
    for part in first:
        part.second()
    fars = [part.far for part in first]
    second = [
        Gather(after(i_out_column, *fars), True),
        Gather(after(i_rest_column, *fars), False),
    ]
    for part in first:
        part.core()
    t_co, i_co = [part.full(()) for part in first]
    for part in second:
        part.second()

    shard_count = t_co.shape[0] // t_rows
    table = t_co[:, 3 * CO_W :].reshape(shard_count, -1)[:, : flat.shape[0]].astype(F32)
    taken = []
    offset = 0
    for piece in small:
        block = table[:, offset : offset + piece.size].reshape((shard_count,) + piece.shape)
        offset += piece.size
        if piece.ndim == 1:
            taken.append(block.reshape(1, -1))
        else:
            taken.append(block.transpose(1, 0, 2).reshape(piece.shape[0], -1))
    t_wide, t_rows8, t_gains, i_wide, i_rows8, i_gains = taken

    image_rows = pad_pairs(near_image)
    image_up = pad_pairs(near_cot)
    text_co = co_project(text_in, t_co, t_wide[0])
    image_co = co_project(image_rows, i_co, i_wide[0])
    text_context, image_context = co_forward(
        lengths, text_co, image_co, ()
    )
    fars = [part.far for part in second] + [image_context]
    third = [
        Gather(after(t_out_column, *fars), True),
        Gather(after(t_rest_column, *fars), False),
    ]
    for part in second:
        part.core()
    i_outw, i_rest = [part.full(()) for part in second]
    for part in third:
        part.second()

    image_block = image_rows.shape[0]
    image_hidden = i_wide.shape[1] - 2 * CO_W
    zhat1, inv1, low1, triple, attended, zhat2, inv2 = attn_forward(
        False,
        image_block,
        lengths,
        image_context,
        image_rows,
        i_rest,
        i_outw,
        i_rows8,
        i_gains,
        (),
    )
    i_final, low2, active, third_low, hidden_low, second_grad, i_sums2, i_upsum = ffn(
        image_block,
        512,
        image_hidden,
        zhat2,
        inv2,
        image_up,
        i_rest,
        i_outw,
        i_wide[:, 2 * CO_W :],
        i_rows8,
        i_gains,
        (),
    )
    image_final = over_x(unpad_pairs(i_final).astype(BF))
    second_low, triple_low, i_first, first_low, i_ctx, i_sums1 = attn_backward(
        False, image_block, lengths, second_grad, triple, zhat1, inv1, i_rest, i_outw, i_gains, ()
    )
    i_rest_sum = Scatter(
        cols_grad(shard_count, True, [(low1, triple_low), (low2, hidden_low)], 512), True
    )
    i_out_sum = Scatter(
        rows_grad(
            shard_count, False,
            [(image_context, first_low), (attended, second_low), (active, third_low)],
            256,
        ),
        False,
    )

    for part in third:
        part.core()
    t_outw, t_rest = [part.full([i_first]) for part in third]

    text_block = 256
    text_hidden = t_wide.shape[1] - 2 * CO_W
    zhat1, inv1, low1, triple, attended, zhat2, inv2 = attn_forward(
        True,
        text_block,
        lengths,
        text_context,
        text_in,
        t_rest,
        t_outw,
        t_rows8,
        t_gains,
        [i_rest_sum.keep, i_out_sum.keep, image_final],
    )
    i_rest_sum.link()
    i_out_sum.link()
    t_final, low2, active, third_low, hidden_low, second_grad, t_sums2, t_upsum = ffn(
        text_block,
        512,
        text_hidden,
        zhat2,
        inv2,
        text_cot,
        t_rest,
        t_outw,
        t_wide[:, 2 * CO_W :],
        t_rows8,
        t_gains,
        [i_rest_sum.send, i_out_sum.send],
    )
    i_rest_sum.came = after(i_rest_sum.came, second_grad)
    i_out_sum.came = after(i_out_sum.came, second_grad)
    i_rest_sum.link()
    i_out_sum.link()
    second_low, triple_low, t_first, first_low, t_ctx, t_sums1 = attn_backward(
        True,
        text_block,
        lengths,
        second_grad,
        triple,
        zhat1,
        inv1,
        t_rest,
        t_outw,
        t_gains,
        [i_rest_sum.send, i_out_sum.send],
    )
    i_rest_sum.came = after(i_rest_sum.came, t_ctx)
    i_out_sum.came = after(i_out_sum.came, t_ctx)
    i_rest_sum.column()
    i_out_sum.column()
    t_rest_sum = Scatter(
        cols_grad(shard_count, False, [(low1, triple_low), (low2, hidden_low)], 768, None, [i_rest_sum.send, i_out_sum.send]), False
    )
    t_out_sum = Scatter(
        rows_grad(
            shard_count, True,
            [(text_context, first_low), (attended, second_low), (active, third_low)],
            256,
            [t_rest_sum.keep],
        ),
        True,
    )

    t_rest_sum.link()
    t_co_grad, i_co_grad, t_co_sum, i_co_sum = co_backward(
        lengths, text_co, image_co, t_ctx, i_ctx, [t_out_sum.keep, t_rest_sum.send]
    )
    t_out_sum.came = after(t_out_sum.came, t_rest_sum.send)
    t_out_sum.link()

    def small_grads(sums1, sums2, up_sum, co_sum):
        wide = jnp.concatenate([co_sum[0, :CO_W], co_sum[0, 2 * CO_W :], up_sum[0]])
        rows8 = jnp.stack(
            [sums1[2], sums1[1], sums1[3], sums1[4], sums2[5], sums2[4], sums2[2], sums2[1]]
        )
        return wide, rows8, jnp.stack([sums1[0], sums2[3], sums2[0]])

    pieces = small_grads(t_sums1, t_sums2, t_upsum, t_co_sum) + small_grads(
        i_sums1, i_sums2, i_upsum, i_co_sum
    )
    packed = []
    for piece in pieces:
        if piece.ndim == 1:
            packed.append(piece.reshape(shard_count, -1))
        else:
            packed.append(
                piece.reshape(piece.shape[0], shard_count, -1)
                .transpose(1, 0, 2)
                .reshape(shard_count, -1)
            )
    packed = jnp.concatenate(packed, 1)
    count = packed.shape[1]
    packed = jnp.pad(packed, ((0, 0), (0, extra * t_rows - count))).reshape(-1, extra)

    i_co_sums = Scatter(
        cols_grad(
            shard_count, True,
            [(image_rows, i_co_grad)],
            512,
            deps=[t_rest_sum.send, t_out_sum.send],
        ),
        True,
    )
    t_co_sums = Scatter(
        cols_grad(shard_count, False, [(text_in, t_co_grad)], 768, packed, [i_co_sums.keep]), False
    )
    i_co_sums.link()
    t_co_sums.came = after(t_co_sums.came, i_co_sums.send)
    t_co_sums.link()
    image_grad = after(i_first, i_co_sums.send) + dot_nt(i_co_grad, i_co)
    image_grad = over_x(unpad_pairs(image_grad).astype(BF)).astype(F32)
    text_grad = after(t_first, t_co_sums.send) + dot_nt(t_co_grad, t_co[:, : 3 * CO_W])
    t_rest_sum.link()
    t_out_sum.link()
    t_out_sum.came = after(t_out_sum.came, t_co_sums.send)
    t_rest_sum.column()
    t_out_sum.column()
    i_co_sums.link()
    t_co_sums.link()
    i_co_sums.column_by_permutes()
    t_co_sums.column_by_permutes()
    image_final = image_final.astype(F32)
    t_cog = t_co_sums.total()

    mine = t_cog[:, 3 * CO_W :].reshape(-1)
    outs = []
    offset = 0
    for piece in small:
        outs.append(mine[offset : offset + piece.size].reshape(piece.shape))
        offset += piece.size
    t_wide_g, t_rows_g, t_gain_g, i_wide_g, i_rows_g, i_gain_g = outs
    return (
        t_final,
        image_final,
        text_grad,
        image_grad,
        jnp.concatenate([t_cog[:, : 3 * CO_W], t_rest_sum.total()], 1),
        t_out_sum.total(),
        t_wide_g,
        t_rows_g,
        t_gain_g,
        jnp.concatenate([i_co_sums.total(), i_rest_sum.total()], 1),
        i_out_sum.total(),
        i_wide_g,
        i_rows_g,
        i_gain_g,
    )


def solution(mesh):
    both = ("stream", "dp")
    rows, cols, flat = P(both, None), P(None, both), P(both)
    weights = (rows, rows, flat, cols, cols)
    return jax.shard_map(
        shards,
        mesh=mesh,
        in_specs=(rows, rows, flat) + weights + weights + (rows, rows),
        out_specs=(rows, rows, rows, rows) + weights + weights,
        check_vma=False,
    )
```

```python
import functools

import jax
import jax.numpy as jnp
from jax import lax
from jax.experimental import pallas as pl
from jax.experimental.pallas import tpu as pltpu
from jax.sharding import PartitionSpec as P

CO_W = 1024
HEADS_T = 12
HEADS_I = 8
CO_HEADS = 8
CAP = 128
REGIONS = 36
SLOTS = 48

epsilon = 1e-05
negative = -1e30
BF = jnp.bfloat16
F32 = jnp.float32
VMEM_LIMIT = 60 * 1024 * 1024
HALF_ROOT = 0.7071067811865476
INV_ROOT = 0.3989422804014327
ANY = pl.BlockSpec(memory_space=pl.ANY)
SMEM = pl.BlockSpec(memory_space=pltpu.SMEM)


def dot_nn(a, b):
    return lax.dot_general(a, b, (((1,), (0,)), ((), ())), preferred_element_type=F32)


def dot_nt(a, b):
    return lax.dot_general(a, b, (((1,), (1,)), ((), ())), preferred_element_type=F32)


def dot_tn(a, b):
    return lax.dot_general(a, b, (((0,), (0,)), ((), ())), preferred_element_type=F32)


def params():
    return pltpu.CompilerParams(vmem_limit_bytes=VMEM_LIMIT)


def call(kernel, deps, operands, in_specs, **kwargs):
    count = len(operands)

    def body(*refs):
        kernel(*refs[:count], *refs[count + len(deps) :])

    return pl.pallas_call(
        body,
        in_specs=in_specs + [ANY] * len(deps),
        compiler_params=params(),
        **kwargs,
    )(*operands, *deps)


def cost(gmacs, mbytes):
    return pl.CostEstimate(
        flops=int(2e9 * gmacs), bytes_accessed=int(1e6 * mbytes), transcendentals=0
    )


def dp_parts():
    total = lax.axis_size("dp")
    index = lax.axis_index("dp")
    return total // 4, index // 4, (index // 2) % 2, index % 2


def over_core(block):
    total = lax.axis_size("dp")
    return lax.ppermute(block, "dp", [(d, d ^ 1) for d in range(total)])


def over_y(block):
    total = lax.axis_size("dp")
    return lax.ppermute(block, "dp", [(d, d ^ 2) for d in range(total)])


def over_x(block):
    total = lax.axis_size("stream")
    return lax.ppermute(block, "stream", [(d, d ^ 1) for d in range(total)])


def over_z(block, shift):
    total = lax.axis_size("dp")
    return lax.ppermute(block, "dp", [(d, (d + 4 * shift) % total) for d in range(total)])


def pick(buffer, position, axis):
    return lax.dynamic_index_in_dim(buffer, position, axis, keepdims=False)


def place_kernel(blocks, table_ref, *refs):
    count = (len(refs) - 3) // 2
    pieces, out_ref = refs[:count], refs[count]
    held, in_sems, out_sems = refs[count + 1 : 2 * count + 1], refs[2 * count + 1], refs[2 * count + 2]
    loads, stores = [], []
    for number in range(count * blocks):
        piece, block = number // blocks, number % blocks
        x, y, c = [table_ref[3 * number + i] for i in range(3)]
        loads.append(
            pltpu.make_async_copy(pieces[piece].at[block], held[piece].at[block], in_sems.at[number])
        )
        stores.append(
            pltpu.make_async_copy(
                held[piece].at[block], out_ref.at[x, :, y, c], out_sems.at[number]
            )
        )
    for load in loads:
        load.start()
    for load, store in zip(loads, stores):
        load.wait()
        store.start()
    for store in stores:
        store.wait()


def place(pieces, table, deps):
    blocks, nz, rows, cols = pieces[0].shape
    size = 4 * len(pieces) * pieces[0].size
    return call(
        functools.partial(place_kernel, blocks),
        deps,
        (table, *pieces),
        [SMEM] + [ANY] * len(pieces),
        out_specs=ANY,
        out_shape=jax.ShapeDtypeStruct((2, nz, 2, 2, rows, cols), pieces[0].dtype),
        scratch_shapes=[pltpu.VMEM(piece.shape, piece.dtype) for piece in pieces]
        + [pltpu.SemaphoreType.DMA((len(pieces) * blocks,))] * 2,
        cost_estimate=pl.CostEstimate(flops=0, bytes_accessed=size, transcendentals=0),
    )


def table_of(rows):
    return jnp.stack([jnp.asarray(v, jnp.int32) for row in rows for v in row])


def z_groups():
    total = lax.axis_size("dp")
    return [[first + 4 * k for k in range(total // 4)] for first in range(4)]


def after_kernel(*refs):
    pass


def after(block, *earlier):
    return pl.pallas_call(
        after_kernel,
        in_specs=[ANY] * (1 + len(earlier)),
        out_specs=ANY,
        out_shape=jax.ShapeDtypeStruct(block.shape, block.dtype),
        input_output_aliases={0: 0},
        compiler_params=params(),
        cost_estimate=pl.CostEstimate(flops=0, bytes_accessed=0, transcendentals=0),
    )(block, *earlier)


def column_by_permutes(own):
    nz, z, _, _ = dp_parts()
    came = jnp.stack([own] + [over_z(own, shift) for shift in range(1, nz)])
    turned = jnp.concatenate([came[::-1]] * 2)
    return lax.dynamic_slice_in_dim(turned, nz - 1 - z, nz, 0)


def column_by_gather(own, rows, cols):
    full = lax.all_gather(own, "dp", axis_index_groups=z_groups(), axis=0)
    return full[:, :rows, :cols]


class Gather:
    def __init__(self, column, y_first):
        self.column = column
        self.links = (over_y, over_x) if y_first else (over_x, over_y)
        self.y_first = y_first
        self.over = self.links[0](column)

    def second(self):
        self.pair = jnp.stack([self.column, self.over])
        self.far = self.links[1](self.pair)

    def core(self):
        self.others = [over_core(self.pair), over_core(self.far)]

    def full(self, deps):
        _, _, y, c = dp_parts()
        x = lax.axis_index("stream")
        table = []
        for core in (0, 1):
            for outer in (0, 1):
                for inner in (0, 1):
                    dx, dy = (outer, inner) if self.y_first else (inner, outer)
                    table.append((x ^ dx, y ^ dy, c ^ core))
        whole = place([self.pair, self.far] + self.others, table_of(table), deps)
        return whole.reshape(-1, whole.shape[-1])


def add_low(kept, came):
    return (kept.astype(F32) + came.astype(F32)).astype(BF)


class Scatter:
    def __init__(self, halves, y_first):
        self.send, self.keep = halves
        self.came = over_core(self.send)
        self.axes = ("y", "x") if y_first else ("x", "y")

    def link(self):
        axis, self.axes = self.axes[0], self.axes[1:]
        at = dp_parts()[2] if axis == "y" else lax.axis_index("stream")
        self.send = add_low(pick(self.keep, 1 - at, 0), pick(self.came, 1 - at, 0))
        self.keep = add_low(pick(self.keep, at, 0), pick(self.came, at, 0))
        self.came = over_y(self.send) if axis == "y" else over_x(self.send)

    def column_by_permutes(self):
        nz, z, _, _ = dp_parts()
        self.send = add_low(self.keep, self.came)
        self.sum = pick(self.send, z, 0).astype(F32)
        for shift in range(1, nz):
            came = over_z(pick(self.send, (z + shift) % nz, 0), shift)
            self.sum = self.sum + came.astype(F32)

    def column(self):
        self.send = add_low(self.keep, self.came)
        self.sum = lax.psum_scatter(
            self.send.reshape(-1, self.send.shape[-1]),
            "dp",
            axis_index_groups=z_groups(),
            scatter_dimension=0,
            tiled=True,
        )

    def total(self):
        return self.sum.astype(F32)


def store_halves(y_first, core_ref, send_ref, keep_ref, block, at):
    columns, rows = send_ref.shape[:2]
    nz = columns // 4

    def store(even_ref, odd_ref):
        for number in range(columns):
            x, z, y = number // (2 * nz), number // 2 % nz, number % 2
            spot = (y * 2 + x if y_first else x * 2 + y) * nz + z
            start = 2 * number * rows
            even_ref[spot, :, at] = block[start : start + rows].astype(BF)
            odd_ref[spot, :, at] = block[start + rows : start + 2 * rows].astype(BF)

    @pl.when(core_ref[0] == 0)
    def _():
        store(keep_ref, send_ref)

    @pl.when(core_ref[0] == 1)
    def _():
        store(send_ref, keep_ref)


def cols_grad_kernel(y_first, counts, tile, has_riders, core_ref, *refs):
    segments = len(counts)
    lhs, ups = refs[:segments], refs[segments : 2 * segments]
    riders = refs[2 * segments] if has_riders else None
    send_ref, keep_ref = refs[2 * segments + has_riders : 2 * segments + has_riders + 2]
    turned = refs[2 * segments + has_riders + 2 :]
    step = pl.program_id(0)

    @pl.when(step == 0)
    def _():
        for flat, kept in zip(lhs, turned):
            kept[...] = flat[...].T

    first = 0
    for count, kept, up in zip(counts, turned, ups):

        @pl.when((step >= first) & (step < first + count))
        def _(kept=kept, up=up):
            at = pl.ds(pl.multiple_of(step * tile, 128), tile) if has_riders else slice(None)
            store_halves(y_first, core_ref, send_ref, keep_ref, dot_nn(kept[...], up[...]), at)

        first += count
    if has_riders:

        @pl.when(step == 0)
        def _():
            width = riders.shape[1]
            start = sum(counts) * tile
            store_halves(y_first, core_ref, send_ref, keep_ref, riders[...], slice(start, start + width))


def half_shapes(shards, rows, cols):
    return [jax.ShapeDtypeStruct((shards // 2, rows, cols), BF)] * 2


def cols_grad(shards, y_first, segments, tile, riders=None, deps=()):
    counts = [up.shape[1] // tile for _, up in segments]
    width = segments[0][0].shape[1]
    length = segments[0][0].shape[0]
    rows = width // shards
    total = sum(counts) * tile + (0 if riders is None else riders.shape[1])
    starts = [sum(counts[:i]) for i in range(len(counts))]

    def up_spec(start, count):
        return pl.BlockSpec((length, tile), lambda j: (0, jnp.clip(j - start, 0, count - 1)))

    whole = [pl.BlockSpec(lhs.shape, lambda j: (0, 0)) for lhs, _ in segments]
    tiles = [up_spec(start, count) for start, count in zip(starts, counts)]
    extra = [] if riders is None else [riders]
    core = jnp.reshape(dp_parts()[3], (1,)).astype(jnp.int32)
    if riders is None:
        out = pl.BlockSpec((shards // 2, rows, tile), lambda j: (0, 0, j))
    else:
        out = pl.BlockSpec((shards // 2, rows, total), lambda j: (0, 0, 0))
    halves = call(
        functools.partial(cols_grad_kernel, y_first, counts, tile, len(extra)),
        deps,
        (core,) + tuple(lhs for lhs, _ in segments) + tuple(up for _, up in segments) + tuple(extra),
        [SMEM] + whole + tiles + [pl.BlockSpec(block.shape, lambda j: (0, 0)) for block in extra],
        grid=(sum(counts),),
        out_specs=[out, out],
        out_shape=half_shapes(shards, rows, total),
        scratch_shapes=[pltpu.VMEM((width, length), BF) for _ in segments],
        cost_estimate=cost(1.3e-9 * length * width * total, 20),
    )
    return [half.reshape(2, 2, -1, rows, total) for half in halves]


def rows_grad_kernel(y_first, segments, tile, core_ref, *refs):
    lhs, ups = refs[:segments], refs[segments : 2 * segments]
    send_ref, keep_ref, total = refs[2 * segments : 2 * segments + 3]
    turned = refs[2 * segments + 3 :]

    @pl.when(pl.program_id(0) == 0)
    def _():
        for flat, kept in zip(lhs, turned):
            kept[...] = flat[...].T

    start = 0
    for kept, up in zip(turned, ups):
        for row in range(0, kept.shape[0], 256):
            total[start + row : start + row + 256] = dot_nn(kept[row : row + 256], up[...])
        start += kept.shape[0]
    store_halves(y_first, core_ref, send_ref, keep_ref, total, slice(None))


def rows_grad(shards, y_first, segments, tile, deps=()):
    length = segments[0][0].shape[0]
    height = sum(lhs.shape[1] for lhs, _ in segments)
    width = segments[0][1].shape[1]
    rows = height // shards
    core = jnp.reshape(dp_parts()[3], (1,)).astype(jnp.int32)
    out = pl.BlockSpec((shards // 2, rows, tile), lambda j: (0, 0, j))
    halves = call(
        functools.partial(rows_grad_kernel, y_first, len(segments), tile),
        deps,
        (core,) + tuple(lhs for lhs, _ in segments) + tuple(up for _, up in segments),
        [SMEM]
        + [
            pl.BlockSpec(lhs.shape, lambda j: (0, 0), pipeline_mode=pl.Buffered(1))
            for lhs, _ in segments
        ]
        + [pl.BlockSpec((length, tile), lambda j: (0, j)) for _ in segments],
        grid=(width // tile,),
        out_specs=[out, out],
        out_shape=half_shapes(shards, rows, width),
        scratch_shapes=[pltpu.VMEM((height, tile), F32)]
        + [pltpu.VMEM((lhs.shape[1], length), BF) for lhs, _ in segments],
        cost_estimate=cost(1.3e-9 * length * height * width, 20),
    )
    return [half.reshape(2, 2, -1, rows, width) for half in halves]


def softmax_rows(scores):
    high = jnp.max(scores, -1, keepdims=True)
    exponent = jnp.exp(scores - high)
    return exponent * (1.0 / jnp.sum(exponent, -1, keepdims=True))


def norm_rows(pre_norm):
    centered = pre_norm - jnp.mean(pre_norm, -1, keepdims=True)
    inverse = lax.rsqrt(jnp.mean(centered * centered, -1, keepdims=True) + epsilon)
    return centered * inverse, inverse


def norm_back_rows(upstream, gain, normed, inverse):
    scaled = upstream * gain
    return inverse * (
        scaled
        - jnp.mean(scaled, -1, keepdims=True)
        - normed * jnp.mean(scaled * normed, -1, keepdims=True)
    )


def col_sum(block):
    return jnp.sum(block, 0, keepdims=True)


def key_mask(shape, count):
    return jnp.where(lax.broadcasted_iota(jnp.int32, shape, 1) < count, 0.0, negative)


def attend_all(units, factor):
    scores = [dot_nt(q, k) * factor + mask for q, k, _, mask in units]
    probs = [softmax_rows(score).astype(BF) for score in scores]
    return [dot_nn(prob, unit[2]) for prob, unit in zip(probs, units)]


def attend_back_all(units, upstreams, factor):
    scores = [dot_nt(q, k) * factor + mask for q, k, _, mask in units]
    raised = [dot_nt(up, unit[2]) for up, unit in zip(upstreams, units)]
    probs = [softmax_rows(score) for score in scores]
    values_grad = [dot_tn(prob.astype(BF), up) for prob, up in zip(probs, upstreams)]
    rounded = [
        (prob * (grad - jnp.sum(prob * grad, -1, keepdims=True)) * factor).astype(BF)
        for prob, grad in zip(probs, raised)
    ]
    queries_grad = [dot_nn(low, unit[1]) for low, unit in zip(rounded, units)]
    keys_grad = [dot_tn(low, unit[0]) for low, unit in zip(rounded, units)]
    return list(zip(queries_grad, keys_grad, values_grad))


def co_forward_kernel(len_ref, text_ref, image_ref, text_out, image_out):
    step = pl.program_id(0)
    factor = (CO_W // CO_HEADS) ** -0.5
    region_mask = key_mask((1, SLOTS), REGIONS)
    text_mask = key_mask((1, CAP), len_ref[step])
    units, places = [], []
    for head in range(CO_HEADS):
        at = [slice(part * CO_W + head * 128, part * CO_W + head * 128 + 128) for part in range(3)]
        tq, tk, tv = [text_ref[:, where] for where in at]
        iq, ik, iv = [image_ref[:, where] for where in at]
        units += [(tq, ik, iv, region_mask), (iq, tk, tv, text_mask)]
        places += [(text_out, at[0]), (image_out, at[0])]
    for (out_ref, where), context in zip(places, attend_all(units, factor)):
        out_ref[:, where] = context.astype(BF)


def co_forward(lengths, text_co, image_co, deps):
    pairs = lengths.shape[0]
    return call(
        co_forward_kernel,
        deps,
        (lengths, text_co, image_co,),
        [
            SMEM,
            pl.BlockSpec((CAP, 3 * CO_W), lambda i: (i, 0)),
            pl.BlockSpec((SLOTS, 3 * CO_W), lambda i: (i, 0)),
        ],
        grid=(pairs,),
        out_specs=[
            pl.BlockSpec((CAP, CO_W), lambda i: (i, 0)),
            pl.BlockSpec((SLOTS, CO_W), lambda i: (i, 0)),
        ],
        out_shape=[
            jax.ShapeDtypeStruct((pairs * CAP, CO_W), BF),
            jax.ShapeDtypeStruct((pairs * SLOTS, CO_W), BF),
        ],
        cost_estimate=cost(2 * lengths.shape[0] * 0.4, 8),
    )


def co_backward_kernel(
    len_ref, text_ref, image_ref, text_up, image_up, text_out, image_out, text_sum, image_sum
):
    step = pl.program_id(0)
    factor = (CO_W // CO_HEADS) ** -0.5
    region_mask = key_mask((1, SLOTS), REGIONS)
    text_mask = key_mask((1, CAP), len_ref[step])

    @pl.when(step == 0)
    def _():
        text_sum[...] = jnp.zeros_like(text_sum)
        image_sum[...] = jnp.zeros_like(image_sum)

    def store(out_ref, sum_ref, where, grad):
        low = grad.astype(BF)
        out_ref[:, where] = low
        sum_ref[:, where] += col_sum(low.astype(F32))

    units, ups, places = [], [], []
    for head in range(CO_HEADS):
        at = [slice(part * CO_W + head * 128, part * CO_W + head * 128 + 128) for part in range(3)]
        tq, tk, tv = [text_ref[:, where] for where in at]
        iq, ik, iv = [image_ref[:, where] for where in at]
        units += [(tq, ik, iv, region_mask), (iq, tk, tv, text_mask)]
        ups += [text_up[:, at[0]], image_up[:, at[0]]]
        places.append(at)
    grads = attend_back_all(units, ups, factor)
    for head, at in enumerate(places):
        dtq, dik, div = grads[2 * head]
        diq, dtk, dtv = grads[2 * head + 1]
        for where, grad in zip(at, (dtq, dtk, dtv)):
            store(text_out, text_sum, where, grad)
        for where, grad in zip(at, (diq, dik, div)):
            store(image_out, image_sum, where, grad)


def co_backward(lengths, text_co, image_co, text_up, image_up, deps):
    pairs = lengths.shape[0]
    wide = 3 * CO_W
    return call(
        co_backward_kernel,
        deps,
        (lengths, text_co, image_co, text_up, image_up,),
        [
            SMEM,
            pl.BlockSpec((CAP, wide), lambda i: (i, 0)),
            pl.BlockSpec((SLOTS, wide), lambda i: (i, 0)),
            pl.BlockSpec((CAP, CO_W), lambda i: (i, 0)),
            pl.BlockSpec((SLOTS, CO_W), lambda i: (i, 0)),
        ],
        grid=(pairs,),
        out_specs=[
            pl.BlockSpec((CAP, wide), lambda i: (i, 0)),
            pl.BlockSpec((SLOTS, wide), lambda i: (i, 0)),
            pl.BlockSpec((1, wide), lambda i: (0, 0)),
            pl.BlockSpec((1, wide), lambda i: (0, 0)),
        ],
        out_shape=[
            jax.ShapeDtypeStruct((pairs * CAP, wide), BF),
            jax.ShapeDtypeStruct((pairs * SLOTS, wide), BF),
            jax.ShapeDtypeStruct((1, wide), F32),
            jax.ShapeDtypeStruct((1, wide), F32),
        ],
        cost_estimate=cost(2 * lengths.shape[0] * 0.5, 20),
    )


def fetch(step, copies):
    @pl.when(step == 0)
    def _():
        for copy in copies:
            copy.start()

    def arrived(number):
        @pl.when(step == 0)
        def _():
            copies[number].wait()

    return arrived


def text_units(len_ref, step, pair_count):
    for pair in range(pair_count):
        mask = key_mask((1, CAP), len_ref[step * pair_count + pair])
        for block in range(HEADS_T // 2):
            yield slice(pair * CAP, pair * CAP + CAP), block * 128, mask


def image_mask():
    shape = (2 * SLOTS, 2 * SLOTS)
    row = lax.broadcasted_iota(jnp.int32, shape, 0)
    col = lax.broadcasted_iota(jnp.int32, shape, 1)
    same = (row >= SLOTS) == (col >= SLOTS)
    local = jnp.where(col >= SLOTS, col - SLOTS, col)
    return jnp.where(same & (local < REGIONS), 0.0, negative)


def image_units(rows):
    mask = image_mask()
    return [
        (slice(start, start + 2 * SLOTS), head * 128, mask)
        for start in range(0, rows, 2 * SLOTS)
        for head in range(HEADS_I)
    ]


def halves(block):
    low = lax.broadcasted_iota(jnp.int32, block.shape, 1) < 64
    zero = jnp.zeros_like(block)
    return jnp.concatenate([jnp.where(low, block, zero), jnp.where(low, zero, block)], 0)


def unhalve(stacked):
    rows = stacked.shape[0] // 2
    low = lax.broadcasted_iota(jnp.int32, (rows, stacked.shape[1]), 1) < 64
    return jnp.where(low, stacked[:rows], stacked[rows:])


def attn_forward_kernel(
    is_text,
    down_at,
    len_ref,
    context_ref,
    input_ref,
    proj_ref,
    out_w_ref,
    bias_ref,
    gain_ref,
    zhat1_ref,
    inv1_ref,
    low1_ref,
    triple_ref,
    attended_ref,
    zhat2_ref,
    inv2_ref,
    wco,
    wqkv,
    wo,
    sems,
):
    step = pl.program_id(0)
    width = input_ref.shape[1]
    rows = input_ref.shape[0]
    arrived = fetch(
        step,
        [
            pltpu.make_async_copy(out_w_ref.at[pl.ds(0, CO_W)], wco, sems.at[0]),
            pltpu.make_async_copy(proj_ref.at[:, pl.ds(0, 3 * width)], wqkv, sems.at[1]),
            pltpu.make_async_copy(out_w_ref.at[pl.ds(CO_W, width)], wo, sems.at[2]),
        ],
    )
    arrived(0)
    normed, inverse = norm_rows(
        input_ref[...].astype(F32) + dot_nn(context_ref[...], wco[...]) + bias_ref[0:1]
    )
    zhat1_ref[...] = normed
    inv1_ref[...] = inverse
    first = normed * gain_ref[0:1] + bias_ref[1:2]
    first_low = first.astype(BF)
    low1_ref[...] = first_low
    arrived(1)
    for part in range(3):
        at = slice(part * width, part * width + width)
        piece = dot_nn(first_low, wqkv[:, at])
        if part == 0:
            piece = piece + bias_ref[2:3]
        if part == 2:
            piece = piece + bias_ref[3:4]
        triple_ref[:, at] = piece.astype(BF)

    def lanes(part, lane):
        return slice(part * width + lane, part * width + lane + 128)

    if is_text:
        places = list(text_units(len_ref, step, rows // CAP))
        factor = (width // HEADS_T) ** -0.5
    else:
        places = image_units(rows)
        factor = (width // HEADS_I) ** -0.5
    units = []
    for where, lane, mask in places:
        q, k, v = [triple_ref[where, lanes(part, lane)] for part in range(3)]
        units.append((halves(q) if is_text else q, k, v, mask))
    for (where, lane, _), context in zip(places, attend_all(units, factor)):
        context = unhalve(context) if is_text else context
        attended_ref[where, lane : lane + 128] = context.astype(BF)
    arrived(2)
    normed, inverse = norm_rows(first + dot_nn(attended_ref[...], wo[...]) + bias_ref[4:5])
    zhat2_ref[...] = normed
    inv2_ref[...] = inverse


def row_spec(rows, cols):
    return pl.BlockSpec((rows, cols), lambda i: (i, 0))


def whole_spec(rows, cols):
    return pl.BlockSpec((rows, cols), lambda i: (0, 0))


def attn_forward(is_text, block, lengths, context, inputs, proj, out_w, bias, gain, deps):
    rows, width = inputs.shape
    shape = jax.ShapeDtypeStruct
    return call(
        functools.partial(attn_forward_kernel, is_text, CO_W + width),
        deps,
        (lengths, context, inputs, proj, out_w, bias, gain,),
        [
            SMEM,
            row_spec(block, CO_W),
            row_spec(block, width),
            ANY,
            ANY,
            whole_spec(8, width),
            whole_spec(3, width),
        ],
        grid=(rows // block,),
        out_specs=[
            row_spec(block, width),
            row_spec(block, 1),
            row_spec(block, width),
            row_spec(block, 3 * width),
            row_spec(block, width),
            row_spec(block, width),
            row_spec(block, 1),
        ],
        out_shape=[
            shape((rows, width), F32),
            shape((rows, 1), F32),
            shape((rows, width), BF),
            shape((rows, 3 * width), BF),
            shape((rows, width), BF),
            shape((rows, width), F32),
            shape((rows, 1), F32),
        ],
        scratch_shapes=[
            pltpu.VMEM((CO_W, width), BF),
            pltpu.VMEM((width, 3 * width), BF),
            pltpu.VMEM((width, width), BF),
            pltpu.SemaphoreType.DMA((3,)),
        ],
        cost_estimate=cost(rows * width * width * 1.6e-8, 40),
    )


def ffn_kernel(
    chunk,
    zhat2_ref,
    inv2_ref,
    cot_ref,
    proj_ref,
    out_w_ref,
    up_bias_ref,
    bias_ref,
    gain_ref,
    final_ref,
    low2_ref,
    active_ref,
    third_low_ref,
    hidden_low_ref,
    second_grad_ref,
    sums_ref,
    up_sum_ref,
    wup,
    wdown,
    slope,
    sems,
):
    step = pl.program_id(0)
    width = zhat2_ref.shape[1]
    hidden = wup.shape[1]
    arrived = fetch(
        step,
        [
            pltpu.make_async_copy(proj_ref.at[:, pl.ds(3 * width, hidden)], wup, sems.at[0]),
            pltpu.make_async_copy(out_w_ref.at[pl.ds(CO_W + width, hidden)], wdown, sems.at[1]),
        ],
    )

    @pl.when(step == 0)
    def _():
        sums_ref[...] = jnp.zeros_like(sums_ref)
        up_sum_ref[...] = jnp.zeros_like(up_sum_ref)

    arrived(0)
    arrived(1)
    second = zhat2_ref[...] * gain_ref[1:2] + bias_ref[5:6]
    second_low = second.astype(BF)
    low2_ref[...] = second_low
    total = second + bias_ref[6:7]
    for start in range(0, hidden, chunk):
        at = slice(start, start + chunk)
        u = dot_nn(second_low, wup[:, at]) + up_bias_ref[:, at]
        phi = 0.5 + 0.5 * lax.erf(u * HALF_ROOT)
        active = (u * phi).astype(BF)
        active_ref[:, at] = active
        slope[:, at] = phi + (u * INV_ROOT) * jnp.exp(-0.5 * u * u)
        total = total + dot_nn(active, wdown[at])
    normed, inverse = norm_rows(total)
    final_ref[...] = normed * gain_ref[2:3] + bias_ref[7:8]
    upstream = cot_ref[...].astype(F32)
    third = norm_back_rows(upstream, gain_ref[2:3], normed, inverse)
    third_low = third.astype(BF)
    third_low_ref[...] = third_low
    sums_ref[0:1] += col_sum(upstream * normed)
    sums_ref[1:2] += col_sum(upstream)
    sums_ref[2:3] += col_sum(third)
    back = third
    for start in range(0, hidden, chunk):
        at = slice(start, start + chunk)
        grad = dot_nt(third_low, wdown[at]) * slope[:, at]
        up_sum_ref[:, at] += col_sum(grad)
        grad_low = grad.astype(BF)
        hidden_low_ref[:, at] = grad_low
        back = back + dot_nt(grad_low, wup[:, at])
    zhat2 = zhat2_ref[...]
    second_grad = norm_back_rows(back, gain_ref[1:2], zhat2, inv2_ref[...])
    second_grad_ref[...] = second_grad
    sums_ref[3:4] += col_sum(back * zhat2)
    sums_ref[4:5] += col_sum(back)
    sums_ref[5:6] += col_sum(second_grad)


def ffn(block, chunk, hidden, zhat2, inv2, cot, proj, out_w, up_bias, bias, gain, deps):
    rows, width = zhat2.shape
    shape = jax.ShapeDtypeStruct
    return call(
        functools.partial(ffn_kernel, chunk),
        deps,
        (zhat2, inv2, cot, proj, out_w, up_bias, bias, gain,),
        [
            row_spec(block, width),
            row_spec(block, 1),
            row_spec(block, width),
            ANY,
            ANY,
            whole_spec(1, hidden),
            whole_spec(8, width),
            whole_spec(3, width),
        ],
        grid=(rows // block,),
        out_specs=[
            row_spec(block, width),
            row_spec(block, width),
            row_spec(block, hidden),
            row_spec(block, width),
            row_spec(block, hidden),
            row_spec(block, width),
            whole_spec(8, width),
            whole_spec(1, hidden),
        ],
        out_shape=[
            shape((rows, width), F32),
            shape((rows, width), BF),
            shape((rows, hidden), BF),
            shape((rows, width), BF),
            shape((rows, hidden), BF),
            shape((rows, width), F32),
            shape((8, width), F32),
            shape((1, hidden), F32),
        ],
        scratch_shapes=[
            pltpu.VMEM((width, hidden), BF),
            pltpu.VMEM((hidden, width), BF),
            pltpu.VMEM((block, hidden), F32),
            pltpu.SemaphoreType.DMA((2,)),
        ],
        cost_estimate=cost(rows * width * hidden * 6.5e-9, 40),
    )


def attn_backward_kernel(
    is_text,
    len_ref,
    second_grad_ref,
    triple_ref,
    zhat1_ref,
    inv1_ref,
    proj_ref,
    out_w_ref,
    gain_ref,
    second_low_ref,
    triple_low_ref,
    first_grad_ref,
    first_low_ref,
    context_low_ref,
    sums_ref,
    wco,
    wqkv,
    wo,
    upstream,
    sems,
):
    step = pl.program_id(0)
    rows, width = second_grad_ref.shape
    arrived = fetch(
        step,
        [
            pltpu.make_async_copy(out_w_ref.at[pl.ds(0, CO_W)], wco, sems.at[0]),
            pltpu.make_async_copy(proj_ref.at[:, pl.ds(0, 3 * width)], wqkv, sems.at[1]),
            pltpu.make_async_copy(out_w_ref.at[pl.ds(CO_W, width)], wo, sems.at[2]),
        ],
    )

    @pl.when(step == 0)
    def _():
        sums_ref[...] = jnp.zeros_like(sums_ref)

    second_low = second_grad_ref[...].astype(BF)
    second_low_ref[...] = second_low
    arrived(2)
    upstream[...] = dot_nt(second_low, wo[...]).astype(BF)

    def lanes(part, lane):
        return slice(part * width + lane, part * width + lane + 128)

    if is_text:
        places = list(text_units(len_ref, step, rows // CAP))
        factor = (width // HEADS_T) ** -0.5
    else:
        places = image_units(rows)
        factor = (width // HEADS_I) ** -0.5
    units, ups = [], []
    for where, lane, mask in places:
        q, k, v = [triple_ref[where, lanes(part, lane)] for part in range(3)]
        up = upstream[where, lane : lane + 128]
        units.append((halves(q) if is_text else q, k, v, mask))
        ups.append(halves(up) if is_text else up)
    for (where, lane, _), grads in zip(places, attend_back_all(units, ups, factor)):
        dq, dk, dv = grads
        for part, grad in enumerate((unhalve(dq) if is_text else dq, dk, dv)):
            triple_low_ref[where, lanes(part, lane)] = grad.astype(BF)
    arrived(1)
    back = second_grad_ref[...]
    for part in range(3):
        at = slice(part * width, part * width + width)
        piece = triple_low_ref[:, at]
        back = back + dot_nt(piece, wqkv[:, at])
        if part != 1:
            row = 3 + part // 2
            sums_ref[row : row + 1] += col_sum(piece.astype(F32))
    zhat1 = zhat1_ref[...]
    first_grad = norm_back_rows(back, gain_ref[0:1], zhat1, inv1_ref[...])
    first_grad_ref[...] = first_grad
    sums_ref[0:1] += col_sum(back * zhat1)
    sums_ref[1:2] += col_sum(back)
    sums_ref[2:3] += col_sum(first_grad)
    first_low = first_grad.astype(BF)
    first_low_ref[...] = first_low
    arrived(0)
    context_low_ref[...] = dot_nt(first_low, wco[...]).astype(BF)


def attn_backward(is_text, block, lengths, second_grad, triple, zhat1, inv1, proj, out_w, gain, deps):
    rows, width = zhat1.shape
    shape = jax.ShapeDtypeStruct
    return call(
        functools.partial(attn_backward_kernel, is_text),
        deps,
        (lengths, second_grad, triple, zhat1, inv1, proj, out_w, gain,),
        [
            SMEM,
            row_spec(block, width),
            row_spec(block, 3 * width),
            row_spec(block, width),
            row_spec(block, 1),
            ANY,
            ANY,
            whole_spec(3, width),
        ],
        grid=(rows // block,),
        out_specs=[
            row_spec(block, width),
            row_spec(block, 3 * width),
            row_spec(block, width),
            row_spec(block, width),
            row_spec(block, CO_W),
            whole_spec(8, width),
        ],
        out_shape=[
            shape((rows, width), BF),
            shape((rows, 3 * width), BF),
            shape((rows, width), F32),
            shape((rows, width), BF),
            shape((rows, CO_W), BF),
            shape((8, width), F32),
        ],
        scratch_shapes=[
            pltpu.VMEM((CO_W, width), BF),
            pltpu.VMEM((width, 3 * width), BF),
            pltpu.VMEM((width, width), BF),
            pltpu.VMEM((block, width), BF),
            pltpu.SemaphoreType.DMA((3,)),
        ],
        cost_estimate=cost(rows * width * width * 1.6e-8, 40),
    )


def co_project(inputs, weight, wide):
    bias = jnp.concatenate([wide[:CO_W], jnp.zeros((CO_W,), F32), wide[CO_W : 2 * CO_W]])
    return (dot_nn(inputs, weight[:, : 3 * CO_W]) + bias).astype(BF)


def pad_pairs(block):
    wide = block.reshape(-1, REGIONS, block.shape[1])
    return jnp.pad(wide, ((0, 0), (0, SLOTS - REGIONS), (0, 0))).reshape(-1, block.shape[1])


def unpad_pairs(block):
    return block.reshape(-1, SLOTS, block.shape[1])[:, :REGIONS].reshape(-1, block.shape[1])


def shards(
    text_in,
    image_in,
    lengths,
    t_proj,
    t_out,
    t_bias_wide,
    t_bias,
    t_gain,
    i_proj,
    i_out,
    i_bias_wide,
    i_bias,
    i_gain,
    text_cot,
    image_cot,
):
    small = (t_bias_wide, t_bias, t_gain, i_bias_wide, i_bias, i_gain)
    flat = jnp.concatenate([piece.reshape(-1) for piece in small])
    t_rows = t_proj.shape[0]
    extra = -(-flat.shape[0] // (t_rows * 128)) * 128
    riders = jnp.pad(flat, (0, extra * t_rows - flat.shape[0])).reshape(t_rows, extra)
    near_image = over_x(image_in)
    near_cot = over_x(image_cot)

    def padded(own, rows, cols):
        return jnp.pad(own, ((0, rows - own.shape[0]), (0, cols - own.shape[1])))

    def z_gather(own):
        rows, cols = own.shape
        short = (1 << 20) - 2 * rows * cols * dp_parts()[0]
        if short > 0:
            line = 2 * dp_parts()[0]
            more_rows = -(-short // (line * cols * 8)) * 8
            more_cols = -(-short // (line * rows * 128)) * 128
            if more_rows * cols < more_cols * rows:
                own = padded(own, rows + more_rows, cols)
            else:
                own = padded(own, rows, cols + more_cols)
        return column_by_gather(own, rows, cols)

    t_co_own = jnp.concatenate([t_proj[:, : 3 * CO_W], riders], 1)
    t_co_column = column_by_permutes(t_co_own)
    i_co_column = after(column_by_permutes(i_proj[:, : 3 * CO_W]), near_image, near_cot)
    i_out_column, i_rest_column = z_gather(i_out), z_gather(i_proj[:, 3 * CO_W :])
    t_out_column, t_rest_column = z_gather(t_out), z_gather(t_proj[:, 3 * CO_W :])
    first = [Gather(t_co_column, True), Gather(i_co_column, False)]
    for part in first:
        part.second()
    fars = [part.far for part in first]
    second = [
        Gather(after(i_out_column, *fars), True),
        Gather(after(i_rest_column, *fars), False),
    ]
    for part in first:
        part.core()
    t_co, i_co = [part.full(()) for part in first]
    for part in second:
        part.second()

    shard_count = t_co.shape[0] // t_rows
    table = t_co[:, 3 * CO_W :].reshape(shard_count, -1)[:, : flat.shape[0]].astype(F32)
    taken = []
    offset = 0
    for piece in small:
        block = table[:, offset : offset + piece.size].reshape((shard_count,) + piece.shape)
        offset += piece.size
        if piece.ndim == 1:
            taken.append(block.reshape(1, -1))
        else:
            taken.append(block.transpose(1, 0, 2).reshape(piece.shape[0], -1))
    t_wide, t_rows8, t_gains, i_wide, i_rows8, i_gains = taken

    image_rows = pad_pairs(near_image)
    image_up = pad_pairs(near_cot)
    text_co = co_project(text_in, t_co, t_wide[0])
    image_co = co_project(image_rows, i_co, i_wide[0])
    text_context, image_context = co_forward(
        lengths, text_co, image_co, ()
    )
    fars = [part.far for part in second] + [image_context]
    third = [
        Gather(after(t_out_column, *fars), True),
        Gather(after(t_rest_column, *fars), False),
    ]
    for part in second:
        part.core()
    i_outw, i_rest = [part.full(()) for part in second]
    for part in third:
        part.second()

    image_block = image_rows.shape[0]
    image_hidden = i_wide.shape[1] - 2 * CO_W
    zhat1, inv1, low1, triple, attended, zhat2, inv2 = attn_forward(
        False,
        image_block,
        lengths,
        image_context,
        image_rows,
        i_rest,
        i_outw,
        i_rows8,
        i_gains,
        (),
    )
    i_final, low2, active, third_low, hidden_low, second_grad, i_sums2, i_upsum = ffn(
        image_block,
        1024,
        image_hidden,
        zhat2,
        inv2,
        image_up,
        i_rest,
        i_outw,
        i_wide[:, 2 * CO_W :],
        i_rows8,
        i_gains,
        (),
    )
    image_final = over_x(unpad_pairs(i_final).astype(BF))
    second_low, triple_low, i_first, first_low, i_ctx, i_sums1 = attn_backward(
        False, image_block, lengths, second_grad, triple, zhat1, inv1, i_rest, i_outw, i_gains, ()
    )
    i_rest_sum = Scatter(
        cols_grad(shard_count, True, [(low1, triple_low), (low2, hidden_low)], 512), True
    )
    i_out_sum = Scatter(
        rows_grad(
            shard_count, False,
            [(image_context, first_low), (attended, second_low), (active, third_low)],
            256,
        ),
        False,
    )

    for part in third:
        part.core()
    t_outw, t_rest = [part.full([i_first]) for part in third]

    text_block = 256
    text_hidden = t_wide.shape[1] - 2 * CO_W
    zhat1, inv1, low1, triple, attended, zhat2, inv2 = attn_forward(
        True,
        2 * text_block,
        lengths,
        text_context,
        text_in,
        t_rest,
        t_outw,
        t_rows8,
        t_gains,
        [i_rest_sum.keep, i_out_sum.keep, image_final],
    )
    i_rest_sum.link()
    i_out_sum.link()
    t_final, low2, active, third_low, hidden_low, second_grad, t_sums2, t_upsum = ffn(
        text_block,
        768,
        text_hidden,
        zhat2,
        inv2,
        text_cot,
        t_rest,
        t_outw,
        t_wide[:, 2 * CO_W :],
        t_rows8,
        t_gains,
        [i_rest_sum.send, i_out_sum.send],
    )
    i_out_sum.came = after(i_out_sum.came, second_grad)
    i_out_sum.link()
    second_low, triple_low, t_first, first_low, t_ctx, t_sums1 = attn_backward(
        True,
        text_block,
        lengths,
        second_grad,
        triple,
        zhat1,
        inv1,
        t_rest,
        t_outw,
        t_gains,
        [i_out_sum.send],
    )
    i_rest_sum.came = after(i_rest_sum.came, t_ctx)
    i_out_sum.came = after(i_out_sum.came, t_ctx)
    i_rest_sum.link()
    i_out_sum.column()
    t_rest_sum = Scatter(
        cols_grad(shard_count, False, [(low1, triple_low), (low2, hidden_low)], 768, None, [i_rest_sum.send, i_out_sum.send]), False
    )
    t_out_sum = Scatter(
        rows_grad(
            shard_count, True,
            [(text_context, first_low), (attended, second_low), (active, third_low)],
            256,
            [t_rest_sum.keep],
        ),
        True,
    )

    t_rest_sum.link()
    i_rest_sum.came = after(i_rest_sum.came, t_out_sum.keep)
    i_rest_sum.column()

    t_co_grad, i_co_grad, t_co_sum, i_co_sum = co_backward(
        lengths, text_co, image_co, t_ctx, i_ctx, [t_out_sum.keep, t_rest_sum.send]
    )
    t_out_sum.came = after(t_out_sum.came, t_rest_sum.send)
    t_out_sum.link()

    def small_grads(sums1, sums2, up_sum, co_sum):
        wide = jnp.concatenate([co_sum[0, :CO_W], co_sum[0, 2 * CO_W :], up_sum[0]])
        rows8 = jnp.stack(
            [sums1[2], sums1[1], sums1[3], sums1[4], sums2[5], sums2[4], sums2[2], sums2[1]]
        )
        return wide, rows8, jnp.stack([sums1[0], sums2[3], sums2[0]])

    pieces = small_grads(t_sums1, t_sums2, t_upsum, t_co_sum) + small_grads(
        i_sums1, i_sums2, i_upsum, i_co_sum
    )
    packed = []
    for piece in pieces:
        if piece.ndim == 1:
            packed.append(piece.reshape(shard_count, -1))
        else:
            packed.append(
                piece.reshape(piece.shape[0], shard_count, -1)
                .transpose(1, 0, 2)
                .reshape(shard_count, -1)
            )
    packed = jnp.concatenate(packed, 1)
    count = packed.shape[1]
    packed = jnp.pad(packed, ((0, 0), (0, extra * t_rows - count))).reshape(-1, extra)

    i_co_sums = Scatter(
        cols_grad(
            shard_count, True,
            [(image_rows, i_co_grad)],
            512,
            deps=[t_rest_sum.send, t_out_sum.send],
        ),
        True,
    )
    t_co_sums = Scatter(
        cols_grad(shard_count, False, [(text_in, t_co_grad)], 768, packed, [i_co_sums.keep]), False
    )
    i_co_sums.link()
    t_co_sums.came = after(t_co_sums.came, i_co_sums.send)
    t_co_sums.link()
    image_grad = after(i_first, i_co_sums.send) + dot_nt(i_co_grad, i_co)
    image_grad = over_x(unpad_pairs(image_grad).astype(BF)).astype(F32)
    text_grad = after(t_first, t_co_sums.send) + dot_nt(t_co_grad, t_co[:, : 3 * CO_W])
    t_rest_sum.link()
    t_out_sum.link()
    t_out_sum.came = after(t_out_sum.came, t_co_sums.send)
    t_rest_sum.column()
    t_out_sum.column()
    i_co_sums.link()
    t_co_sums.link()
    i_co_sums.column_by_permutes()
    t_co_sums.column_by_permutes()
    image_final = image_final.astype(F32)
    t_cog = t_co_sums.total()

    mine = t_cog[:, 3 * CO_W :].reshape(-1)
    outs = []
    offset = 0
    for piece in small:
        outs.append(mine[offset : offset + piece.size].reshape(piece.shape))
        offset += piece.size
    t_wide_g, t_rows_g, t_gain_g, i_wide_g, i_rows_g, i_gain_g = outs
    return (
        t_final,
        image_final,
        text_grad,
        image_grad,
        jnp.concatenate([t_cog[:, : 3 * CO_W], t_rest_sum.total()], 1),
        t_out_sum.total(),
        t_wide_g,
        t_rows_g,
        t_gain_g,
        jnp.concatenate([i_co_sums.total(), i_rest_sum.total()], 1),
        i_out_sum.total(),
        i_wide_g,
        i_rows_g,
        i_gain_g,
    )


def solution(mesh):
    both = ("stream", "dp")
    rows, cols, flat = P(both, None), P(None, both), P(both)
    weights = (rows, rows, flat, cols, cols)
    return jax.shard_map(
        shards,
        mesh=mesh,
        in_specs=(rows, rows, flat) + weights + weights + (rows, rows),
        out_specs=(rows, rows, rows, rows) + weights + weights,
        check_vma=False,
    )
```

```python
import functools

import jax
import jax.numpy as jnp
from jax import lax
from jax.experimental import pallas as pl
from jax.experimental.pallas import tpu as pltpu
from jax.sharding import PartitionSpec as P

CO_W = 1024
HEADS_T = 12
HEADS_I = 8
CO_HEADS = 8
CAP = 128
REGIONS = 36
SLOTS = 48

epsilon = 1e-05
negative = -1e30
BF = jnp.bfloat16
F32 = jnp.float32
VMEM_LIMIT = 60 * 1024 * 1024
HALF_ROOT = 0.7071067811865476
INV_ROOT = 0.3989422804014327
ANY = pl.BlockSpec(memory_space=pl.ANY)
SMEM = pl.BlockSpec(memory_space=pltpu.SMEM)


def dot_nn(a, b):
    return lax.dot_general(a, b, (((1,), (0,)), ((), ())), preferred_element_type=F32)


def dot_nt(a, b):
    return lax.dot_general(a, b, (((1,), (1,)), ((), ())), preferred_element_type=F32)


def dot_tn(a, b):
    return lax.dot_general(a, b, (((0,), (0,)), ((), ())), preferred_element_type=F32)


def params():
    return pltpu.CompilerParams(vmem_limit_bytes=VMEM_LIMIT)


def call(kernel, deps, operands, in_specs, **kwargs):
    count = len(operands)

    def body(*refs):
        kernel(*refs[:count], *refs[count + len(deps) :])

    return pl.pallas_call(
        body,
        in_specs=in_specs + [ANY] * len(deps),
        compiler_params=params(),
        **kwargs,
    )(*operands, *deps)


def cost(gmacs, mbytes):
    return pl.CostEstimate(
        flops=int(2e9 * gmacs), bytes_accessed=int(1e6 * mbytes), transcendentals=0
    )


def dp_parts():
    total = lax.axis_size("dp")
    index = lax.axis_index("dp")
    return total // 4, index // 4, (index // 2) % 2, index % 2


def over_core(block):
    total = lax.axis_size("dp")
    return lax.ppermute(block, "dp", [(d, d ^ 1) for d in range(total)])


def over_y(block):
    total = lax.axis_size("dp")
    return lax.ppermute(block, "dp", [(d, d ^ 2) for d in range(total)])


def over_x(block):
    total = lax.axis_size("stream")
    return lax.ppermute(block, "stream", [(d, d ^ 1) for d in range(total)])


def over_z(block, shift):
    total = lax.axis_size("dp")
    return lax.ppermute(block, "dp", [(d, (d + 4 * shift) % total) for d in range(total)])


def pick(buffer, position, axis):
    return lax.dynamic_index_in_dim(buffer, position, axis, keepdims=False)


def place_kernel(blocks, table_ref, *refs):
    count = (len(refs) - 3) // 2
    pieces, out_ref = refs[:count], refs[count]
    held, in_sems, out_sems = refs[count + 1 : 2 * count + 1], refs[2 * count + 1], refs[2 * count + 2]
    loads, stores = [], []
    for number in range(count * blocks):
        piece, block = number // blocks, number % blocks
        x, y, c = [table_ref[3 * number + i] for i in range(3)]
        loads.append(
            pltpu.make_async_copy(pieces[piece].at[block], held[piece].at[block], in_sems.at[number])
        )
        stores.append(
            pltpu.make_async_copy(
                held[piece].at[block], out_ref.at[x, :, y, c], out_sems.at[number]
            )
        )
    for load in loads:
        load.start()
    for load, store in zip(loads, stores):
        load.wait()
        store.start()
    for store in stores:
        store.wait()


def place(pieces, table, deps):
    blocks, nz, rows, cols = pieces[0].shape
    size = 4 * len(pieces) * pieces[0].size
    return call(
        functools.partial(place_kernel, blocks),
        deps,
        (table, *pieces),
        [SMEM] + [ANY] * len(pieces),
        out_specs=ANY,
        out_shape=jax.ShapeDtypeStruct((2, nz, 2, 2, rows, cols), pieces[0].dtype),
        scratch_shapes=[pltpu.VMEM(piece.shape, piece.dtype) for piece in pieces]
        + [pltpu.SemaphoreType.DMA((len(pieces) * blocks,))] * 2,
        cost_estimate=pl.CostEstimate(flops=0, bytes_accessed=size, transcendentals=0),
    )


def table_of(rows):
    return jnp.stack([jnp.asarray(v, jnp.int32) for row in rows for v in row])


def z_groups():
    total = lax.axis_size("dp")
    return [[first + 4 * k for k in range(total // 4)] for first in range(4)]


def after_kernel(*refs):
    pass


def after(block, *earlier):
    return pl.pallas_call(
        after_kernel,
        in_specs=[ANY] * (1 + len(earlier)),
        out_specs=ANY,
        out_shape=jax.ShapeDtypeStruct(block.shape, block.dtype),
        input_output_aliases={0: 0},
        compiler_params=params(),
        cost_estimate=pl.CostEstimate(flops=0, bytes_accessed=0, transcendentals=0),
    )(block, *earlier)


def column_by_permutes(own):
    nz, z, _, _ = dp_parts()
    came = jnp.stack([own] + [over_z(own, shift) for shift in range(1, nz)])
    turned = jnp.concatenate([came[::-1]] * 2)
    return lax.dynamic_slice_in_dim(turned, nz - 1 - z, nz, 0)


def column_by_gather(own, rows, cols):
    full = lax.all_gather(own, "dp", axis_index_groups=z_groups(), axis=0)
    return full[:, :rows, :cols]


class Gather:
    def __init__(self, column, y_first):
        self.column = column
        self.links = (over_y, over_x) if y_first else (over_x, over_y)
        self.y_first = y_first
        self.over = self.links[0](column)

    def second(self):
        self.pair = jnp.stack([self.column, self.over])
        self.far = self.links[1](self.pair)

    def core(self):
        self.others = [over_core(self.pair), over_core(self.far)]

    def full(self, deps):
        _, _, y, c = dp_parts()
        x = lax.axis_index("stream")
        table = []
        for core in (0, 1):
            for outer in (0, 1):
                for inner in (0, 1):
                    dx, dy = (outer, inner) if self.y_first else (inner, outer)
                    table.append((x ^ dx, y ^ dy, c ^ core))
        whole = place([self.pair, self.far] + self.others, table_of(table), deps)
        return whole.reshape(-1, whole.shape[-1])


def add_low(kept, came):
    return (kept.astype(F32) + came.astype(F32)).astype(BF)


class Scatter:
    def __init__(self, halves, y_first):
        self.send, self.keep = halves
        self.came = over_core(self.send)
        self.axes = ("y", "x") if y_first else ("x", "y")

    def link(self):
        axis, self.axes = self.axes[0], self.axes[1:]
        at = dp_parts()[2] if axis == "y" else lax.axis_index("stream")
        self.send = add_low(pick(self.keep, 1 - at, 0), pick(self.came, 1 - at, 0))
        self.keep = add_low(pick(self.keep, at, 0), pick(self.came, at, 0))
        self.came = over_y(self.send) if axis == "y" else over_x(self.send)

    def column_by_permutes(self):
        nz, z, _, _ = dp_parts()
        self.send = add_low(self.keep, self.came)
        self.sum = pick(self.send, z, 0).astype(F32)
        for shift in range(1, nz):
            came = over_z(pick(self.send, (z + shift) % nz, 0), shift)
            self.sum = self.sum + came.astype(F32)

    def column(self):
        self.send = add_low(self.keep, self.came)
        self.sum = lax.psum_scatter(
            self.send.reshape(-1, self.send.shape[-1]),
            "dp",
            axis_index_groups=z_groups(),
            scatter_dimension=0,
            tiled=True,
        )

    def total(self):
        return self.sum.astype(F32)


def store_halves(y_first, core_ref, send_ref, keep_ref, block, at):
    columns, rows = send_ref.shape[:2]
    nz = columns // 4

    def store(even_ref, odd_ref):
        for number in range(columns):
            x, z, y = number // (2 * nz), number // 2 % nz, number % 2
            spot = (y * 2 + x if y_first else x * 2 + y) * nz + z
            start = 2 * number * rows
            even_ref[spot, :, at] = block[start : start + rows].astype(BF)
            odd_ref[spot, :, at] = block[start + rows : start + 2 * rows].astype(BF)

    @pl.when(core_ref[0] == 0)
    def _():
        store(keep_ref, send_ref)

    @pl.when(core_ref[0] == 1)
    def _():
        store(send_ref, keep_ref)


def cols_grad_kernel(y_first, counts, tile, has_riders, core_ref, *refs):
    segments = len(counts)
    lhs, ups = refs[:segments], refs[segments : 2 * segments]
    riders = refs[2 * segments] if has_riders else None
    send_ref, keep_ref = refs[2 * segments + has_riders : 2 * segments + has_riders + 2]
    turned = refs[2 * segments + has_riders + 2 :]
    step = pl.program_id(0)

    @pl.when(step == 0)
    def _():
        for flat, kept in zip(lhs, turned):
            kept[...] = flat[...].T

    first = 0
    for count, kept, up in zip(counts, turned, ups):

        @pl.when((step >= first) & (step < first + count))
        def _(kept=kept, up=up):
            at = pl.ds(pl.multiple_of(step * tile, 128), tile) if has_riders else slice(None)
            store_halves(y_first, core_ref, send_ref, keep_ref, dot_nn(kept[...], up[...]), at)

        first += count
    if has_riders:

        @pl.when(step == 0)
        def _():
            width = riders.shape[1]
            start = sum(counts) * tile
            store_halves(y_first, core_ref, send_ref, keep_ref, riders[...], slice(start, start + width))


def half_shapes(shards, rows, cols):
    return [jax.ShapeDtypeStruct((shards // 2, rows, cols), BF)] * 2


def cols_grad(shards, y_first, segments, tile, riders=None, deps=()):
    counts = [up.shape[1] // tile for _, up in segments]
    width = segments[0][0].shape[1]
    length = segments[0][0].shape[0]
    rows = width // shards
    total = sum(counts) * tile + (0 if riders is None else riders.shape[1])
    starts = [sum(counts[:i]) for i in range(len(counts))]

    def up_spec(start, count):
        return pl.BlockSpec((length, tile), lambda j: (0, jnp.clip(j - start, 0, count - 1)))

    whole = [pl.BlockSpec(lhs.shape, lambda j: (0, 0)) for lhs, _ in segments]
    tiles = [up_spec(start, count) for start, count in zip(starts, counts)]
    extra = [] if riders is None else [riders]
    core = jnp.reshape(dp_parts()[3], (1,)).astype(jnp.int32)
    if riders is None:
        out = pl.BlockSpec((shards // 2, rows, tile), lambda j: (0, 0, j))
    else:
        out = pl.BlockSpec((shards // 2, rows, total), lambda j: (0, 0, 0))
    halves = call(
        functools.partial(cols_grad_kernel, y_first, counts, tile, len(extra)),
        deps,
        (core,) + tuple(lhs for lhs, _ in segments) + tuple(up for _, up in segments) + tuple(extra),
        [SMEM] + whole + tiles + [pl.BlockSpec(block.shape, lambda j: (0, 0)) for block in extra],
        grid=(sum(counts),),
        out_specs=[out, out],
        out_shape=half_shapes(shards, rows, total),
        scratch_shapes=[pltpu.VMEM((width, length), BF) for _ in segments],
        cost_estimate=cost(1.3e-9 * length * width * total, 20),
    )
    return [half.reshape(2, 2, -1, rows, total) for half in halves]


def rows_grad_kernel(y_first, segments, tile, core_ref, *refs):
    lhs, ups = refs[:segments], refs[segments : 2 * segments]
    send_ref, keep_ref, total = refs[2 * segments : 2 * segments + 3]
    turned = refs[2 * segments + 3 :]

    @pl.when(pl.program_id(0) == 0)
    def _():
        for flat, kept in zip(lhs, turned):
            kept[...] = flat[...].T

    start = 0
    for kept, up in zip(turned, ups):
        for row in range(0, kept.shape[0], 256):
            total[start + row : start + row + 256] = dot_nn(kept[row : row + 256], up[...])
        start += kept.shape[0]
    store_halves(y_first, core_ref, send_ref, keep_ref, total, slice(None))


def rows_grad(shards, y_first, segments, tile, deps=()):
    length = segments[0][0].shape[0]
    height = sum(lhs.shape[1] for lhs, _ in segments)
    width = segments[0][1].shape[1]
    rows = height // shards
    core = jnp.reshape(dp_parts()[3], (1,)).astype(jnp.int32)
    out = pl.BlockSpec((shards // 2, rows, tile), lambda j: (0, 0, j))
    halves = call(
        functools.partial(rows_grad_kernel, y_first, len(segments), tile),
        deps,
        (core,) + tuple(lhs for lhs, _ in segments) + tuple(up for _, up in segments),
        [SMEM]
        + [
            pl.BlockSpec(lhs.shape, lambda j: (0, 0), pipeline_mode=pl.Buffered(1))
            for lhs, _ in segments
        ]
        + [pl.BlockSpec((length, tile), lambda j: (0, j)) for _ in segments],
        grid=(width // tile,),
        out_specs=[out, out],
        out_shape=half_shapes(shards, rows, width),
        scratch_shapes=[pltpu.VMEM((height, tile), F32)]
        + [pltpu.VMEM((lhs.shape[1], length), BF) for lhs, _ in segments],
        cost_estimate=cost(1.3e-9 * length * height * width, 20),
    )
    return [half.reshape(2, 2, -1, rows, width) for half in halves]


def softmax_rows(scores):
    high = jnp.max(scores, -1, keepdims=True)
    exponent = jnp.exp(scores - high)
    return exponent * (1.0 / jnp.sum(exponent, -1, keepdims=True))


def norm_rows(pre_norm):
    centered = pre_norm - jnp.mean(pre_norm, -1, keepdims=True)
    inverse = lax.rsqrt(jnp.mean(centered * centered, -1, keepdims=True) + epsilon)
    return centered * inverse, inverse


def norm_back_rows(upstream, gain, normed, inverse):
    scaled = upstream * gain
    return inverse * (
        scaled
        - jnp.mean(scaled, -1, keepdims=True)
        - normed * jnp.mean(scaled * normed, -1, keepdims=True)
    )


def col_sum(block):
    return jnp.sum(block, 0, keepdims=True)


def key_mask(shape, count):
    return jnp.where(lax.broadcasted_iota(jnp.int32, shape, 1) < count, 0.0, negative)


def attend_all(units, factor):
    scores = [dot_nt(q, k) * factor + mask for q, k, _, mask in units]
    probs = [softmax_rows(score).astype(BF) for score in scores]
    return [dot_nn(prob, unit[2]) for prob, unit in zip(probs, units)]


def attend_back_all(units, upstreams, factor):
    scores = [dot_nt(q, k) * factor + mask for q, k, _, mask in units]
    raised = [dot_nt(up, unit[2]) for up, unit in zip(upstreams, units)]
    probs = [softmax_rows(score) for score in scores]
    values_grad = [dot_tn(prob.astype(BF), up) for prob, up in zip(probs, upstreams)]
    rounded = [
        (prob * (grad - jnp.sum(prob * grad, -1, keepdims=True)) * factor).astype(BF)
        for prob, grad in zip(probs, raised)
    ]
    queries_grad = [dot_nn(low, unit[1]) for low, unit in zip(rounded, units)]
    keys_grad = [dot_tn(low, unit[0]) for low, unit in zip(rounded, units)]
    return list(zip(queries_grad, keys_grad, values_grad))


def co_forward_kernel(len_ref, text_ref, image_ref, text_out, image_out):
    step = pl.program_id(0)
    factor = (CO_W // CO_HEADS) ** -0.5
    region_mask = key_mask((1, SLOTS), REGIONS)
    text_mask = key_mask((1, CAP), len_ref[step])
    units, places = [], []
    for head in range(CO_HEADS):
        at = [slice(part * CO_W + head * 128, part * CO_W + head * 128 + 128) for part in range(3)]
        tq, tk, tv = [text_ref[:, where] for where in at]
        iq, ik, iv = [image_ref[:, where] for where in at]
        units += [(tq, ik, iv, region_mask), (iq, tk, tv, text_mask)]
        places += [(text_out, at[0]), (image_out, at[0])]
    for (out_ref, where), context in zip(places, attend_all(units, factor)):
        out_ref[:, where] = context.astype(BF)


def co_forward(lengths, text_co, image_co, deps):
    pairs = lengths.shape[0]
    return call(
        co_forward_kernel,
        deps,
        (lengths, text_co, image_co,),
        [
            SMEM,
            pl.BlockSpec((CAP, 3 * CO_W), lambda i: (i, 0)),
            pl.BlockSpec((SLOTS, 3 * CO_W), lambda i: (i, 0)),
        ],
        grid=(pairs,),
        out_specs=[
            pl.BlockSpec((CAP, CO_W), lambda i: (i, 0)),
            pl.BlockSpec((SLOTS, CO_W), lambda i: (i, 0)),
        ],
        out_shape=[
            jax.ShapeDtypeStruct((pairs * CAP, CO_W), BF),
            jax.ShapeDtypeStruct((pairs * SLOTS, CO_W), BF),
        ],
        cost_estimate=cost(2 * lengths.shape[0] * 0.4, 8),
    )


def co_backward_kernel(
    len_ref, text_ref, image_ref, text_up, image_up, text_out, image_out, text_sum, image_sum
):
    step = pl.program_id(0)
    factor = (CO_W // CO_HEADS) ** -0.5
    region_mask = key_mask((1, SLOTS), REGIONS)
    text_mask = key_mask((1, CAP), len_ref[step])

    @pl.when(step == 0)
    def _():
        text_sum[...] = jnp.zeros_like(text_sum)
        image_sum[...] = jnp.zeros_like(image_sum)

    def store(out_ref, sum_ref, where, grad):
        low = grad.astype(BF)
        out_ref[:, where] = low
        sum_ref[:, where] += col_sum(low.astype(F32))

    units, ups, places = [], [], []
    for head in range(CO_HEADS):
        at = [slice(part * CO_W + head * 128, part * CO_W + head * 128 + 128) for part in range(3)]
        tq, tk, tv = [text_ref[:, where] for where in at]
        iq, ik, iv = [image_ref[:, where] for where in at]
        units += [(tq, ik, iv, region_mask), (iq, tk, tv, text_mask)]
        ups += [text_up[:, at[0]], image_up[:, at[0]]]
        places.append(at)
    grads = attend_back_all(units, ups, factor)
    for head, at in enumerate(places):
        dtq, dik, div = grads[2 * head]
        diq, dtk, dtv = grads[2 * head + 1]
        for where, grad in zip(at, (dtq, dtk, dtv)):
            store(text_out, text_sum, where, grad)
        for where, grad in zip(at, (diq, dik, div)):
            store(image_out, image_sum, where, grad)


def co_backward(lengths, text_co, image_co, text_up, image_up, deps):
    pairs = lengths.shape[0]
    wide = 3 * CO_W
    return call(
        co_backward_kernel,
        deps,
        (lengths, text_co, image_co, text_up, image_up,),
        [
            SMEM,
            pl.BlockSpec((CAP, wide), lambda i: (i, 0)),
            pl.BlockSpec((SLOTS, wide), lambda i: (i, 0)),
            pl.BlockSpec((CAP, CO_W), lambda i: (i, 0)),
            pl.BlockSpec((SLOTS, CO_W), lambda i: (i, 0)),
        ],
        grid=(pairs,),
        out_specs=[
            pl.BlockSpec((CAP, wide), lambda i: (i, 0)),
            pl.BlockSpec((SLOTS, wide), lambda i: (i, 0)),
            pl.BlockSpec((1, wide), lambda i: (0, 0)),
            pl.BlockSpec((1, wide), lambda i: (0, 0)),
        ],
        out_shape=[
            jax.ShapeDtypeStruct((pairs * CAP, wide), BF),
            jax.ShapeDtypeStruct((pairs * SLOTS, wide), BF),
            jax.ShapeDtypeStruct((1, wide), F32),
            jax.ShapeDtypeStruct((1, wide), F32),
        ],
        cost_estimate=cost(2 * lengths.shape[0] * 0.5, 20),
    )


def fetch(step, copies):
    @pl.when(step == 0)
    def _():
        for copy in copies:
            copy.start()

    def arrived(number):
        @pl.when(step == 0)
        def _():
            copies[number].wait()

    return arrived


def text_units(len_ref, step, pair_count):
    for pair in range(pair_count):
        mask = key_mask((1, CAP), len_ref[step * pair_count + pair])
        for block in range(HEADS_T // 2):
            yield slice(pair * CAP, pair * CAP + CAP), block * 128, mask


def image_mask():
    shape = (2 * SLOTS, 2 * SLOTS)
    row = lax.broadcasted_iota(jnp.int32, shape, 0)
    col = lax.broadcasted_iota(jnp.int32, shape, 1)
    same = (row >= SLOTS) == (col >= SLOTS)
    local = jnp.where(col >= SLOTS, col - SLOTS, col)
    return jnp.where(same & (local < REGIONS), 0.0, negative)


def image_units(rows):
    mask = image_mask()
    return [
        (slice(start, start + 2 * SLOTS), head * 128, mask)
        for start in range(0, rows, 2 * SLOTS)
        for head in range(HEADS_I)
    ]


def halves(block):
    low = lax.broadcasted_iota(jnp.int32, block.shape, 1) < 64
    zero = jnp.zeros_like(block)
    return jnp.concatenate([jnp.where(low, block, zero), jnp.where(low, zero, block)], 0)


def unhalve(stacked):
    rows = stacked.shape[0] // 2
    low = lax.broadcasted_iota(jnp.int32, (rows, stacked.shape[1]), 1) < 64
    return jnp.where(low, stacked[:rows], stacked[rows:])


def attn_forward_kernel(
    is_text,
    down_at,
    len_ref,
    context_ref,
    input_ref,
    proj_ref,
    out_w_ref,
    bias_ref,
    gain_ref,
    zhat1_ref,
    inv1_ref,
    low1_ref,
    triple_ref,
    attended_ref,
    zhat2_ref,
    inv2_ref,
    wco,
    wqkv,
    wo,
    sems,
):
    step = pl.program_id(0)
    width = input_ref.shape[1]
    rows = input_ref.shape[0]
    arrived = fetch(
        step,
        [
            pltpu.make_async_copy(out_w_ref.at[pl.ds(0, CO_W)], wco, sems.at[0]),
            pltpu.make_async_copy(proj_ref.at[:, pl.ds(0, 3 * width)], wqkv, sems.at[1]),
            pltpu.make_async_copy(out_w_ref.at[pl.ds(CO_W, width)], wo, sems.at[2]),
        ],
    )
    arrived(0)
    normed, inverse = norm_rows(
        input_ref[...].astype(F32) + dot_nn(context_ref[...], wco[...]) + bias_ref[0:1]
    )
    zhat1_ref[...] = normed
    inv1_ref[...] = inverse
    first = normed * gain_ref[0:1] + bias_ref[1:2]
    first_low = first.astype(BF)
    low1_ref[...] = first_low
    arrived(1)
    for part in range(3):
        at = slice(part * width, part * width + width)
        piece = dot_nn(first_low, wqkv[:, at])
        if part == 0:
            piece = piece + bias_ref[2:3]
        if part == 2:
            piece = piece + bias_ref[3:4]
        triple_ref[:, at] = piece.astype(BF)

    def lanes(part, lane):
        return slice(part * width + lane, part * width + lane + 128)

    if is_text:
        places = list(text_units(len_ref, step, rows // CAP))
        factor = (width // HEADS_T) ** -0.5
    else:
        places = image_units(rows)
        factor = (width // HEADS_I) ** -0.5
    units = []
    for where, lane, mask in places:
        q, k, v = [triple_ref[where, lanes(part, lane)] for part in range(3)]
        units.append((halves(q) if is_text else q, k, v, mask))
    for (where, lane, _), context in zip(places, attend_all(units, factor)):
        context = unhalve(context) if is_text else context
        attended_ref[where, lane : lane + 128] = context.astype(BF)
    arrived(2)
    normed, inverse = norm_rows(first + dot_nn(attended_ref[...], wo[...]) + bias_ref[4:5])
    zhat2_ref[...] = normed
    inv2_ref[...] = inverse


def row_spec(rows, cols):
    return pl.BlockSpec((rows, cols), lambda i: (i, 0))


def whole_spec(rows, cols):
    return pl.BlockSpec((rows, cols), lambda i: (0, 0))


def attn_forward(is_text, block, lengths, context, inputs, proj, out_w, bias, gain, deps):
    rows, width = inputs.shape
    shape = jax.ShapeDtypeStruct
    return call(
        functools.partial(attn_forward_kernel, is_text, CO_W + width),
        deps,
        (lengths, context, inputs, proj, out_w, bias, gain,),
        [
            SMEM,
            row_spec(block, CO_W),
            row_spec(block, width),
            ANY,
            ANY,
            whole_spec(8, width),
            whole_spec(3, width),
        ],
        grid=(rows // block,),
        out_specs=[
            row_spec(block, width),
            row_spec(block, 1),
            row_spec(block, width),
            row_spec(block, 3 * width),
            row_spec(block, width),
            row_spec(block, width),
            row_spec(block, 1),
        ],
        out_shape=[
            shape((rows, width), F32),
            shape((rows, 1), F32),
            shape((rows, width), BF),
            shape((rows, 3 * width), BF),
            shape((rows, width), BF),
            shape((rows, width), F32),
            shape((rows, 1), F32),
        ],
        scratch_shapes=[
            pltpu.VMEM((CO_W, width), BF),
            pltpu.VMEM((width, 3 * width), BF),
            pltpu.VMEM((width, width), BF),
            pltpu.SemaphoreType.DMA((3,)),
        ],
        cost_estimate=cost(rows * width * width * 1.6e-8, 40),
    )


def ffn_kernel(
    chunk,
    zhat2_ref,
    inv2_ref,
    cot_ref,
    proj_ref,
    out_w_ref,
    up_bias_ref,
    bias_ref,
    gain_ref,
    final_ref,
    low2_ref,
    active_ref,
    third_low_ref,
    hidden_low_ref,
    second_grad_ref,
    sums_ref,
    up_sum_ref,
    wup,
    wdown,
    slope,
    sems,
):
    step = pl.program_id(0)
    width = zhat2_ref.shape[1]
    hidden = wup.shape[1]
    arrived = fetch(
        step,
        [
            pltpu.make_async_copy(proj_ref.at[:, pl.ds(3 * width, hidden)], wup, sems.at[0]),
            pltpu.make_async_copy(out_w_ref.at[pl.ds(CO_W + width, hidden)], wdown, sems.at[1]),
        ],
    )

    @pl.when(step == 0)
    def _():
        sums_ref[...] = jnp.zeros_like(sums_ref)
        up_sum_ref[...] = jnp.zeros_like(up_sum_ref)

    arrived(0)
    arrived(1)
    second = zhat2_ref[...] * gain_ref[1:2] + bias_ref[5:6]
    second_low = second.astype(BF)
    low2_ref[...] = second_low
    total = second + bias_ref[6:7]
    for start in range(0, hidden, chunk):
        at = slice(start, start + chunk)
        u = dot_nn(second_low, wup[:, at]) + up_bias_ref[:, at]
        phi = 0.5 + 0.5 * lax.erf(u * HALF_ROOT)
        active = (u * phi).astype(BF)
        active_ref[:, at] = active
        slope[:, at] = phi + (u * INV_ROOT) * jnp.exp(-0.5 * u * u)
        total = total + dot_nn(active, wdown[at])
    normed, inverse = norm_rows(total)
    final_ref[...] = normed * gain_ref[2:3] + bias_ref[7:8]
    upstream = cot_ref[...].astype(F32)
    third = norm_back_rows(upstream, gain_ref[2:3], normed, inverse)
    third_low = third.astype(BF)
    third_low_ref[...] = third_low
    sums_ref[0:1] += col_sum(upstream * normed)
    sums_ref[1:2] += col_sum(upstream)
    sums_ref[2:3] += col_sum(third)
    back = third
    for start in range(0, hidden, chunk):
        at = slice(start, start + chunk)
        grad = dot_nt(third_low, wdown[at]) * slope[:, at]
        up_sum_ref[:, at] += col_sum(grad)
        grad_low = grad.astype(BF)
        hidden_low_ref[:, at] = grad_low
        back = back + dot_nt(grad_low, wup[:, at])
    zhat2 = zhat2_ref[...]
    second_grad = norm_back_rows(back, gain_ref[1:2], zhat2, inv2_ref[...])
    second_grad_ref[...] = second_grad
    sums_ref[3:4] += col_sum(back * zhat2)
    sums_ref[4:5] += col_sum(back)
    sums_ref[5:6] += col_sum(second_grad)


def ffn(block, chunk, hidden, zhat2, inv2, cot, proj, out_w, up_bias, bias, gain, deps):
    rows, width = zhat2.shape
    shape = jax.ShapeDtypeStruct
    return call(
        functools.partial(ffn_kernel, chunk),
        deps,
        (zhat2, inv2, cot, proj, out_w, up_bias, bias, gain,),
        [
            row_spec(block, width),
            row_spec(block, 1),
            row_spec(block, width),
            ANY,
            ANY,
            whole_spec(1, hidden),
            whole_spec(8, width),
            whole_spec(3, width),
        ],
        grid=(rows // block,),
        out_specs=[
            row_spec(block, width),
            row_spec(block, width),
            row_spec(block, hidden),
            row_spec(block, width),
            row_spec(block, hidden),
            row_spec(block, width),
            whole_spec(8, width),
            whole_spec(1, hidden),
        ],
        out_shape=[
            shape((rows, width), F32),
            shape((rows, width), BF),
            shape((rows, hidden), BF),
            shape((rows, width), BF),
            shape((rows, hidden), BF),
            shape((rows, width), F32),
            shape((8, width), F32),
            shape((1, hidden), F32),
        ],
        scratch_shapes=[
            pltpu.VMEM((width, hidden), BF),
            pltpu.VMEM((hidden, width), BF),
            pltpu.VMEM((block, hidden), F32),
            pltpu.SemaphoreType.DMA((2,)),
        ],
        cost_estimate=cost(rows * width * hidden * 6.5e-9, 40),
    )


def attn_backward_kernel(
    is_text,
    len_ref,
    second_grad_ref,
    triple_ref,
    zhat1_ref,
    inv1_ref,
    proj_ref,
    out_w_ref,
    gain_ref,
    second_low_ref,
    triple_low_ref,
    first_grad_ref,
    first_low_ref,
    context_low_ref,
    sums_ref,
    wco,
    wqkv,
    wo,
    upstream,
    sems,
):
    step = pl.program_id(0)
    rows, width = second_grad_ref.shape
    arrived = fetch(
        step,
        [
            pltpu.make_async_copy(out_w_ref.at[pl.ds(0, CO_W)], wco, sems.at[0]),
            pltpu.make_async_copy(proj_ref.at[:, pl.ds(0, 3 * width)], wqkv, sems.at[1]),
            pltpu.make_async_copy(out_w_ref.at[pl.ds(CO_W, width)], wo, sems.at[2]),
        ],
    )

    @pl.when(step == 0)
    def _():
        sums_ref[...] = jnp.zeros_like(sums_ref)

    second_low = second_grad_ref[...].astype(BF)
    second_low_ref[...] = second_low
    arrived(2)
    upstream[...] = dot_nt(second_low, wo[...]).astype(BF)

    def lanes(part, lane):
        return slice(part * width + lane, part * width + lane + 128)

    if is_text:
        places = list(text_units(len_ref, step, rows // CAP))
        factor = (width // HEADS_T) ** -0.5
    else:
        places = image_units(rows)
        factor = (width // HEADS_I) ** -0.5
    units, ups = [], []
    for where, lane, mask in places:
        q, k, v = [triple_ref[where, lanes(part, lane)] for part in range(3)]
        up = upstream[where, lane : lane + 128]
        units.append((halves(q) if is_text else q, k, v, mask))
        ups.append(halves(up) if is_text else up)
    for (where, lane, _), grads in zip(places, attend_back_all(units, ups, factor)):
        dq, dk, dv = grads
        for part, grad in enumerate((unhalve(dq) if is_text else dq, dk, dv)):
            triple_low_ref[where, lanes(part, lane)] = grad.astype(BF)
    arrived(1)
    back = second_grad_ref[...]
    for part in range(3):
        at = slice(part * width, part * width + width)
        piece = triple_low_ref[:, at]
        back = back + dot_nt(piece, wqkv[:, at])
        if part != 1:
            row = 3 + part // 2
            sums_ref[row : row + 1] += col_sum(piece.astype(F32))
    zhat1 = zhat1_ref[...]
    first_grad = norm_back_rows(back, gain_ref[0:1], zhat1, inv1_ref[...])
    first_grad_ref[...] = first_grad
    sums_ref[0:1] += col_sum(back * zhat1)
    sums_ref[1:2] += col_sum(back)
    sums_ref[2:3] += col_sum(first_grad)
    first_low = first_grad.astype(BF)
    first_low_ref[...] = first_low
    arrived(0)
    context_low_ref[...] = dot_nt(first_low, wco[...]).astype(BF)


def attn_backward(is_text, block, lengths, second_grad, triple, zhat1, inv1, proj, out_w, gain, deps):
    rows, width = zhat1.shape
    shape = jax.ShapeDtypeStruct
    return call(
        functools.partial(attn_backward_kernel, is_text),
        deps,
        (lengths, second_grad, triple, zhat1, inv1, proj, out_w, gain,),
        [
            SMEM,
            row_spec(block, width),
            row_spec(block, 3 * width),
            row_spec(block, width),
            row_spec(block, 1),
            ANY,
            ANY,
            whole_spec(3, width),
        ],
        grid=(rows // block,),
        out_specs=[
            row_spec(block, width),
            row_spec(block, 3 * width),
            row_spec(block, width),
            row_spec(block, width),
            row_spec(block, CO_W),
            whole_spec(8, width),
        ],
        out_shape=[
            shape((rows, width), BF),
            shape((rows, 3 * width), BF),
            shape((rows, width), F32),
            shape((rows, width), BF),
            shape((rows, CO_W), BF),
            shape((8, width), F32),
        ],
        scratch_shapes=[
            pltpu.VMEM((CO_W, width), BF),
            pltpu.VMEM((width, 3 * width), BF),
            pltpu.VMEM((width, width), BF),
            pltpu.VMEM((block, width), BF),
            pltpu.SemaphoreType.DMA((3,)),
        ],
        cost_estimate=cost(rows * width * width * 1.6e-8, 40),
    )


def co_project(inputs, weight, wide):
    bias = jnp.concatenate([wide[:CO_W], jnp.zeros((CO_W,), F32), wide[CO_W : 2 * CO_W]])
    return (dot_nn(inputs, weight[:, : 3 * CO_W]) + bias).astype(BF)


def pad_pairs(block):
    wide = block.reshape(-1, REGIONS, block.shape[1])
    return jnp.pad(wide, ((0, 0), (0, SLOTS - REGIONS), (0, 0))).reshape(-1, block.shape[1])


def unpad_pairs(block):
    return block.reshape(-1, SLOTS, block.shape[1])[:, :REGIONS].reshape(-1, block.shape[1])


def shards(
    text_in,
    image_in,
    lengths,
    t_proj,
    t_out,
    t_bias_wide,
    t_bias,
    t_gain,
    i_proj,
    i_out,
    i_bias_wide,
    i_bias,
    i_gain,
    text_cot,
    image_cot,
):
    small = (t_bias_wide, t_bias, t_gain, i_bias_wide, i_bias, i_gain)
    flat = jnp.concatenate([piece.reshape(-1) for piece in small])
    t_rows = t_proj.shape[0]
    extra = -(-flat.shape[0] // (t_rows * 128)) * 128
    riders = jnp.pad(flat, (0, extra * t_rows - flat.shape[0])).reshape(t_rows, extra)
    near_image = over_x(image_in)
    near_cot = over_x(image_cot)

    def padded(own, rows, cols):
        return jnp.pad(own, ((0, rows - own.shape[0]), (0, cols - own.shape[1])))

    def z_gather(own):
        rows, cols = own.shape
        short = (1 << 20) - 2 * rows * cols * dp_parts()[0]
        if short > 0:
            line = 2 * dp_parts()[0]
            more_rows = -(-short // (line * cols * 8)) * 8
            more_cols = -(-short // (line * rows * 128)) * 128
            if more_rows * cols < more_cols * rows:
                own = padded(own, rows + more_rows, cols)
            else:
                own = padded(own, rows, cols + more_cols)
        return column_by_gather(own, rows, cols)

    t_co_own = jnp.concatenate([t_proj[:, : 3 * CO_W], riders], 1)
    t_co_column = column_by_permutes(t_co_own)
    i_co_column = after(column_by_permutes(i_proj[:, : 3 * CO_W]), near_image, near_cot)
    i_out_column, i_rest_column = z_gather(i_out), z_gather(i_proj[:, 3 * CO_W :])
    t_out_column, t_rest_column = z_gather(t_out), z_gather(t_proj[:, 3 * CO_W :])
    first = [Gather(t_co_column, True), Gather(i_co_column, False)]
    for part in first:
        part.second()
    fars = [part.far for part in first]
    second = [
        Gather(after(i_out_column, *fars), True),
        Gather(after(i_rest_column, *fars), False),
    ]
    for part in first:
        part.core()
    t_co, i_co = [part.full(()) for part in first]
    for part in second:
        part.second()

    shard_count = t_co.shape[0] // t_rows
    table = t_co[:, 3 * CO_W :].reshape(shard_count, -1)[:, : flat.shape[0]].astype(F32)
    taken = []
    offset = 0
    for piece in small:
        block = table[:, offset : offset + piece.size].reshape((shard_count,) + piece.shape)
        offset += piece.size
        if piece.ndim == 1:
            taken.append(block.reshape(1, -1))
        else:
            taken.append(block.transpose(1, 0, 2).reshape(piece.shape[0], -1))
    t_wide, t_rows8, t_gains, i_wide, i_rows8, i_gains = taken

    image_rows = pad_pairs(near_image)
    image_up = pad_pairs(near_cot)
    text_co = co_project(text_in, t_co, t_wide[0])
    image_co = co_project(image_rows, i_co, i_wide[0])
    text_context, image_context = co_forward(
        lengths, text_co, image_co, ()
    )
    fars = [part.far for part in second] + [image_context]
    third = [
        Gather(after(t_out_column, *fars), True),
        Gather(after(t_rest_column, *fars), False),
    ]
    for part in second:
        part.core()
    i_outw, i_rest = [part.full(()) for part in second]
    for part in third:
        part.second()

    image_block = image_rows.shape[0]
    image_hidden = i_wide.shape[1] - 2 * CO_W
    zhat1, inv1, low1, triple, attended, zhat2, inv2 = attn_forward(
        False,
        image_block,
        lengths,
        image_context,
        image_rows,
        i_rest,
        i_outw,
        i_rows8,
        i_gains,
        (),
    )
    i_final, low2, active, third_low, hidden_low, second_grad, i_sums2, i_upsum = ffn(
        image_block,
        1024,
        image_hidden,
        zhat2,
        inv2,
        image_up,
        i_rest,
        i_outw,
        i_wide[:, 2 * CO_W :],
        i_rows8,
        i_gains,
        (),
    )
    image_final = over_x(unpad_pairs(i_final).astype(BF))
    second_low, triple_low, i_first, first_low, i_ctx, i_sums1 = attn_backward(
        False, image_block, lengths, second_grad, triple, zhat1, inv1, i_rest, i_outw, i_gains, ()
    )
    i_rest_sum = Scatter(
        cols_grad(shard_count, True, [(low1, triple_low), (low2, hidden_low)], 512), True
    )
    i_out_sum = Scatter(
        rows_grad(
            shard_count, False,
            [(image_context, first_low), (attended, second_low), (active, third_low)],
            256,
        ),
        False,
    )

    for part in third:
        part.core()
    t_outw, t_rest = [part.full([i_first]) for part in third]

    text_block = 256
    text_hidden = t_wide.shape[1] - 2 * CO_W
    zhat1, inv1, low1, triple, attended, zhat2, inv2 = attn_forward(
        True,
        2 * text_block,
        lengths,
        text_context,
        text_in,
        t_rest,
        t_outw,
        t_rows8,
        t_gains,
        [i_rest_sum.keep, i_out_sum.keep, image_final],
    )
    i_rest_sum.link()
    i_out_sum.link()
    t_final, low2, active, third_low, hidden_low, second_grad, t_sums2, t_upsum = ffn(
        text_block,
        768,
        text_hidden,
        zhat2,
        inv2,
        text_cot,
        t_rest,
        t_outw,
        t_wide[:, 2 * CO_W :],
        t_rows8,
        t_gains,
        [i_rest_sum.send, i_out_sum.send],
    )
    i_out_sum.came = after(i_out_sum.came, second_grad)
    i_out_sum.link()
    second_low, triple_low, t_first, first_low, t_ctx, t_sums1 = attn_backward(
        True,
        text_block,
        lengths,
        second_grad,
        triple,
        zhat1,
        inv1,
        t_rest,
        t_outw,
        t_gains,
        [i_out_sum.send],
    )
    i_rest_sum.came = after(i_rest_sum.came, t_ctx)
    i_out_sum.came = after(i_out_sum.came, t_ctx)
    i_rest_sum.link()
    i_out_sum.column()
    t_rest_sum = Scatter(
        cols_grad(shard_count, False, [(low1, triple_low), (low2, hidden_low)], 768, None, [i_rest_sum.send, i_out_sum.send]), False
    )
    t_out_sum = Scatter(
        rows_grad(
            shard_count, True,
            [(text_context, first_low), (attended, second_low), (active, third_low)],
            256,
            [t_rest_sum.keep],
        ),
        True,
    )

    t_rest_sum.link()
    i_rest_sum.came = after(i_rest_sum.came, t_out_sum.keep)
    i_rest_sum.column()

    t_co_grad, i_co_grad, t_co_sum, i_co_sum = co_backward(
        lengths, text_co, image_co, t_ctx, i_ctx, [t_out_sum.keep, t_rest_sum.send]
    )
    t_out_sum.came = after(t_out_sum.came, t_rest_sum.send)
    t_out_sum.link()

    def small_grads(sums1, sums2, up_sum, co_sum):
        wide = jnp.concatenate([co_sum[0, :CO_W], co_sum[0, 2 * CO_W :], up_sum[0]])
        rows8 = jnp.stack(
            [sums1[2], sums1[1], sums1[3], sums1[4], sums2[5], sums2[4], sums2[2], sums2[1]]
        )
        return wide, rows8, jnp.stack([sums1[0], sums2[3], sums2[0]])

    pieces = small_grads(t_sums1, t_sums2, t_upsum, t_co_sum) + small_grads(
        i_sums1, i_sums2, i_upsum, i_co_sum
    )
    packed = []
    for piece in pieces:
        if piece.ndim == 1:
            packed.append(piece.reshape(shard_count, -1))
        else:
            packed.append(
                piece.reshape(piece.shape[0], shard_count, -1)
                .transpose(1, 0, 2)
                .reshape(shard_count, -1)
            )
    packed = jnp.concatenate(packed, 1)
    count = packed.shape[1]
    packed = jnp.pad(packed, ((0, 0), (0, extra * t_rows - count))).reshape(-1, extra)

    i_co_sums = Scatter(
        cols_grad(
            shard_count, True,
            [(image_rows, i_co_grad)],
            512,
            deps=[t_rest_sum.send, t_out_sum.send],
        ),
        True,
    )
    t_co_sums = Scatter(
        cols_grad(shard_count, False, [(text_in, t_co_grad)], 768, packed, [i_co_sums.keep]), False
    )
    i_co_sums.link()
    t_co_sums.came = after(t_co_sums.came, i_co_sums.send)
    t_co_sums.link()
    image_grad = after(i_first, i_co_sums.send) + dot_nt(i_co_grad, i_co)
    image_grad = over_x(unpad_pairs(image_grad).astype(BF)).astype(F32)
    text_grad = after(t_first, t_co_sums.send) + dot_nt(t_co_grad, t_co[:, : 3 * CO_W])
    t_rest_sum.link()
    t_out_sum.link()
    t_rest_sum.column()
    t_out_sum.column()
    i_co_sums.link()
    t_co_sums.link()
    i_co_sums.column_by_permutes()
    t_co_sums.column_by_permutes()
    image_final = image_final.astype(F32)
    t_cog = t_co_sums.total()

    mine = t_cog[:, 3 * CO_W :].reshape(-1)
    outs = []
    offset = 0
    for piece in small:
        outs.append(mine[offset : offset + piece.size].reshape(piece.shape))
        offset += piece.size
    t_wide_g, t_rows_g, t_gain_g, i_wide_g, i_rows_g, i_gain_g = outs
    return (
        t_final,
        image_final,
        text_grad,
        image_grad,
        jnp.concatenate([t_cog[:, : 3 * CO_W], t_rest_sum.total()], 1),
        t_out_sum.total(),
        t_wide_g,
        t_rows_g,
        t_gain_g,
        jnp.concatenate([i_co_sums.total(), i_rest_sum.total()], 1),
        i_out_sum.total(),
        i_wide_g,
        i_rows_g,
        i_gain_g,
    )


def solution(mesh):
    both = ("stream", "dp")
    rows, cols, flat = P(both, None), P(None, both), P(both)
    weights = (rows, rows, flat, cols, cols)
    return jax.shard_map(
        shards,
        mesh=mesh,
        in_specs=(rows, rows, flat) + weights + weights + (rows, rows),
        out_specs=(rows, rows, rows, rows) + weights + weights,
        check_vma=False,
    )
```
